128 devices in a mesh: rows: 32 (over y, x_lo, z), protos: 4 (over x_hi, core).
Axes of the slice: x: 4 (x_hi: 2, x_lo: 2; x = x_hi * 2 + x_lo), y: 4, z: 4, core: 2. Of those that a mesh axis runs over, the one named last changes fastest.
Arguments:
- student: bfloat16 [16384, 256], P('rows'), may hold values from -256 to 256
- teacher: bfloat16 [16384, 256], P('rows'), may hold values from -256 to 256
- prototypes: bfloat16 [65536, 256], P('protos'), may hold values from -1 to 1
- masked: int32 [16384], P('rows'), may hold values from 0 to 1, as said below
Outputs:
- feature_grad: bfloat16 [16384, 256], P(('rows', 'protos'))
- proto_grad: bfloat16 [65536, 256], P(('protos', 'rows'))
The draws below stay inside these ranges and needn't reach their ends.
Inputs may be any that keep to these rules, and one draw needn't show every extreme that they name: Rows whose index is a multiple of 16 are masked.
All inputs are finite; a program needn't handle non-finite values.
Results may differ from the reference program's by a relative error of at most 0.02.
Values may be sent and summed in bfloat16 or wider, within the bound.
No kernel may reach another device: no remote copies, remote signals or barrier semaphores. Data moves between devices by JAX's collectives and lax.ppermute only.
A program may use at most 256 MiB of HBM per device.

```python
import math
import jax
import jax.numpy as jnp
from jax import lax

D = 256
K = 65536
ITERS = 3
ROWS = 16384


def proto_table(key):
    key_raw, key_scale = jax.random.split(key)
    raw_rows = jax.random.normal(key_raw, (K, D), jnp.float32) * (64.0 * D) ** (-0.5)
    scales = jnp.exp(jax.random.uniform(key_scale, (K, 1), jnp.float32, math.log(0.5), math.log(2.0)))
    row_index = jnp.arange(K)[:, None]
    paired = row_index % 64 == 3
    proto_rows = jnp.where(paired, 0.985 * jnp.roll(raw_rows, 1, axis=0) + 0.05 * raw_rows, raw_rows)
    scales = jnp.where(paired, jnp.roll(scales, 1, axis=0), scales)
    return proto_rows * scales


def draw_prototypes(key, part):
    proto_rows = proto_table(key)
    return proto_rows.astype(jnp.bfloat16)


def draw_student(key, part):
    key = jax.random.fold_in(key, 11)
    key_base, key_rows = jax.random.split(key, 2)
    row_scale = jnp.exp(jax.random.uniform(key_rows, (ROWS, 1), jnp.float32, math.log(0.3), math.log(3.0)))
    return (jax.random.normal(key_base, (ROWS, D), jnp.float32) * row_scale).astype(jnp.bfloat16)


def draw_teacher(key, part):
    key = jax.random.fold_in(key, 12)
    key_base, key_rows = jax.random.split(key, 2)
    row_scale = jnp.exp(jax.random.uniform(key_rows, (ROWS, 1), jnp.float32, math.log(0.3), math.log(3.0)))
    return (jax.random.normal(key_base, (ROWS, D), jnp.float32) * row_scale).astype(jnp.bfloat16)


def draw_masked(key, part):
    key = jax.random.fold_in(key, 13)
    row_index = jnp.arange(ROWS)
    threshold = 200 + 600 * row_index // ROWS
    drawn = jax.random.randint(key, (ROWS,), 0, 1000)
    chosen = (drawn < threshold) | (row_index % 16 == 0)
    return jnp.where(chosen, 1, 0).astype(jnp.int32)


def setup_inputs(seed: int = 0) -> dict:
    seeds = jax.random.split(jax.random.key(seed), 5)
    student = draw_student(jax.random.fold_in(seeds[4], 71), 0)
    teacher = draw_teacher(jax.random.fold_in(seeds[4], 71), 0)
    prototypes = draw_prototypes(jax.random.fold_in(seeds[4], 71), 0)
    masked = draw_masked(jax.random.fold_in(seeds[4], 71), 0)
    return {"student": student, "teacher": teacher, "prototypes": prototypes, "masked": masked}


student_temp = 0.1
teacher_temp = 0.05

def expo_block(teach_block, keep_block, prototypes):
    logits = jnp.dot(teach_block, prototypes.T, preferred_element_type=jnp.float32) / teacher_temp
    return keep_block[:, None] * jnp.exp(logits - lax.optimization_barrier(jnp.max(logits, axis=1, keepdims=True)))

def reference(student, teacher, prototypes, masked):
    highest = lax.Precision.HIGHEST
    proto_count = prototypes.shape[0]
    width = prototypes.shape[1]
    row_total = student.shape[0]
    block_rows = math.gcd(row_total, 512)
    block_count = row_total // block_rows
    row_keep = masked.astype(jnp.float32)
    teach_blocks = teacher.reshape(block_count, block_rows, width)
    stud_blocks = student.reshape(block_count, block_rows, width)
    keep_blocks = row_keep.reshape(block_count, block_rows)
    weights = keep_blocks

    def column_total(carry, inputs):
        teach_block, keep_block, weight_block = inputs
        expo = expo_block(teach_block, keep_block, prototypes)
        return (carry + jnp.dot(weight_block, expo, precision=highest), None)

    def row_total_fn(inputs):
        expo = expo_block(inputs[0], inputs[1], prototypes)
        return jnp.dot(expo, inputs[2], precision=highest)
    col_scale = jnp.zeros((proto_count,), jnp.float32)
    for iteration in range(ITERS):
        colsum, unused = lax.scan(column_total, jnp.zeros((proto_count,), jnp.float32), (teach_blocks, keep_blocks, weights))
        col_scale = 1.0 / (proto_count * colsum)
        scales_rep = jnp.broadcast_to(col_scale, (block_count, proto_count))
        rowsum = lax.map(row_total_fn, (teach_blocks, keep_blocks, scales_rep))
        weights = keep_blocks / jnp.where(keep_blocks > 0, rowsum, 1.0)

    def final_block(carry, inputs):
        teach_block, stud_block, keep_block, weight_block = inputs
        expo = expo_block(teach_block, keep_block, prototypes)
        plan = weight_block[:, None] * expo * col_scale[None, :]
        stud_logit = jnp.dot(stud_block, prototypes.T, preferred_element_type=jnp.float32) / student_temp
        stud_exp = jnp.exp(stud_logit - lax.optimization_barrier(jnp.max(stud_logit, axis=1, keepdims=True)))
        probs = stud_exp / lax.optimization_barrier(jnp.sum(stud_exp, axis=1, keepdims=True))
        grad_logit = (keep_block[:, None] * (proto_count * (probs - plan))).astype(jnp.bfloat16)
        feature_part = jnp.dot(grad_logit, prototypes, preferred_element_type=jnp.float32)
        proto_part = jnp.dot(grad_logit.T, stud_block, preferred_element_type=jnp.float32)
        return (carry + proto_part, feature_part)
    proto_sum, feature_blocks = lax.scan(final_block, jnp.zeros((proto_count, width), jnp.float32), (teach_blocks, stud_blocks, keep_blocks, weights))
    mask_total = jnp.sum(row_keep)
    feature_grad = (feature_blocks.reshape(row_total, width) / (student_temp * math.sqrt(proto_count))).astype(jnp.bfloat16)
    proto_grad = (proto_sum / jnp.sqrt(mask_total)).astype(jnp.bfloat16)
    return (feature_grad, proto_grad)
```

```python
import functools
import math

import jax
import jax.numpy as jnp
from jax import lax
from jax.experimental import pallas as pl
from jax.experimental.pallas import tpu as pltpu
from jax.sharding import Mesh
from jax.sharding import PartitionSpec as P

ITERS = 3
student_temp = 0.1
teacher_temp = 0.05

F32 = jnp.float32
BF16 = jnp.bfloat16
TILE = 256
LANES = 128
FAR = 1e30
INFO = 16
VMEM_LIMIT = 30 * 2**20

NT = (((1,), (1,)), ((), ()))


def params(limit=VMEM_LIMIT):
    return pltpu.CompilerParams(vmem_limit_bytes=limit)


def vmem():
    return pl.BlockSpec(memory_space=pltpu.VMEM)


def smem():
    return pl.BlockSpec(memory_space=pltpu.SMEM)


def split(value):
    high = value.astype(BF16)
    low = (value - high.astype(F32)).astype(BF16)
    return high, low


def as_row(block):
    pieces = []
    for start in range(0, block.shape[0], LANES):
        part = block[start : start + LANES]
        total = part[:, :LANES]
        for lane in range(LANES, block.shape[1], LANES):
            total = total + part[:, lane : lane + LANES]
        pieces.append(jnp.sum(jnp.transpose(total), axis=0, keepdims=True))
    return jnp.concatenate(pieces, axis=1)


def compact_kernel(mask_ref, teach_ref, stud_ref, teach_out, stud_out):
    rows, width = teach_ref.shape
    mask = mask_ref[...]
    down = lax.broadcasted_iota(jnp.int32, (rows, rows), 0)
    along = lax.broadcasted_iota(jnp.int32, (rows, rows), 1)
    upper = jnp.where(down <= along, 1.0, 0.0).astype(BF16)
    many = jnp.broadcast_to(mask, (16, rows)).astype(BF16)
    rank = jnp.dot(many, upper, preferred_element_type=F32)[:1]
    place = jnp.where(mask > 0, rank - 1.0, -1.0)
    onehot = jnp.where(down.astype(F32) == place, 1.0, 0.0).astype(BF16)
    teach_out[:rows] = jnp.dot(onehot, teach_ref[...], preferred_element_type=F32).astype(BF16)
    stud_out[...] = jnp.dot(onehot, stud_ref[...], preferred_element_type=F32).astype(BF16)
    which = lax.broadcasted_iota(jnp.int32, (INFO, width), 0)
    info = jnp.zeros((INFO, width), F32)
    for piece in range(rows // width):
        info = jnp.where(which == piece, mask[:, piece * width : (piece + 1) * width], info)
    teach_out[rows:] = info.astype(BF16)


def compact(mask_row, teacher, student):
    rows, width = teacher.shape
    return pl.pallas_call(
        compact_kernel,
        out_shape=(
            jax.ShapeDtypeStruct((rows + INFO, width), BF16),
            jax.ShapeDtypeStruct((rows, width), BF16),
        ),
        in_specs=[vmem()] * 3,
        out_specs=(vmem(), vmem()),
        compiler_params=params(),
        name="compact",
    )(mask_row, teacher, student)


def max_kernel(teach_ref, proto_ref, out_ref):
    step = pl.program_id(0)
    rows = out_ref.shape[1]
    chunk = 512

    @pl.when(step == 0)
    def _():
        out_ref[...] = jnp.full_like(out_ref, -FAR)

    feats = teach_ref[:rows]
    best = out_ref[...]
    for start in range(0, proto_ref.shape[0], chunk):
        logit = lax.dot_general(
            proto_ref[start : start + chunk], feats, NT, preferred_element_type=F32
        )
        best = jnp.maximum(best, jnp.max(logit, axis=0, keepdims=True))
    out_ref[...] = best


def row_max(feats, protos, rows):
    count, width = protos.shape
    block = 2048
    return pl.pallas_call(
        max_kernel,
        grid=(count // block,),
        out_shape=jax.ShapeDtypeStruct((1, rows), F32),
        in_specs=[
            pl.BlockSpec(feats.shape, lambda i: (0, 0)),
            pl.BlockSpec((block, width), lambda i: (i, 0)),
        ],
        out_specs=pl.BlockSpec((1, rows), lambda i: (0, 0)),
        compiler_params=params(),
        cost_estimate=pl.CostEstimate(
            flops=2 * count * width * rows, bytes_accessed=count * width * 2, transcendentals=0
        ),
        name="row_max",
    )(feats, protos)


def soft_kernel(feat_ref, proto_ref, top_ref, sum_ref):
    step = pl.program_id(0)
    chunk = 512

    @pl.when(step == 0)
    def _():
        top_ref[...] = jnp.full_like(top_ref, -FAR)
        sum_ref[...] = jnp.zeros_like(sum_ref)

    feats = feat_ref[...]
    top = top_ref[...]
    total = sum_ref[...]
    for start in range(0, proto_ref.shape[0], chunk):
        logit = lax.dot_general(
            proto_ref[start : start + chunk], feats, NT, preferred_element_type=F32
        )
        higher = jnp.maximum(top, jnp.max(logit, axis=0, keepdims=True))
        total = total * jnp.exp((top - higher) * (1 / student_temp)) + jnp.sum(
            jnp.exp((logit - higher) * (1 / student_temp)), axis=0, keepdims=True
        )
        top = higher
    top_ref[...] = top
    sum_ref[...] = total


def row_soft(feats, protos):
    count, width = protos.shape
    rows = feats.shape[0]
    block = 2048
    row = pl.BlockSpec((1, rows), lambda i: (0, 0))
    return pl.pallas_call(
        soft_kernel,
        grid=(count // block,),
        out_shape=(jax.ShapeDtypeStruct((1, rows), F32),) * 2,
        in_specs=[
            pl.BlockSpec(feats.shape, lambda i: (0, 0)),
            pl.BlockSpec((block, width), lambda i: (i, 0)),
        ],
        out_specs=(row, row),
        compiler_params=params(),
        cost_estimate=pl.CostEstimate(
            flops=2 * count * width * rows,
            bytes_accessed=count * width * 2,
            transcendentals=count * rows,
        ),
        name="row_soft",
    )(feats, protos)


def load_rows(meta, mine_ref, other_ref, rows_ref, rows):
    blocks = mine_ref.shape[0]
    first = meta[2 * blocks + 2] == 0
    for block in range(blocks):
        offset = pl.multiple_of(meta[block], LANES)
        mine = mine_ref[block, :rows]
        other = other_ref[block, :rows]
        rows_ref[pl.ds(offset, rows), :LANES] = jnp.where(first, mine, other)
        rows_ref[pl.ds(offset, rows), LANES:] = jnp.where(first, other, mine)
    tail = pl.multiple_of(meta[2 * blocks], LANES)
    rows_ref[pl.ds(tail, TILE), :] = jnp.zeros((TILE, rows_ref.shape[1]), BF16)


def load_line(meta, line_ref, out_ref, fill):
    blocks, _, rows = line_ref.shape
    out_ref[...] = jnp.full_like(out_ref, fill)
    lane = lax.broadcasted_iota(jnp.int32, (1, rows), 1)
    for block in range(blocks):
        offset = pl.multiple_of(meta[block], LANES)
        out_ref[:, pl.ds(offset, rows)] = jnp.where(
            lane < meta[blocks + block], line_ref[block], fill
        )


def expo_kernel(meta, mine_ref, other_ref, top_ref, proto_ref, expo_ref, col_ref, valid_ref, rows_ref, line_ref, acc_ref):
    blocks, _, rows = top_ref.shape
    load_rows(meta, mine_ref, other_ref, rows_ref, rows)
    load_line(meta, top_ref, line_ref, FAR)
    valid_ref[...] = jnp.where(line_ref[...] < 0.5 * FAR, 1.0, 0.0)
    acc_ref[...] = jnp.zeros_like(acc_ref)
    chunk = 512

    @pl.loop(0, meta[2 * blocks + 1])
    def _(tile):
        start = pl.multiple_of(tile * TILE, TILE)
        feats = rows_ref[pl.ds(start, TILE), :]
        top = line_ref[:, pl.ds(start, TILE)]
        for k in range(0, proto_ref.shape[0], chunk):
            logit = lax.dot_general(proto_ref[k : k + chunk], feats, NT, preferred_element_type=F32)
            expo = jnp.exp((logit - top) * (1 / teacher_temp))
            expo_ref[tile, k : k + chunk] = expo.astype(BF16)
            acc_ref[k : k + chunk] += expo

    protos = proto_ref.shape[0]
    col_ref[:, :protos] = as_row(acc_ref[...])
    col_ref[:, protos:] = jnp.zeros((1, LANES), F32) + jnp.sum(valid_ref[...])


def expo_step(meta, mine, other, tops, protos):
    blocks, _, rows = tops.shape
    count, width = protos.shape
    total = blocks * rows
    return pl.pallas_call(
        expo_kernel,
        out_shape=(
            pltpu.VMEM((total // TILE, count, TILE), BF16),
            jax.ShapeDtypeStruct((1, count + LANES), F32),
            jax.ShapeDtypeStruct((1, total), F32),
        ),
        in_specs=[smem()] + [vmem()] * 4,
        out_specs=(vmem(),) * 3,
        scratch_shapes=[
            pltpu.VMEM((total + TILE, width), BF16),
            pltpu.VMEM((1, total), F32),
            pltpu.VMEM((count, TILE), F32),
        ],
        compiler_params=params(),
        name="expo",
    )(meta, mine, other, tops, protos)


def col_scale_of(parts_ref, count, proto_total):
    total = parts_ref[0][:, :count]
    for part in range(1, parts_ref.shape[0]):
        total = total + parts_ref[part][:, :count]
    return 1.0 / (proto_total * total)


def row_kernel(proto_total, meta, parts_ref, expo_ref, out_ref):
    count = expo_ref.shape[1]
    high, low = split(col_scale_of(parts_ref, count, proto_total))
    which = lax.broadcasted_iota(jnp.int32, (16, count), 0)
    lhs = jnp.where(which == 0, high.astype(F32), jnp.where(which == 1, low.astype(F32), 0.0)).astype(BF16)
    out_ref[...] = jnp.zeros_like(out_ref)

    @pl.loop(0, meta[17])
    def _(tile):
        start = pl.multiple_of(tile * TILE, TILE)
        both = jnp.dot(lhs, expo_ref[tile], preferred_element_type=F32)
        out_ref[:, pl.ds(start, TILE)] = both[:1] + both[1:2]


def row_step(meta, parts, expo, proto_total):
    tiles, count, _ = expo.shape
    return pl.pallas_call(
        functools.partial(row_kernel, proto_total),
        out_shape=jax.ShapeDtypeStruct((1, tiles * TILE), F32),
        in_specs=[smem()] + [vmem()] * 2,
        out_specs=vmem(),
        compiler_params=params(),
        name="row_step",
    )(meta, parts, expo)


def weights_of(parts_ref, valid_ref):
    total = parts_ref[0]
    for part in range(1, parts_ref.shape[0]):
        total = total + parts_ref[part]
    valid = valid_ref[...]
    return valid / jnp.where(valid > 0, total, 1.0)


def col_kernel(meta, parts_ref, valid_ref, expo_ref, out_ref, line_ref, acc_ref):
    line_ref[...] = weights_of(parts_ref, valid_ref)
    acc_ref[...] = jnp.zeros_like(acc_ref)
    which = lax.broadcasted_iota(jnp.int32, (16, TILE), 0)

    @pl.loop(0, meta[17])
    def _(tile):
        start = pl.multiple_of(tile * TILE, TILE)
        high, low = split(line_ref[:, pl.ds(start, TILE)])
        lhs = jnp.where(which == 0, high.astype(F32), jnp.where(which == 1, low.astype(F32), 0.0)).astype(BF16)
        acc_ref[...] += lax.dot_general(lhs, expo_ref[tile], NT, preferred_element_type=F32)

    out_ref[...] = acc_ref[:1] + acc_ref[1:2]


def col_step(meta, parts, valid, expo):
    tiles, count, _ = expo.shape
    return pl.pallas_call(
        col_kernel,
        out_shape=jax.ShapeDtypeStruct((1, count), F32),
        in_specs=[smem()] + [vmem()] * 3,
        out_specs=vmem(),
        scratch_shapes=[pltpu.VMEM((1, tiles * TILE), F32), pltpu.VMEM((16, count), F32)],
        compiler_params=params(),
        name="col_step",
    )(meta, parts, valid, expo)


def store_blocks(meta, rows_ref, out_ref):
    blocks, rows, _ = out_ref.shape
    for block in range(blocks):
        offset = pl.multiple_of(meta[block], LANES)
        out_ref[block] = rows_ref[pl.ds(offset, rows), :]


def student_kernel(meta, mine_ref, other_ref, lse_ref, proto_ref, turned_ref, grad_ref, feat_ref, rows_ref, line_ref, acc_ref, sums_ref):
    blocks, _, rows = lse_ref.shape
    load_rows(meta, mine_ref, other_ref, rows_ref, rows)
    load_line(meta, lse_ref, line_ref, FAR)
    acc_ref[...] = jnp.zeros_like(acc_ref)
    sums_ref[...] = jnp.zeros_like(sums_ref)
    chunk = 512

    @pl.loop(0, meta[2 * blocks + 1])
    def _(tile):
        start = pl.multiple_of(tile * TILE, TILE)
        feats = rows_ref[pl.ds(start, TILE), :]
        lse = line_ref[:, pl.ds(start, TILE)]
        turned = jnp.zeros((proto_ref.shape[1], TILE), F32)
        for k in range(0, proto_ref.shape[0], chunk):
            logit = lax.dot_general(proto_ref[k : k + chunk], feats, NT, preferred_element_type=F32)
            probs = jnp.exp(logit * (1 / student_temp) - lse).astype(BF16)
            acc_ref[k : k + chunk] += jnp.dot(probs, feats, preferred_element_type=F32)
            turned += jnp.dot(turned_ref[:, k : k + chunk], probs, preferred_element_type=F32)
        sums_ref[pl.ds(start, TILE), :] = jnp.transpose(turned).astype(BF16)

    store_blocks(meta, sums_ref, feat_ref)
    grad_ref[...] = acc_ref[...].astype(BF16)


def student_step(meta, mine, other, lses, protos, turned):
    blocks, _, rows = lses.shape
    count, width = protos.shape
    total = blocks * rows
    return pl.pallas_call(
        student_kernel,
        out_shape=(
            jax.ShapeDtypeStruct((count, width), BF16),
            jax.ShapeDtypeStruct((blocks, rows, width), BF16),
        ),
        in_specs=[smem()] + [vmem()] * 5,
        out_specs=(vmem(),) * 2,
        scratch_shapes=[
            pltpu.VMEM((total + TILE, width), BF16),
            pltpu.VMEM((1, total), F32),
            pltpu.VMEM((count, width), F32),
            pltpu.VMEM((total, width), BF16),
        ],
        compiler_params=params(),
        name="student",
    )(meta, mine, other, lses, protos, turned)


def feature_kernel(proto_total, meta, parts_ref, expo_ref, turned_ref, feat_ref, sums_ref):
    count = expo_ref.shape[1]
    scale = col_scale_of(parts_ref, count, proto_total)
    scaled = (turned_ref[...].astype(F32) * scale).astype(BF16)
    sums_ref[...] = jnp.zeros_like(sums_ref)

    @pl.loop(0, meta[17])
    def _(tile):
        start = pl.multiple_of(tile * TILE, TILE)
        turned = jnp.dot(scaled, expo_ref[tile], preferred_element_type=F32)
        sums_ref[pl.ds(start, TILE), :] = jnp.transpose(turned).astype(BF16)

    store_blocks(meta, sums_ref, feat_ref)


def feature_step(meta, parts, expo, turned, proto_total):
    tiles, count, _ = expo.shape
    width = turned.shape[0]
    return pl.pallas_call(
        functools.partial(feature_kernel, proto_total),
        out_shape=jax.ShapeDtypeStruct((8, tiles * TILE // 8, width), BF16),
        in_specs=[smem()] + [vmem()] * 3,
        out_specs=vmem(),
        scratch_shapes=[pltpu.VMEM((tiles * TILE, width), BF16)],
        compiler_params=params(),
        name="feature_step",
    )(meta, parts, expo, turned)


def grad_kernel(meta, parts_ref, valid_ref, mine_ref, other_ref, expo_ref, grad_ref, weight_ref, rows_ref, acc_ref):
    blocks = mine_ref.shape[0]
    load_rows(meta, mine_ref, other_ref, rows_ref, mine_ref.shape[1])
    weight_ref[...] = weights_of(parts_ref, valid_ref)
    acc_ref[...] = jnp.zeros_like(acc_ref)
    chunk = 512

    @pl.loop(0, meta[2 * blocks + 1])
    def _(tile):
        start = pl.multiple_of(tile * TILE, TILE)
        weight = weight_ref[:, pl.ds(start, TILE)]
        feats = rows_ref[pl.ds(start, TILE), :].astype(F32)
        parts = []
        for lane in range(0, TILE, LANES):
            column = jnp.transpose(jnp.broadcast_to(weight[:, lane : lane + LANES], (LANES, LANES)))
            part = feats[lane : lane + LANES]
            parts.append(
                jnp.concatenate(
                    [part[:, d : d + LANES] * column for d in range(0, part.shape[1], LANES)], axis=1
                )
            )
        scaled = jnp.concatenate(parts, axis=0).astype(BF16)
        for k in range(0, acc_ref.shape[0], chunk):
            acc_ref[k : k + chunk] += jnp.dot(
                expo_ref[tile, k : k + chunk], scaled, preferred_element_type=F32
            )

    grad_ref[...] = acc_ref[...].astype(BF16)


def grad_step(meta, parts, valid, mine, other, expo):
    tiles, count, _ = expo.shape
    width = 2 * LANES
    total = tiles * TILE
    return pl.pallas_call(
        grad_kernel,
        out_shape=(
            jax.ShapeDtypeStruct((count, width), BF16),
            jax.ShapeDtypeStruct((1, total), F32),
        ),
        in_specs=[smem()] + [vmem()] * 5,
        out_specs=(vmem(),) * 2,
        scratch_shapes=[
            pltpu.VMEM((total + TILE, width), BF16),
            pltpu.VMEM((count, width), F32),
        ],
        compiler_params=params(),
        name="grad_step",
    )(meta, parts, valid, mine, other, expo)


def swap(value, axis):
    return lax.ppermute(value, axis, [(0, 1), (1, 0)])


def spread(value, axes, size):
    many = jnp.broadcast_to(value[None], (size,) + value.shape)
    return lax.all_to_all(many, axes, 0, 0, tiled=True)


def gather_blocks(block, core):
    half = lax.dynamic_slice_in_dim(block, core * LANES, LANES, 1)
    beside = swap(half, "xl")
    low = lax.axis_index("xl") == 0
    pair = jnp.stack([jnp.where(low, half, beside), jnp.where(low, beside, half)])
    mine = spread(pair, "y", 4)
    mine = mine.reshape((8,) + half.shape)
    return mine, swap(mine, "c")


def scatter_rows(value, core):
    blocks, rows, width = value.shape
    width //= 2
    value = value.reshape(blocks * rows, 2 * width)
    keep = lax.dynamic_slice_in_dim(value, core * width, width, 1)
    give = lax.dynamic_slice_in_dim(value, (1 - core) * width, width, 1)
    total = (keep.astype(F32) + swap(give, "c").astype(F32)).astype(BF16)
    parts = lax.all_to_all(total.reshape(4, -1, width), "y", 0, 0, tiled=True)
    total = jnp.sum(parts.astype(F32), axis=0).astype(BF16)
    rows = total.shape[0] // 2
    side = lax.axis_index("xl")
    keep = lax.dynamic_slice_in_dim(total, side * rows, rows, 0)
    give = lax.dynamic_slice_in_dim(total, (1 - side) * rows, rows, 0)
    return keep.astype(F32) + swap(give, "xl").astype(F32)


def local(student, teacher, prototypes, masked):
    rows, width = student.shape
    y, xl, z = lax.axis_index("y"), lax.axis_index("xl"), lax.axis_index("z")
    xh, core = lax.axis_index("xh"), lax.axis_index("c")
    block_id = y * 2 + xl
    count = prototypes.shape[0] // 8
    proto_total = prototypes.shape[0] * 4
    mask_row = masked.astype(F32)[None]

    teach, stud = compact(mask_row, teacher, student)
    protos = lax.dynamic_slice_in_dim(prototypes, block_id * count, count, 0)
    turned = jnp.transpose(protos)

    mine, other = gather_blocks(teach, core)
    top = row_max(teach, prototypes, rows)
    top = jnp.maximum(top, swap(top, "c"))
    top = jnp.maximum(top, swap(top, "xh"))
    tops = spread(top, ("y", "xl"), 8)

    counts = jnp.sum(mine[:, rows:].astype(F32), axis=(1, 2)) + jnp.sum(other[:, rows:].astype(F32), axis=(1, 2))
    counts = counts.astype(jnp.int32)
    padded = (counts + (LANES - 1)) // LANES * LANES
    ends = jnp.cumsum(padded)
    tail = ends[-1:]
    meta = jnp.concatenate(
        [ends - padded, counts, tail, (tail + (TILE - 1)) // TILE, core.astype(jnp.int32)[None]]
    )

    expo, col, valid = expo_step(meta, mine, other, tops, protos)
    col_parts = spread(col, "z", 4)
    mask_total = jnp.sum(col_parts[:, 0, count])

    stud_mine, stud_other = gather_blocks(stud, core)
    soft_top, soft_sum = row_soft(stud, prototypes)
    for axis in ("c", "xh"):
        far_top, far_sum = swap(soft_top, axis), swap(soft_sum, axis)
        high = jnp.maximum(soft_top, far_top)
        soft_sum = soft_sum * jnp.exp((soft_top - high) / student_temp) + far_sum * jnp.exp(
            (far_top - high) / student_temp
        )
        soft_top = high
    lse = soft_top / student_temp + jnp.log(soft_sum)
    lses = spread(lse, ("y", "xl"), 8)
    stud_grad, stud_feat = student_step(meta, stud_mine, stud_other, lses, protos, turned)

    for iteration in range(ITERS):
        row = row_step(meta, col_parts, expo, proto_total)
        row = row + swap(row, "c")
        row_parts = spread(row, ("y", "xl", "xh"), 16)
        if iteration < ITERS - 1:
            col = col_step(meta, row_parts, valid, expo)
            col_parts = spread(col, "z", 4)

    plan_feat = feature_step(meta, col_parts, expo, turned, proto_total)
    plan_own = scatter_rows(plan_feat, core)
    stud_own = scatter_rows(stud_feat, core)

    plan_grad, weights = grad_step(meta, row_parts, valid, stud_mine, stud_other, expo)

    half = width // 2
    weight_row = lax.dynamic_slice(weights, (0, meta[block_id]), (1, rows))
    own = (stud_own - weight_row[0][:, None] * plan_own).astype(BF16)
    place = jnp.where(masked > 0, jnp.cumsum(masked) - 1, -1)
    onehot = (place[:, None] == jnp.arange(rows)[None, :]).astype(BF16)
    own = jnp.dot(onehot, own, preferred_element_type=F32)
    keep = lax.dynamic_slice_in_dim(own, xh * (rows // 2), rows // 2, 0)
    give = lax.dynamic_slice_in_dim(own, (1 - xh) * (rows // 2), rows // 2, 0)
    own = keep + swap(give.astype(BF16), "xh").astype(F32)
    quarter = rows // 4
    keep = lax.dynamic_slice_in_dim(own, core * quarter, quarter, 0)
    give = lax.dynamic_slice_in_dim(own, (1 - core) * quarter, quarter, 0)
    got = swap(give.astype(BF16), "c").astype(F32)
    joined = jnp.where(core == 0, jnp.concatenate([keep, got], 1), jnp.concatenate([got, keep], 1))
    feature_grad = (joined * (math.sqrt(proto_total) / student_temp)).astype(BF16)

    stud_parts = lax.all_to_all(stud_grad.reshape(4, -1, width), "z", 0, 0, tiled=True)
    plan_parts = lax.all_to_all(plan_grad.reshape(4, -1, width), "z", 0, 0, tiled=True)
    col_total = jnp.sum(col_parts[:, 0, :count], axis=0)
    scale = 1.0 / (proto_total * lax.dynamic_slice_in_dim(col_total, z * (count // 4), count // 4, 0))
    stud_sum = jnp.sum(stud_parts.astype(F32), axis=0)
    plan_sum = jnp.sum(plan_parts.astype(F32), axis=0)
    proto_grad = (
        (stud_sum - scale[:, None] * plan_sum) * (proto_total / jnp.sqrt(mask_total))
    ).astype(BF16)
    return feature_grad, proto_grad


def solution(mesh):
    fine = Mesh(mesh.devices.reshape(4, 2, 4, 2, 2), ("y", "xl", "z", "xh", "c"))
    rows, protos = ("y", "xl", "z"), ("xh", "c")
    in_specs = (P(rows, None), P(rows, None), P(protos, None), P(rows))
    out_specs = (P(rows + protos, None), P(protos + rows, None))
    return jax.shard_map(local, mesh=fine, in_specs=in_specs, out_specs=out_specs, check_vma=False)
```

```python
import functools
import math

import jax
import jax.numpy as jnp
from jax import lax
from jax.experimental import pallas as pl
from jax.experimental.pallas import tpu as pltpu
from jax.sharding import Mesh
from jax.sharding import PartitionSpec as P

ITERS = 3
student_temp = 0.1
teacher_temp = 0.05

F32 = jnp.float32
BF16 = jnp.bfloat16
TILE = 512
LANES = 128
ALIGN = 16
FAR = 1e30
INFO = 16
BLOCKS = 8
END, TILES = 2 * BLOCKS, 2 * BLOCKS + 1
MIB = 2**20

NT = (((1,), (1,)), ((), ()))


def params(mib):
    return pltpu.CompilerParams(vmem_limit_bytes=mib * MIB)


def vmem():
    return pl.BlockSpec(memory_space=pltpu.VMEM)


def smem():
    return pl.BlockSpec(memory_space=pltpu.SMEM)


def hbm():
    return pl.BlockSpec(memory_space=pltpu.HBM)


def pinned(value):
    return pltpu.with_memory_space_constraint(value, pltpu.VMEM)


def streamed(value):
    return pltpu.with_memory_space_constraint(value, pltpu.HBM)


def own_protos(place, proto_ref, own_ref, sem):
    count = own_ref.shape[0]
    start = pl.multiple_of(place[3] * count, count)
    return pltpu.make_async_copy(proto_ref.at[pl.ds(start, count)], own_ref, sem)


def turn(own_ref):
    chunk = 512
    return jnp.concatenate(
        [jnp.transpose(own_ref[k : k + chunk]) for k in range(0, own_ref.shape[0], chunk)], axis=1
    )


def split(value):
    high = value.astype(BF16)
    low = (value - high.astype(F32)).astype(BF16)
    return high, low


def as_row(block):
    pieces = []
    for start in range(0, block.shape[0], LANES):
        part = block[start : start + LANES]
        total = part[:, :LANES]
        for lane in range(LANES, block.shape[1], LANES):
            total = total + part[:, lane : lane + LANES]
        pieces.append(jnp.sum(jnp.transpose(total), axis=0, keepdims=True))
    return jnp.concatenate(pieces, axis=1)


def compact_kernel(mask_ref, teach_ref, stud_ref, teach_out, stud_out):
    rows, width = teach_ref.shape
    mask = mask_ref[...]
    down = lax.broadcasted_iota(jnp.int32, (rows, rows), 0)
    along = lax.broadcasted_iota(jnp.int32, (rows, rows), 1)
    upper = jnp.where(down <= along, 1.0, 0.0).astype(BF16)
    many = jnp.broadcast_to(mask, (16, rows)).astype(BF16)
    rank = jnp.dot(many, upper, preferred_element_type=F32)[:1]
    place = jnp.where(mask > 0, rank - 1.0, -1.0)
    onehot = jnp.where(down.astype(F32) == place, 1.0, 0.0).astype(BF16)
    teach_out[:rows] = jnp.dot(onehot, teach_ref[...], preferred_element_type=F32).astype(BF16)
    stud_out[...] = jnp.dot(onehot, stud_ref[...], preferred_element_type=F32).astype(BF16)
    which = lax.broadcasted_iota(jnp.int32, (INFO, width), 0)
    info = jnp.zeros((INFO, width), F32)
    for piece in range(rows // width):
        info = jnp.where(which == piece, mask[:, piece * width : (piece + 1) * width], info)
    teach_out[rows:] = info.astype(BF16)


def compact(mask_row, teacher, student):
    rows, width = teacher.shape
    return pl.pallas_call(
        compact_kernel,
        out_shape=(
            jax.ShapeDtypeStruct((rows + INFO, width), BF16),
            jax.ShapeDtypeStruct((rows, width), BF16),
        ),
        in_specs=[vmem()] * 3,
        out_specs=(vmem(), vmem()),
        compiler_params=params(12),
        name="compact",
    )(mask_row, teacher, student)


def max_kernel(teach_ref, proto_ref, out_ref, turned_ref):
    rows = out_ref.shape[1]
    chunk = 512

    @pl.when(pl.program_id(0) == 0)
    def _():
        out_ref[...] = jnp.full_like(out_ref, -FAR)
        turned_ref[...] = jnp.transpose(teach_ref[:rows])

    best = out_ref[...]
    for start in range(0, proto_ref.shape[0], chunk):
        logit = jnp.dot(proto_ref[start : start + chunk], turned_ref[...], preferred_element_type=F32)
        best = jnp.maximum(best, jnp.max(logit, axis=0, keepdims=True))
    out_ref[...] = best


def row_max(feats, protos, rows, part, parts):
    count, width = protos.shape
    block = 2048
    steps = count // block // parts
    return pl.pallas_call(
        max_kernel,
        grid=(steps,),
        out_shape=jax.ShapeDtypeStruct((1, rows), F32),
        in_specs=[
            pl.BlockSpec(feats.shape, lambda i: (0, 0)),
            pl.BlockSpec((block, width), lambda i: (i + part * steps, 0)),
        ],
        out_specs=pl.BlockSpec((1, rows), lambda i: (0, 0)),
        scratch_shapes=[pltpu.VMEM((width, rows), BF16)],
        compiler_params=params(14),
        cost_estimate=cost(2 * count * width * rows // parts),
        name="row_max",
    )(feats, protos)


def soft_kernel(feat_ref, proto_ref, top_ref, sum_ref, turned_ref):
    chunk = 512

    @pl.when(pl.program_id(0) == 0)
    def _():
        top_ref[...] = jnp.full_like(top_ref, -FAR)
        sum_ref[...] = jnp.zeros_like(sum_ref)
        turned_ref[...] = jnp.transpose(feat_ref[...])

    top = top_ref[...]
    total = sum_ref[...]
    for start in range(0, proto_ref.shape[0], chunk):
        logit = jnp.dot(proto_ref[start : start + chunk], turned_ref[...], preferred_element_type=F32)
        higher = jnp.maximum(top, jnp.max(logit, axis=0, keepdims=True))
        total = total * jnp.exp((top - higher) * (1 / student_temp)) + jnp.sum(
            jnp.exp((logit - higher) * (1 / student_temp)), axis=0, keepdims=True
        )
        top = higher
    top_ref[...] = top
    sum_ref[...] = total


def row_soft(feats, protos, part, parts):
    count, width = protos.shape
    rows = feats.shape[0]
    block = 2048
    steps = count // block // parts
    row = pl.BlockSpec((1, rows), lambda i: (0, 0))
    return pl.pallas_call(
        soft_kernel,
        grid=(steps,),
        out_shape=(jax.ShapeDtypeStruct((1, rows), F32),) * 2,
        in_specs=[
            pl.BlockSpec(feats.shape, lambda i: (0, 0)),
            pl.BlockSpec((block, width), lambda i: (i + part * steps, 0)),
        ],
        out_specs=(row, row),
        scratch_shapes=[pltpu.VMEM((width, rows), BF16)],
        compiler_params=params(14),
        cost_estimate=cost(3 * count * width * rows // parts),
        name="row_soft",
    )(feats, protos)


def cost(flops):
    return pl.CostEstimate(flops=flops, bytes_accessed=2**20, transcendentals=0)


def joined(place, refs, block, rows):
    piece, side = block // 2, block % 2
    mine = refs[piece][side, :rows]
    other = refs[4 + piece][side, :rows]
    first = place[1] == 0
    return jnp.where(first, mine, other), jnp.where(first, other, mine)


def true_block(place, block):
    return (place[0] ^ (block // 2)) * 2 + block % 2


def load_rows(place, meta, refs, rows_ref, rows):
    for true in range(BLOCKS):

        def fill(block, true=true):
            @pl.when(place[0] == (true // 2) ^ (block // 2))
            def _():
                offset = pl.multiple_of(meta[true], ALIGN)
                low, high = joined(place, refs, block, rows)
                rows_ref[pl.ds(offset, rows), :LANES] = low
                rows_ref[pl.ds(offset, rows), LANES:] = high

        for piece in range(4):
            fill(piece * 2 + true % 2)
    tail = pl.multiple_of(meta[END], ALIGN)
    rows_ref[pl.ds(tail, TILE), :] = jnp.zeros((TILE, rows_ref.shape[1]), BF16)


def load_line(meta, lines, out_ref, fill):
    rows = lines[0].shape[1]
    out_ref[...] = jnp.full_like(out_ref, fill)
    lane = lax.broadcasted_iota(jnp.int32, (1, rows + LANES), 1)
    for block in range(BLOCKS):
        offset = meta[block]
        shift = lax.rem(offset, LANES)
        base = pl.multiple_of(offset - shift, LANES)
        wide = jnp.concatenate([lines[block], jnp.zeros((1, LANES), F32)], axis=1)
        wide = pltpu.roll(jnp.broadcast_to(wide, (8, rows + LANES)), shift, axis=1)[:1]
        there = (lane >= shift) & (lane < shift + meta[BLOCKS + block])
        out_ref[:, pl.ds(base, rows + LANES)] = jnp.where(
            there, wide, out_ref[:, pl.ds(base, rows + LANES)]
        )


def place_blocks(place, meta, refs, rows):
    for block in range(BLOCKS):
        piece, side = block // 2, block % 2
        info = refs[piece][side, rows:].astype(F32) + refs[4 + piece][side, rows:].astype(F32)
        meta[BLOCKS + true_block(place, block)] = jnp.sum(info).astype(jnp.int32)
    end = jnp.int32(0)
    for block in range(BLOCKS):
        meta[block] = end
        end = end + (meta[BLOCKS + block] + (ALIGN - 1)) // ALIGN * ALIGN
    meta[END] = end
    meta[TILES] = (end + (TILE - 1)) // TILE


def expo_kernel(place, *refs):
    pieces, (top_ref, proto_ref), refs = refs[:8], refs[8:10], refs[10:]
    expo_ref, col_ref, valid_ref, meta, rows_ref, line_ref, acc_ref, own_ref, sem = refs
    rows = top_ref.shape[2]
    protos = own_protos(place, proto_ref, own_ref, sem)
    protos.start()
    place_blocks(place, meta, pieces, rows)
    load_rows(place, meta, pieces, rows_ref, rows)
    lines = [jnp.maximum(top_ref[2 * block], top_ref[2 * block + 1]) for block in range(BLOCKS)]
    load_line(meta, lines, line_ref, FAR)
    valid_ref[...] = jnp.where(line_ref[:, : valid_ref.shape[1]] < 0.5 * FAR, 1.0, 0.0)
    acc_ref[...] = jnp.zeros_like(acc_ref)
    protos.wait()
    chunk = 512
    count = own_ref.shape[0]

    @pl.loop(0, meta[TILES])
    def _(tile):
        start = pl.multiple_of(tile * TILE, TILE)
        feats = jnp.transpose(rows_ref[pl.ds(start, TILE), :])
        top = line_ref[:, pl.ds(start, TILE)]
        for k in range(0, count, chunk):
            logit = jnp.dot(own_ref[k : k + chunk], feats, preferred_element_type=F32)
            expo = jnp.exp((logit - top) * (1 / teacher_temp))
            expo_ref[tile, k : k + chunk] = expo.astype(BF16)
            acc_ref[k : k + chunk] += fold(expo)

    col_ref[:, :count] = as_row(acc_ref[...])
    col_ref[:, count:] = jnp.zeros((1, LANES), F32) + jnp.sum(valid_ref[...])


def fold(block):
    total = block[:, :LANES]
    for lane in range(LANES, block.shape[1], LANES):
        total = total + block[:, lane : lane + LANES]
    return total


def expo_step(place, pieces, tops, protos):
    rows = tops.shape[2]
    width = protos.shape[1]
    count = protos.shape[0] // BLOCKS
    total = BLOCKS * rows
    return pl.pallas_call(
        expo_kernel,
        out_shape=(
            pltpu.VMEM((total // TILE, count, TILE), BF16),
            jax.ShapeDtypeStruct((1, count + LANES), F32),
            jax.ShapeDtypeStruct((1, total), F32),
            jax.ShapeDtypeStruct((24,), jnp.int32),
        ),
        in_specs=[smem()] + [vmem()] * 9 + [hbm()],
        out_specs=(vmem(), vmem(), vmem(), smem()),
        scratch_shapes=[
            pltpu.VMEM((total + TILE, width), BF16),
            pltpu.VMEM((1, total + LANES), F32),
            pltpu.VMEM((count, LANES), F32),
            pltpu.VMEM((count, width), BF16),
            pltpu.SemaphoreType.DMA,
        ],
        compiler_params=params(26),
        cost_estimate=cost(count * total * width * 2),
        name="expo",
    )(place, *[streamed(piece) for piece in pieces], tops, streamed(protos))


def col_scale_of(total_ref, count, proto_total):
    return 1.0 / (proto_total * total_ref[:, :count])


def two_rows(value):
    high, low = split(value)
    which = lax.broadcasted_iota(jnp.int32, (16, value.shape[1]), 0)
    return jnp.where(which == 0, high.astype(F32), jnp.where(which == 1, low.astype(F32), 0.0)).astype(BF16)


def row_kernel(proto_total, meta, total_ref, expo_ref, out_ref):
    lhs = two_rows(col_scale_of(total_ref, expo_ref.shape[1], proto_total))
    out_ref[...] = jnp.zeros_like(out_ref)

    @pl.loop(0, meta[TILES])
    def _(tile):
        start = pl.multiple_of(tile * TILE, TILE)
        both = jnp.dot(lhs, expo_ref[tile], preferred_element_type=F32)
        out_ref[:, pl.ds(start, TILE)] = both[:1] + both[1:2]


def row_step(meta, total, expo, proto_total):
    tiles, count, _ = expo.shape
    return pl.pallas_call(
        functools.partial(row_kernel, proto_total),
        out_shape=jax.ShapeDtypeStruct((1, tiles * TILE), F32),
        in_specs=[smem(), vmem(), vmem()],
        out_specs=vmem(),
        compiler_params=params(10),
        cost_estimate=cost(count * tiles * TILE * 400),
        name="row_step",
    )(meta, total, pinned(expo))


def weights_of(total_ref, valid_ref):
    valid = valid_ref[...]
    return valid / jnp.where(valid > 0, total_ref[...], 1.0)


def col_kernel(meta, total_ref, valid_ref, expo_ref, out_ref, line_ref, acc_ref):
    line_ref[...] = weights_of(total_ref, valid_ref)
    acc_ref[...] = jnp.zeros_like(acc_ref)
    chunk = 64

    @pl.loop(0, meta[TILES])
    def _(tile):
        start = pl.multiple_of(tile * TILE, TILE)
        weight = line_ref[:, pl.ds(start, TILE)]
        for k in range(0, acc_ref.shape[0], chunk):
            acc_ref[k : k + chunk] += fold(expo_ref[tile, k : k + chunk].astype(F32) * weight)

    out_ref[...] = as_row(acc_ref[...])


def col_step(meta, total, valid, expo):
    tiles, count, _ = expo.shape
    return pl.pallas_call(
        col_kernel,
        out_shape=jax.ShapeDtypeStruct((1, count), F32),
        in_specs=[smem()] + [vmem()] * 3,
        out_specs=vmem(),
        scratch_shapes=[pltpu.VMEM((1, tiles * TILE), F32), pltpu.VMEM((count, LANES), F32)],
        compiler_params=params(10),
        cost_estimate=cost(count * tiles * TILE * 400),
        name="col_step",
    )(meta, total, valid, pinned(expo))


def store_features(place, meta, rows_ref, keep_refs, give_refs):
    rows = keep_refs[0].shape[1]
    for block in range(BLOCKS):
        offset = pl.multiple_of(meta[true_block(place, block)], ALIGN)
        piece, side = block // 2, block % 2
        low = rows_ref[pl.ds(offset, rows), :LANES]
        high = rows_ref[pl.ds(offset, rows), LANES:]
        first = place[1] == 0
        keep_refs[piece][side] = jnp.where(first, low, high)
        give_refs[piece][side] = jnp.where(first, high, low)


def store_protos(place, acc_ref, out_refs):
    rows = out_refs[0].shape[0]
    for piece in range(len(out_refs)):
        start = pl.multiple_of((place[2] ^ piece) * rows, rows)
        out_refs[piece][...] = acc_ref[pl.ds(start, rows), :].astype(BF16)


def student_kernel(place, meta, *refs):
    pieces, lse_refs, proto_ref, refs = refs[:8], refs[8:12], refs[12], refs[13:]
    grads, keeps, gives, refs = refs[:4], refs[4:8], refs[8:12], refs[12:]
    rows_ref, line_ref, acc_ref, sums_ref, own_ref, sem = refs
    rows = pieces[0].shape[1]
    protos = own_protos(place, proto_ref, own_ref, sem)
    protos.start()
    load_rows(place, meta, pieces, rows_ref, rows)
    lines = []
    for block in range(BLOCKS):
        line = lse_refs[0][block % 2]
        for piece in range(1, 4):
            line = jnp.where((place[0] ^ piece) == block // 2, lse_refs[piece][block % 2], line)
        lines.append(line)
    load_line(meta, lines, line_ref, FAR)
    acc_ref[...] = jnp.zeros_like(acc_ref)
    sums_ref[...] = jnp.zeros_like(sums_ref)
    protos.wait()
    turned_protos = turn(own_ref)
    chunk = 512

    @pl.loop(0, meta[TILES])
    def _(tile):
        start = pl.multiple_of(tile * TILE, TILE)
        feats = rows_ref[pl.ds(start, TILE), :]
        across = jnp.transpose(feats)
        lse = line_ref[:, pl.ds(start, TILE)]
        turned = jnp.zeros((own_ref.shape[1], TILE), F32)
        for k in range(0, own_ref.shape[0], chunk):
            logit = jnp.dot(own_ref[k : k + chunk], across, preferred_element_type=F32)
            probs = jnp.exp(logit * (1 / student_temp) - lse).astype(BF16)
            acc_ref[k : k + chunk] += jnp.dot(probs, feats, preferred_element_type=F32)
            turned += jnp.dot(turned_protos[:, k : k + chunk], probs, preferred_element_type=F32)
        sums_ref[pl.ds(start, TILE), :] = jnp.transpose(turned).astype(BF16)

    store_features(place, meta, sums_ref, keeps, gives)
    store_protos(place, acc_ref, grads)


def student_step(place, meta, pieces, lses, protos):
    rows = lses[0].shape[2]
    width = protos.shape[1]
    count = protos.shape[0] // BLOCKS
    total = BLOCKS * rows
    grad = jax.ShapeDtypeStruct((count // 4, width), BF16)
    feat = jax.ShapeDtypeStruct((2, rows, LANES), BF16)
    out = pl.pallas_call(
        student_kernel,
        out_shape=(grad,) * 4 + (feat,) * 8,
        in_specs=[smem()] * 2 + [vmem()] * 12 + [hbm()],
        out_specs=(vmem(),) * 12,
        scratch_shapes=[
            pltpu.VMEM((total + TILE, width), BF16),
            pltpu.VMEM((1, total + LANES), F32),
            pltpu.VMEM((count, width), F32),
            pltpu.VMEM((total, width), BF16),
            pltpu.VMEM((count, width), BF16),
            pltpu.SemaphoreType.DMA,
        ],
        compiler_params=params(26),
        cost_estimate=cost(count * total * width * 6),
        name="student",
    )(place, meta, *pieces, *lses, streamed(protos))
    return out[:4], out[4:8], out[8:]


def feature_kernel(proto_total, place, meta, total_ref, expo_ref, proto_ref, *refs):
    keeps, gives, (sums_ref, own_ref, sem) = refs[:4], refs[4:8], refs[8:]
    protos = own_protos(place, proto_ref, own_ref, sem)
    protos.start()
    scale = col_scale_of(total_ref, expo_ref.shape[1], proto_total)
    sums_ref[...] = jnp.zeros_like(sums_ref)
    protos.wait()
    scaled = (turn(own_ref).astype(F32) * scale).astype(BF16)

    @pl.loop(0, meta[TILES])
    def _(tile):
        start = pl.multiple_of(tile * TILE, TILE)
        turned = jnp.dot(scaled, expo_ref[tile], preferred_element_type=F32)
        sums_ref[pl.ds(start, TILE), :] = jnp.transpose(turned).astype(BF16)

    store_features(place, meta, sums_ref, keeps, gives)


def feature_step(place, meta, total, expo, protos, proto_total):
    tiles, count, _ = expo.shape
    width = protos.shape[1]
    feat = jax.ShapeDtypeStruct((2, tiles * TILE // BLOCKS, LANES), BF16)
    out = pl.pallas_call(
        functools.partial(feature_kernel, proto_total),
        out_shape=(feat,) * 8,
        in_specs=[smem()] * 2 + [vmem()] * 2 + [hbm()],
        out_specs=(vmem(),) * 8,
        scratch_shapes=[
            pltpu.VMEM((tiles * TILE, width), BF16),
            pltpu.VMEM((count, width), BF16),
            pltpu.SemaphoreType.DMA,
        ],
        compiler_params=params(18),
        cost_estimate=cost(count * tiles * TILE * width * 2),
        name="feature_step",
    )(place, meta, total, pinned(expo), streamed(protos))
    return out[:4], out[4:]


def grad_kernel(place, meta, total_ref, valid_ref, *refs):
    pieces, expo_ref, grads, refs = refs[:8], refs[8], refs[9:13], refs[13:]
    weight_ref, rows_ref, acc_ref = refs
    load_rows(place, meta, pieces, rows_ref, pieces[0].shape[1])
    weight_ref[...] = weights_of(total_ref, valid_ref)
    acc_ref[...] = jnp.zeros_like(acc_ref)
    chunk = 512

    @pl.loop(0, meta[TILES])
    def _(tile):
        start = pl.multiple_of(tile * TILE, TILE)
        weight = weight_ref[:, pl.ds(start, TILE)]
        feats = rows_ref[pl.ds(start, TILE), :].astype(F32)
        parts = []
        for lane in range(0, TILE, LANES):
            column = jnp.transpose(jnp.broadcast_to(weight[:, lane : lane + LANES], (LANES, LANES)))
            part = feats[lane : lane + LANES]
            parts.append(
                jnp.concatenate(
                    [part[:, d : d + LANES] * column for d in range(0, part.shape[1], LANES)], axis=1
                )
            )
        scaled = jnp.concatenate(parts, axis=0).astype(BF16)
        for k in range(0, acc_ref.shape[0], chunk):
            acc_ref[k : k + chunk] += jnp.dot(
                expo_ref[tile, k : k + chunk], scaled, preferred_element_type=F32
            )

    store_protos(place, acc_ref, grads)


def grad_step(place, meta, total, valid, pieces, expo):
    tiles, count, _ = expo.shape
    width = 2 * LANES
    rows = tiles * TILE
    out = pl.pallas_call(
        grad_kernel,
        out_shape=(jax.ShapeDtypeStruct((count // 4, width), BF16),) * 4
        + (jax.ShapeDtypeStruct((1, rows), F32),),
        in_specs=[smem()] * 2 + [vmem()] * 11,
        out_specs=(vmem(),) * 5,
        scratch_shapes=[
            pltpu.VMEM((rows + TILE, width), BF16),
            pltpu.VMEM((count, width), F32),
        ],
        compiler_params=params(20),
        cost_estimate=cost(count * rows * width * 2),
        name="grad_step",
    )(place, meta, total, valid, *pieces, pinned(expo))
    return out[:4], out[4]


def swap(value, axis):
    return lax.ppermute(value, axis, [(0, 1), (1, 0)])


def from_xor(value, axis, mask):
    return lax.ppermute(value, axis, [(i, i ^ mask) for i in range(4)])


def exchange(many, axes):
    return lax.all_to_all(many, axes, 0, 0, tiled=True)


def spread(value, axes, size):
    return exchange(jnp.broadcast_to(value[None], (size,) + value.shape), axes)


def tie(*values):
    return lax.optimization_barrier(values)


def pair_of(half):
    beside = swap(half, "xl")
    low = lax.axis_index("xl") == 0
    return jnp.stack([jnp.where(low, half, beside), jnp.where(low, beside, half)])


def gather_along(pair):
    return [pair] + [from_xor(pair, "y", mask) for mask in (1, 3, 2)]


def ordered(pieces):
    own, one, three, two = pieces
    return [own, one, two, three]


def scatter_protos(pieces):
    return [pieces[0]] + [from_xor(pieces[mask], "z", mask) for mask in (1, 3, 2)]


def scatter_cores(keeps, gives):
    return [
        (keep.astype(F32) + swap(give, "c").astype(F32)).astype(BF16) for keep, give in zip(keeps, gives)
    ]


def scatter_features(totals):
    total = totals[0].astype(F32)
    for mask in (1, 3, 2):
        total = total + from_xor(totals[mask], "y", mask).astype(F32)
    total = total.astype(BF16)
    side = lax.axis_index("xl")
    keep = lax.dynamic_index_in_dim(total, side, 0, keepdims=False)
    give = lax.dynamic_index_in_dim(total, 1 - side, 0, keepdims=False)
    return keep.astype(F32) + swap(give, "xl").astype(F32)


def ring_sum(value, axes, masks, work=None, *extra):
    value, extra = tie(value, extra)
    got = [lax.ppermute(value, axes, [(i, i ^ mask) for i in range(4)]) for mask in masks]
    out = work(*extra) if work else extra
    got, out = tie(got, out)
    return value + got[0] + got[1] + got[2], out


def local(student, teacher, prototypes, masked):
    rows, width = student.shape
    y, xl, z = lax.axis_index("y"), lax.axis_index("xl"), lax.axis_index("z")
    xh, core = lax.axis_index("xh"), lax.axis_index("c")
    block_id = y * 2 + xl
    count = prototypes.shape[0] // BLOCKS
    proto_total = prototypes.shape[0] * 4
    place = jnp.stack([y, core, z, block_id]).astype(jnp.int32)
    far_first = {"z": ("z", (2, 1, 3)), "y": ("y", (2, 1, 3)), "x": (("xl", "xh"), (1, 2, 3))}

    teach, stud = compact(masked.astype(F32)[None], streamed(teacher), streamed(student))
    half, teach = tie(lax.dynamic_slice_in_dim(teach, core * LANES, LANES, 1), teach)
    pair = pair_of(half)
    top = row_max(teach, streamed(prototypes), rows, 0, 2)
    pair, top, teach = tie(pair, top, teach)
    mine = gather_along(pair)
    top = jnp.maximum(top, row_max(teach, streamed(prototypes), rows, 1, 2))
    tops = spread(jnp.maximum(top, swap(top, "c")), ("y", "xl", "xh"), 16)
    other = [swap(piece, "c") for piece in mine]
    mine, other, tops, stud, masked = tie(mine, other, tops, stud, masked)
    expo, col, valid, meta = expo_step(place, ordered(mine) + ordered(other), tops, prototypes)
    col, stud, masked = tie(col, stud, masked)

    def merged(one, two):
        high = jnp.maximum(one[0], two[0])
        return high, one[1] * jnp.exp((one[0] - high) / student_temp) + two[1] * jnp.exp(
            (two[0] - high) / student_temp
        )

    def soft_half(part):
        return lambda stud: row_soft(stud, streamed(prototypes), part, 2)

    col, soft = ring_sum(col, *far_first["z"], soft_half(0), stud)
    mask_total = col[0, count]
    row = row_step(meta, col, expo, proto_total)
    row = row + swap(row, "c")
    stud_half = lax.dynamic_slice_in_dim(stud, core * LANES, LANES, 1)
    row, (soft_two, stud_pair) = ring_sum(
        row, *far_first["x"], lambda stud, half: (soft_half(1)(stud), pair_of(half)), stud, stud_half
    )
    row, (soft, stud_mine) = ring_sum(
        row,
        *far_first["y"],
        lambda one, two, pair: (merged(merged(one, two), [swap(part, "c") for part in merged(one, two)]), gather_along(pair)),
        soft,
        soft_two,
        stud_pair,
    )

    col = col_step(meta, row, valid, expo)
    col, (soft, stud_other) = ring_sum(
        col,
        *far_first["z"],
        lambda soft, mine: (merged(soft, [swap(part, "xh") for part in soft]), [swap(piece, "c") for piece in mine]),
        soft,
        stud_mine,
    )
    stud_pieces = ordered(stud_mine) + ordered(stud_other)
    row = row_step(meta, col, expo, proto_total)
    row = row + swap(row, "c")

    def spread_lse(soft):
        lse = soft[0] / student_temp + jnp.log(soft[1])
        beside = swap(lse, "xl")
        pair = jnp.stack([jnp.where(xl == 0, lse, beside), jnp.where(xl == 0, beside, lse)])
        return ordered(gather_along(pair))

    row, lses = ring_sum(row, *far_first["x"], spread_lse, soft)
    row, (stud_grad, stud_keep, stud_give) = ring_sum(
        row,
        *far_first["y"],
        lambda lses: student_step(place, meta, stud_pieces, lses, prototypes),
        lses,
    )

    col = col_step(meta, row, valid, expo)
    col, stud_feat = ring_sum(col, *far_first["z"], scatter_cores, stud_keep, stud_give)
    row = row_step(meta, col, expo, proto_total)
    row = row + swap(row, "c")
    row, (plan_keep, plan_give) = ring_sum(
        row,
        *far_first["x"],
        lambda total: feature_step(place, meta, total, expo, prototypes, proto_total),
        col,
    )
    row, plan_feat = ring_sum(row, *far_first["y"], scatter_cores, plan_keep, plan_give)
    plan_grad, weights = grad_step(place, meta, row, valid, stud_pieces, expo)
    plan_grad, plan_feat, stud_feat, stud_grad, weights, masked = tie(
        plan_grad, plan_feat, stud_feat, stud_grad, weights, masked
    )

    plan_parts = scatter_protos(plan_grad)
    stud_parts = scatter_protos(stud_grad)
    stud_own = scatter_features(stud_feat)
    plan_own = scatter_features(plan_feat)

    weight_row = lax.dynamic_slice(weights, (0, meta[block_id]), (1, rows))
    own = (stud_own - weight_row[0][:, None] * plan_own).astype(BF16)
    place_row = jnp.where(masked > 0, jnp.cumsum(masked) - 1, -1)
    onehot = (place_row[:, None] == jnp.arange(rows)[None, :]).astype(BF16)
    own = jnp.dot(onehot, own, preferred_element_type=F32)
    keep = lax.dynamic_slice_in_dim(own, xh * (rows // 2), rows // 2, 0)
    give = lax.dynamic_slice_in_dim(own, (1 - xh) * (rows // 2), rows // 2, 0)
    own = keep + swap(give.astype(BF16), "xh").astype(F32)
    quarter = rows // 4
    keep = lax.dynamic_slice_in_dim(own, core * quarter, quarter, 0)
    give = lax.dynamic_slice_in_dim(own, (1 - core) * quarter, quarter, 0)
    got = swap(give.astype(BF16), "c").astype(F32)
    both = jnp.where(core == 0, jnp.concatenate([keep, got], 1), jnp.concatenate([got, keep], 1))
    feature_grad = (both * (math.sqrt(proto_total) / student_temp)).astype(BF16)

    scale = 1.0 / (proto_total * lax.dynamic_slice_in_dim(col[0], z * (count // 4), count // 4, 0))
    stud_sum = sum(part.astype(F32) for part in stud_parts)
    plan_sum = sum(part.astype(F32) for part in plan_parts)
    proto_grad = (
        (stud_sum - scale[:, None] * plan_sum) * (proto_total / jnp.sqrt(mask_total))
    ).astype(BF16)
    return feature_grad, proto_grad


def solution(mesh):
    fine = Mesh(mesh.devices.reshape(4, 2, 4, 2, 2), ("y", "xl", "z", "xh", "c"))
    rows, protos = ("y", "xl", "z"), ("xh", "c")
    in_specs = (P(rows, None), P(rows, None), P(protos, None), P(rows))
    out_specs = (P(rows + protos, None), P(protos + rows, None))
    return jax.shard_map(local, mesh=fine, in_specs=in_specs, out_specs=out_specs, check_vma=False)
```

```python
import functools
import math

import jax
import jax.numpy as jnp
from jax import lax
from jax.experimental import pallas as pl
from jax.experimental.pallas import tpu as pltpu
from jax.sharding import Mesh
from jax.sharding import PartitionSpec as P

ITERS = 3
student_temp = 0.1
teacher_temp = 0.05

F32 = jnp.float32
BF16 = jnp.bfloat16
TILE = 512
LANES = 128
ALIGN = 16
FAR = 1e30
INFO = 16
BLOCKS = 8
END, TILES = 2 * BLOCKS, 2 * BLOCKS + 1
MIB = 2**20

NT = (((1,), (1,)), ((), ()))


def params(mib):
    return pltpu.CompilerParams(vmem_limit_bytes=mib * MIB)


def vmem():
    return pl.BlockSpec(memory_space=pltpu.VMEM)


def smem():
    return pl.BlockSpec(memory_space=pltpu.SMEM)


def hbm():
    return pl.BlockSpec(memory_space=pltpu.HBM)


def pinned(value):
    return pltpu.with_memory_space_constraint(value, pltpu.VMEM)


def streamed(value):
    return pltpu.with_memory_space_constraint(value, pltpu.HBM)


def own_protos(place, proto_ref, own_ref, sem):
    count = own_ref.shape[0]
    start = pl.multiple_of(place[3] * count, count)
    return pltpu.make_async_copy(proto_ref.at[pl.ds(start, count)], own_ref, sem)


def turn(own_ref):
    chunk = 512
    return jnp.concatenate(
        [jnp.transpose(own_ref[k : k + chunk]) for k in range(0, own_ref.shape[0], chunk)], axis=1
    )


def split(value):
    high = value.astype(BF16)
    low = (value - high.astype(F32)).astype(BF16)
    return high, low


def as_row(block):
    pieces = []
    for start in range(0, block.shape[0], LANES):
        part = block[start : start + LANES]
        total = part[:, :LANES]
        for lane in range(LANES, block.shape[1], LANES):
            total = total + part[:, lane : lane + LANES]
        pieces.append(jnp.sum(jnp.transpose(total), axis=0, keepdims=True))
    return jnp.concatenate(pieces, axis=1)


def compact_kernel(mask_ref, teach_ref, stud_ref, teach_out, stud_out):
    rows, width = teach_ref.shape
    mask = mask_ref[...]
    down = lax.broadcasted_iota(jnp.int32, (rows, rows), 0)
    along = lax.broadcasted_iota(jnp.int32, (rows, rows), 1)
    upper = jnp.where(down <= along, 1.0, 0.0).astype(BF16)
    many = jnp.broadcast_to(mask, (16, rows)).astype(BF16)
    rank = jnp.dot(many, upper, preferred_element_type=F32)[:1]
    place = jnp.where(mask > 0, rank - 1.0, -1.0)
    onehot = jnp.where(down.astype(F32) == place, 1.0, 0.0).astype(BF16)
    teach_out[:rows] = jnp.dot(onehot, teach_ref[...], preferred_element_type=F32).astype(BF16)
    stud_out[:rows] = jnp.dot(onehot, stud_ref[...], preferred_element_type=F32).astype(BF16)
    which = lax.broadcasted_iota(jnp.int32, (INFO, width), 0)
    info = jnp.zeros((INFO, width), F32)
    for piece in range(rows // width):
        info = jnp.where(which == piece, mask[:, piece * width : (piece + 1) * width], info)
    teach_out[rows:] = info.astype(BF16)
    stud_out[rows:] = info.astype(BF16)


def compact(mask_row, teacher, student):
    rows, width = teacher.shape
    return pl.pallas_call(
        compact_kernel,
        out_shape=(jax.ShapeDtypeStruct((rows + INFO, width), BF16),) * 2,
        in_specs=[vmem()] * 3,
        out_specs=(vmem(), vmem()),
        compiler_params=params(12),
        name="compact",
    )(mask_row, teacher, student)


def max_kernel(teach_ref, proto_ref, out_ref, turned_ref):
    rows = out_ref.shape[1]
    chunk = 512

    @pl.when(pl.program_id(0) == 0)
    def _():
        out_ref[...] = jnp.full_like(out_ref, -FAR)
        turned_ref[...] = jnp.transpose(teach_ref[:rows])

    best = out_ref[...]
    for start in range(0, proto_ref.shape[0], chunk):
        logit = jnp.dot(proto_ref[start : start + chunk], turned_ref[...], preferred_element_type=F32)
        best = jnp.maximum(best, jnp.max(logit, axis=0, keepdims=True))
    out_ref[...] = best


def row_max(feats, protos, rows, part, parts):
    count, width = protos.shape
    block = 2048
    steps = count // block // parts
    return pl.pallas_call(
        max_kernel,
        grid=(steps,),
        out_shape=jax.ShapeDtypeStruct((1, rows), F32),
        in_specs=[
            pl.BlockSpec(feats.shape, lambda i: (0, 0)),
            pl.BlockSpec((block, width), lambda i: (i + part * steps, 0)),
        ],
        out_specs=pl.BlockSpec((1, rows), lambda i: (0, 0)),
        scratch_shapes=[pltpu.VMEM((width, rows), BF16)],
        compiler_params=params(14),
        cost_estimate=cost(2 * count * width * rows // parts),
        name="row_max",
    )(feats, protos)


def soft_kernel(feat_ref, proto_ref, top_ref, sum_ref, turned_ref):
    chunk = 512

    @pl.when(pl.program_id(0) == 0)
    def _():
        top_ref[...] = jnp.full_like(top_ref, -FAR)
        sum_ref[...] = jnp.zeros_like(sum_ref)
        turned_ref[...] = jnp.transpose(feat_ref[: turned_ref.shape[1]])

    top = top_ref[...]
    total = sum_ref[...]
    for start in range(0, proto_ref.shape[0], chunk):
        logit = jnp.dot(proto_ref[start : start + chunk], turned_ref[...], preferred_element_type=F32)
        higher = jnp.maximum(top, jnp.max(logit, axis=0, keepdims=True))
        total = total * jnp.exp((top - higher) * (1 / student_temp)) + jnp.sum(
            jnp.exp((logit - higher) * (1 / student_temp)), axis=0, keepdims=True
        )
        top = higher
    top_ref[...] = top
    sum_ref[...] = total


def row_soft(feats, protos, rows, part, parts):
    count, width = protos.shape
    block = 2048
    steps = count // block // parts
    row = pl.BlockSpec((1, rows), lambda i: (0, 0))
    return pl.pallas_call(
        soft_kernel,
        grid=(steps,),
        out_shape=(jax.ShapeDtypeStruct((1, rows), F32),) * 2,
        in_specs=[
            pl.BlockSpec(feats.shape, lambda i: (0, 0)),
            pl.BlockSpec((block, width), lambda i: (i + part * steps, 0)),
        ],
        out_specs=(row, row),
        scratch_shapes=[pltpu.VMEM((width, rows), BF16)],
        compiler_params=params(14),
        cost_estimate=cost(3 * count * width * rows // parts),
        name="row_soft",
    )(feats, protos)


def cost(flops):
    return pl.CostEstimate(flops=flops, bytes_accessed=2**20, transcendentals=0)


def joined(place, refs, block, rows):
    piece, side = block // 2, block % 2
    mine = refs[piece][side, :rows]
    other = refs[4 + piece][side, :rows]
    first = place[1] == 0
    return jnp.where(first, mine, other), jnp.where(first, other, mine)


def true_block(place, block):
    return (place[0] ^ (block // 2)) * 2 + block % 2


def load_rows(place, meta, refs, rows_ref, rows):
    for true in range(BLOCKS):

        def fill(block, true=true):
            @pl.when(place[0] == (true // 2) ^ (block // 2))
            def _():
                offset = pl.multiple_of(meta[true], ALIGN)
                low, high = joined(place, refs, block, rows)
                rows_ref[pl.ds(offset, rows), :LANES] = low
                rows_ref[pl.ds(offset, rows), LANES:] = high

        for piece in range(4):
            fill(piece * 2 + true % 2)
    tail = pl.multiple_of(meta[END], ALIGN)
    rows_ref[pl.ds(tail, TILE), :] = jnp.zeros((TILE, rows_ref.shape[1]), BF16)


def load_line(meta, lines, out_ref, fill):
    rows = lines[0].shape[1]
    out_ref[...] = jnp.full_like(out_ref, fill)
    lane = lax.broadcasted_iota(jnp.int32, (1, rows + LANES), 1)
    for block in range(BLOCKS):
        offset = meta[block]
        shift = lax.rem(offset, LANES)
        base = pl.multiple_of(offset - shift, LANES)
        wide = jnp.concatenate([lines[block], jnp.zeros((1, LANES), F32)], axis=1)
        wide = pltpu.roll(jnp.broadcast_to(wide, (8, rows + LANES)), shift, axis=1)[:1]
        there = (lane >= shift) & (lane < shift + meta[BLOCKS + block])
        out_ref[:, pl.ds(base, rows + LANES)] = jnp.where(
            there, wide, out_ref[:, pl.ds(base, rows + LANES)]
        )


def place_blocks(place, meta, refs, rows):
    for block in range(BLOCKS):
        piece, side = block // 2, block % 2
        info = refs[piece][side, rows:].astype(F32) + refs[4 + piece][side, rows:].astype(F32)
        meta[BLOCKS + true_block(place, block)] = jnp.sum(info).astype(jnp.int32)
    end = jnp.int32(0)
    for block in range(BLOCKS):
        meta[block] = end
        end = end + (meta[BLOCKS + block] + (ALIGN - 1)) // ALIGN * ALIGN
    meta[END] = end
    meta[TILES] = (end + (TILE - 1)) // TILE


def expo_kernel(place, *refs):
    pieces, tops, proto_ref, refs = refs[:8], refs[8:12], refs[12], refs[13:]
    expo_ref, col_ref, valid_ref, meta, rows_ref, line_ref, acc_ref, own_ref, sem = refs
    rows = tops[0].shape[2]
    protos = own_protos(place, proto_ref, own_ref, sem)
    protos.start()
    place_blocks(place, meta, pieces, rows)
    load_rows(place, meta, pieces, rows_ref, rows)
    lines = []
    for block in range(BLOCKS):
        line = tops[0][block % 2]
        for piece in range(1, 4):
            line = jnp.where((place[0] ^ piece) == block // 2, tops[piece][block % 2], line)
        lines.append(line)
    load_line(meta, lines, line_ref, FAR)
    valid_ref[...] = jnp.where(line_ref[:, : valid_ref.shape[1]] < 0.5 * FAR, 1.0, 0.0)
    acc_ref[...] = jnp.zeros_like(acc_ref)
    protos.wait()
    chunk = 512
    count = own_ref.shape[0]

    @pl.loop(0, meta[TILES])
    def _(tile):
        start = pl.multiple_of(tile * TILE, TILE)
        feats = jnp.transpose(rows_ref[pl.ds(start, TILE), :])
        top = line_ref[:, pl.ds(start, TILE)]
        for k in range(0, count, chunk):
            logit = jnp.dot(own_ref[k : k + chunk], feats, preferred_element_type=F32)
            expo = jnp.exp((logit - top) * (1 / teacher_temp))
            expo_ref[tile, k : k + chunk] = expo.astype(BF16)
            acc_ref[k : k + chunk] += fold(expo)

    col_ref[:, :count] = as_row(acc_ref[...])
    col_ref[:, count:] = jnp.zeros((1, LANES), F32) + jnp.sum(valid_ref[...])


def fold(block):
    total = block[:, :LANES]
    for lane in range(LANES, block.shape[1], LANES):
        total = total + block[:, lane : lane + LANES]
    return total


def expo_step(place, pieces, tops, protos):
    rows = tops[0].shape[2]
    width = protos.shape[1]
    count = protos.shape[0] // BLOCKS
    total = BLOCKS * rows
    return pl.pallas_call(
        expo_kernel,
        out_shape=(
            pltpu.VMEM((total // TILE, count, TILE), BF16),
            jax.ShapeDtypeStruct((1, count + LANES), F32),
            jax.ShapeDtypeStruct((1, total), F32),
            jax.ShapeDtypeStruct((24,), jnp.int32),
        ),
        in_specs=[smem()] + [vmem()] * 12 + [hbm()],
        out_specs=(vmem(), vmem(), vmem(), smem()),
        scratch_shapes=[
            pltpu.VMEM((total + TILE, width), BF16),
            pltpu.VMEM((1, total + LANES), F32),
            pltpu.VMEM((count, LANES), F32),
            pltpu.VMEM((count, width), BF16),
            pltpu.SemaphoreType.DMA,
        ],
        compiler_params=params(26),
        cost_estimate=cost(count * total * width * 2),
        name="expo",
    )(place, *pieces, *tops, streamed(protos))


def col_scale_of(total_ref, count, proto_total):
    return 1.0 / (proto_total * total_ref[:, :count])


def two_rows(value):
    high, low = split(value)
    which = lax.broadcasted_iota(jnp.int32, (16, value.shape[1]), 0)
    return jnp.where(which == 0, high.astype(F32), jnp.where(which == 1, low.astype(F32), 0.0)).astype(BF16)


def row_kernel(proto_total, with_lse, place, meta, total_ref, expo_ref, *refs):
    out_ref = refs[-1]
    lhs = two_rows(col_scale_of(total_ref, expo_ref.shape[1], proto_total))
    out_ref[...] = jnp.zeros_like(out_ref)
    if with_lse:
        lse_ref = refs[0]
        rows = lse_ref.shape[1]
        start = pl.multiple_of(rows * BLOCKS + place[3] * rows, rows)
        out_ref[:, pl.ds(start, rows)] = lse_ref[...] * 0.25

    @pl.loop(0, meta[TILES])
    def _(tile):
        start = pl.multiple_of(tile * TILE, TILE)
        both = jnp.dot(lhs, expo_ref[tile], preferred_element_type=F32)
        out_ref[:, pl.ds(start, TILE)] = both[:1] + both[1:2]


def row_step(place, meta, total, expo, proto_total, lse=None):
    tiles, count, _ = expo.shape
    more = () if lse is None else (lse,)
    return pl.pallas_call(
        functools.partial(row_kernel, proto_total, lse is not None),
        out_shape=jax.ShapeDtypeStruct((1, (1 + len(more)) * tiles * TILE), F32),
        in_specs=[smem()] * 2 + [vmem()] * (2 + len(more)),
        out_specs=vmem(),
        compiler_params=params(10),
        cost_estimate=cost(count * tiles * TILE * 400),
        name="row_step",
    )(place, meta, total, pinned(expo), *more)


def weights_of(total_ref, valid_ref):
    valid = valid_ref[...]
    return valid / jnp.where(valid > 0, total_ref[:, : valid.shape[1]], 1.0)


def col_kernel(meta, total_ref, valid_ref, expo_ref, out_ref, line_ref, acc_ref):
    line_ref[...] = weights_of(total_ref, valid_ref)
    acc_ref[...] = jnp.zeros_like(acc_ref)
    chunk = 64

    @pl.loop(0, meta[TILES])
    def _(tile):
        start = pl.multiple_of(tile * TILE, TILE)
        weight = line_ref[:, pl.ds(start, TILE)]
        for k in range(0, acc_ref.shape[0], chunk):
            acc_ref[k : k + chunk] += fold(expo_ref[tile, k : k + chunk].astype(F32) * weight)

    out_ref[...] = as_row(acc_ref[...])


def col_step(meta, total, valid, expo):
    tiles, count, _ = expo.shape
    return pl.pallas_call(
        col_kernel,
        out_shape=jax.ShapeDtypeStruct((1, count), F32),
        in_specs=[smem()] + [vmem()] * 3,
        out_specs=vmem(),
        scratch_shapes=[pltpu.VMEM((1, tiles * TILE), F32), pltpu.VMEM((count, LANES), F32)],
        compiler_params=params(10),
        cost_estimate=cost(count * tiles * TILE * 400),
        name="col_step",
    )(meta, total, valid, pinned(expo))


def load_kernel(place, meta, *refs):
    pieces, proto_ref, refs = refs[:8], refs[8], refs[9:]
    out_ref, rank_ref, own_out, turned_ref, rows_ref, own_ref, sem = refs
    protos = own_protos(place, proto_ref, own_ref, sem)
    protos.start()
    rows = pieces[0].shape[1] - INFO
    load_rows(place, meta, pieces, rows_ref, rows)
    out_ref[...] = rows_ref[...]
    masks = [jnp.zeros((1, rows), F32)] * BLOCKS
    for block in range(BLOCKS):
        low, high = joined(place, pieces, block, rows + INFO)
        low, high = low[rows:].astype(F32), high[rows:].astype(F32)
        line = []
        for index in range(rows // (2 * LANES)):
            line += [low[index : index + 1], high[index : index + 1]]
        line = jnp.concatenate(line, axis=1)
        for true in range(block % 2, BLOCKS, 2):
            masks[true] = jnp.where(true_block(place, block) == true, line, masks[true])
    masks = jnp.concatenate(masks, axis=0)
    down = lax.broadcasted_iota(jnp.int32, (rows, rows), 0)
    along = lax.broadcasted_iota(jnp.int32, (rows, rows), 1)
    upper = jnp.where(down <= along, 1.0, 0.0).astype(BF16)
    many = jnp.concatenate([masks, masks], axis=0).astype(BF16)
    rank = jnp.dot(many, upper, preferred_element_type=F32)[:BLOCKS]
    rank_ref[...] = jnp.where(masks > 0, rank - 1.0, -1.0)
    protos.wait()
    own_out[...] = own_ref[...]
    turned_ref[...] = turn(own_ref)


def load_step(place, meta, pieces, protos):
    rows = pieces[0].shape[1] - INFO
    width = protos.shape[1]
    count = protos.shape[0] // BLOCKS
    total = BLOCKS * rows
    return pl.pallas_call(
        load_kernel,
        out_shape=(
            jax.ShapeDtypeStruct((total + TILE, width), BF16),
            jax.ShapeDtypeStruct((BLOCKS, rows), F32),
            jax.ShapeDtypeStruct((count, width), BF16),
            jax.ShapeDtypeStruct((width, count), BF16),
        ),
        in_specs=[smem()] * 2 + [vmem()] * 8 + [hbm()],
        out_specs=(vmem(),) * 4,
        scratch_shapes=[
            pltpu.VMEM((total + TILE, width), BF16),
            pltpu.VMEM((count, width), BF16),
            pltpu.SemaphoreType.DMA,
        ],
        compiler_params=params(18),
        cost_estimate=cost(2**31),
        name="load_student",
    )(place, meta, *pieces, streamed(protos))


def student_kernel(part, place, meta, rows_ref, all_ref, own_ref, turned_ref, *refs):
    if part == 1:
        sums_in, refs = refs[0], refs[1:]
    grads, (sums_out, acc_ref, line_ref) = refs[:2], refs[2:]
    total = sums_out.shape[0]
    rows = total // BLOCKS
    load_line(
        meta, [all_ref[:, total + block * rows : total + (block + 1) * rows] for block in range(BLOCKS)], line_ref, FAR
    )
    acc_ref[...] = jnp.zeros_like(acc_ref)
    sums_out[...] = jnp.zeros_like(sums_out)
    chunk = grads[0].shape[0]

    @pl.loop(0, meta[TILES])
    def _(tile):
        start = pl.multiple_of(tile * TILE, TILE)
        feats = rows_ref[pl.ds(start, TILE), :]
        across = jnp.transpose(feats)
        lse = line_ref[:, pl.ds(start, TILE)]
        turned = jnp.zeros((turned_ref.shape[0], TILE), F32)
        for piece in range(2):
            k = pl.multiple_of((place[2] ^ (2 * part + piece)) * chunk, chunk)
            logit = jnp.dot(own_ref[pl.ds(k, chunk), :], across, preferred_element_type=F32)
            probs = jnp.exp(logit * (1 / student_temp) - lse).astype(BF16)
            acc_ref[piece] += jnp.dot(probs, feats, preferred_element_type=F32)
            turned += jnp.dot(turned_ref[:, pl.ds(k, chunk)], probs, preferred_element_type=F32)
        sums = jnp.transpose(turned)
        if part == 1:
            sums = sums + sums_in[pl.ds(start, TILE), :].astype(F32)
        sums_out[pl.ds(start, TILE), :] = sums.astype(BF16)

    for piece in range(2):
        grads[piece][...] = acc_ref[piece].astype(BF16)


def student_step(part, place, meta, rows, line, own, turned, *sums):
    width, count = turned.shape
    total = line.shape[1] // 2
    outs = (jax.ShapeDtypeStruct((count // 4, width), BF16),) * 2 + (jax.ShapeDtypeStruct((total, width), BF16),)
    return pl.pallas_call(
        functools.partial(student_kernel, part),
        out_shape=outs,
        in_specs=[smem()] * 2 + [vmem()] * (4 + len(sums)),
        out_specs=(vmem(),) * len(outs),
        scratch_shapes=[pltpu.VMEM((2, count // 4, width), F32), pltpu.VMEM((1, total + LANES), F32)],
        compiler_params=params(20),
        cost_estimate=cost(count * total * width * 3),
        name="student",
    )(place, meta, rows, line, own, turned, *sums)


def scaled_rows(feats, factor):
    parts = []
    for start in range(0, feats.shape[0], LANES):
        column = jnp.transpose(jnp.broadcast_to(factor[:, start : start + LANES], (LANES, LANES)))
        part = feats[start : start + LANES].astype(F32)
        parts.append(
            jnp.concatenate([part[:, d : d + LANES] * column for d in range(0, part.shape[1], LANES)], axis=1)
        )
    return jnp.concatenate(parts, axis=0)


def feature_kernel(proto_total, meta, total_ref, expo_ref, turned_ref, sums_ref):
    scale = col_scale_of(total_ref, expo_ref.shape[1], proto_total)
    sums_ref[...] = jnp.zeros_like(sums_ref)
    scaled = (turned_ref[...].astype(F32) * scale).astype(BF16)

    @pl.loop(0, meta[TILES])
    def _(tile):
        start = pl.multiple_of(tile * TILE, TILE)
        turned = jnp.dot(scaled, expo_ref[tile], preferred_element_type=F32)
        sums_ref[pl.ds(start, TILE), :] = jnp.transpose(turned).astype(BF16)


def feature_step(meta, total, expo, turned, proto_total):
    tiles, count, _ = expo.shape
    width = turned.shape[0]
    return pl.pallas_call(
        functools.partial(feature_kernel, proto_total),
        out_shape=jax.ShapeDtypeStruct((tiles * TILE, width), BF16),
        in_specs=[smem()] + [vmem()] * 3,
        out_specs=vmem(),
        compiler_params=params(14),
        cost_estimate=cost(count * tiles * TILE * width * 2),
        name="feature_step",
    )(meta, total, pinned(expo), turned)


def join_kernel(place, meta, total_ref, valid_ref, rank_ref, stud_ref, plan_ref, keep_ref, give_ref, weight_ref, sums_ref):
    weight_ref[...] = weights_of(total_ref, valid_ref)

    @pl.loop(0, meta[TILES])
    def _(tile):
        start = pl.multiple_of(tile * TILE, TILE)
        plan = scaled_rows(plan_ref[pl.ds(start, TILE), :], weight_ref[:, pl.ds(start, TILE)])
        sums_ref[pl.ds(start, TILE), :] = (stud_ref[pl.ds(start, TILE), :].astype(F32) - plan).astype(BF16)

    tail = pl.multiple_of(meta[TILES] * TILE, TILE)
    rows = rank_ref.shape[1]
    sums_ref[pl.ds(tail, rows), :] = jnp.zeros((rows, sums_ref.shape[1]), BF16)
    along = lax.broadcasted_iota(jnp.int32, (LANES, rows), 1).astype(F32)
    first = place[1] == 0
    for block in range(BLOCKS):
        offset = pl.multiple_of(meta[block], ALIGN)
        sums = sums_ref[pl.ds(offset, rows), :]
        pieces = []
        for start in range(0, rows, LANES):
            column = jnp.transpose(jnp.broadcast_to(rank_ref[block : block + 1, start : start + LANES], (LANES, LANES)))
            column = jnp.concatenate([column] * (rows // LANES), axis=1)
            onehot = jnp.where(column == along, 1.0, 0.0).astype(BF16)
            pieces.append(jnp.dot(onehot, sums, preferred_element_type=F32).astype(BF16))
        for half in range(2):
            low, high = pieces[2 * half], pieces[2 * half + 1]
            keep_ref[2 * block + half] = jnp.where(first, low, high)
            give_ref[2 * block + half] = jnp.where(first, high, low)


def join_step(place, meta, total, valid, rank, stud, plan):
    all_rows, width = stud.shape
    out = jax.ShapeDtypeStruct((2 * BLOCKS, LANES, width), BF16)
    return pl.pallas_call(
        join_kernel,
        out_shape=(out, out),
        in_specs=[smem()] * 2 + [vmem()] * 5,
        out_specs=(vmem(),) * 2,
        scratch_shapes=[
            pltpu.VMEM((1, all_rows), F32),
            pltpu.VMEM((all_rows + rank.shape[1], width), BF16),
        ],
        compiler_params=params(14),
        cost_estimate=cost(2**31),
        name="join_step",
    )(place, meta, total, valid, rank, stud, plan)


def grad_kernel(proto_total, place, meta, total_ref, valid_ref, rows_ref, expo_ref, col_ref, *refs):
    studs, grads, (weight_ref, acc_ref) = refs[:4], refs[4:8], refs[8:]
    weight_ref[...] = weights_of(total_ref, valid_ref)
    acc_ref[...] = jnp.zeros_like(acc_ref)
    chunk = 512

    @pl.loop(0, meta[TILES])
    def _(tile):
        start = pl.multiple_of(tile * TILE, TILE)
        scaled = scaled_rows(rows_ref[pl.ds(start, TILE), :], weight_ref[:, pl.ds(start, TILE)]).astype(BF16)
        for k in range(0, acc_ref.shape[0], chunk):
            acc_ref[k : k + chunk] += jnp.dot(
                expo_ref[tile, k : k + chunk], scaled, preferred_element_type=F32
            )

    rows = grads[0].shape[0]
    for piece in range(len(grads)):
        start = pl.multiple_of((place[2] ^ piece) * rows, rows)
        scale = 1.0 / (proto_total * col_ref[:, pl.ds(start, rows)])
        plan = scaled_rows(acc_ref[pl.ds(start, rows), :], scale)
        grads[piece][...] = (studs[piece][...].astype(F32) - plan).astype(BF16)


def grad_step(place, meta, total, valid, rows, expo, col, studs, proto_total):
    tiles, count, _ = expo.shape
    width = rows.shape[1]
    return pl.pallas_call(
        functools.partial(grad_kernel, proto_total),
        out_shape=(jax.ShapeDtypeStruct((count // 4, width), BF16),) * 4,
        in_specs=[smem()] * 2 + [vmem()] * 9,
        out_specs=(vmem(),) * 4,
        scratch_shapes=[pltpu.VMEM((1, tiles * TILE), F32), pltpu.VMEM((count, width), F32)],
        compiler_params=params(18),
        cost_estimate=cost(count * tiles * TILE * width * 2),
        name="grad_step",
    )(place, meta, total, valid, rows, pinned(expo), col, *studs)


def swap(value, axis):
    return lax.ppermute(value, axis, [(0, 1), (1, 0)])


def from_xor(value, axis, mask):
    return lax.ppermute(value, axis, [(i, i ^ mask) for i in range(4)])


def exchange(many, axes):
    return lax.all_to_all(many, axes, 0, 0, tiled=True)


def spread(value, axes, size):
    return exchange(jnp.broadcast_to(value[None], (size,) + value.shape), axes)


def tie(*values):
    return lax.optimization_barrier(values)


def pair_of(half, low):
    return jnp.stack(choose(low, half, swap(half, "xl")))


def gather_along(pair):
    return [pair] + [from_xor(pair, "y", mask) for mask in (1, 3, 2)]


def ordered(pieces):
    own, one, three, two = pieces
    return [own, one, two, three]


def scatter_protos(pieces):
    return [pieces[0]] + [from_xor(pieces[mask], "z", mask) for mask in (1, 3, 2)]


def choose(first, one, two):
    return jnp.where(first, one, two), jnp.where(first, two, one)


RINGS = {"x": (("xl", "xh"), (1, 2, 3)), "y": ("y", (2, 1, 3)), "z": ("z", (2, 1, 3))}


def ring(value, name):
    axes, masks = RINGS[name]
    return [lax.ppermute(value, axes, [(i, i ^ mask) for i in range(4)]) for mask in masks]


def total_of(value, got):
    return value + got[0] + got[1] + got[2]


def merged(one, two):
    high = jnp.maximum(one[0], two[0])
    return high, one[1] * jnp.exp((one[0] - high) / student_temp) + two[1] * jnp.exp(
        (two[0] - high) / student_temp
    )


def local(student, teacher, prototypes, masked):
    rows, width = student.shape
    y, xl, z = lax.axis_index("y"), lax.axis_index("xl"), lax.axis_index("z")
    core = lax.axis_index("c")
    block_id = y * 2 + xl
    count = prototypes.shape[0] // BLOCKS
    proto_total = prototypes.shape[0] * 4
    place = jnp.stack([y, core, z, block_id]).astype(jnp.int32)
    low_x, low_c = xl == 0, core == 0
    table = streamed(prototypes)

    teach, stud = compact(masked.astype(F32)[None], streamed(teacher), streamed(student))
    t_half, _ = choose(low_c, teach[:, :LANES], teach[:, LANES:])
    s_half, _ = choose(low_c, stud[:, :LANES], stud[:, LANES:])
    t_half, s_half, teach, stud = tie(t_half, s_half, teach, stud)
    t_beside, s_beside = swap(t_half, "xl"), swap(s_half, "xl")
    top = row_max(teach, table, rows, 0, 1)
    t_beside, s_beside, top, stud = tie(t_beside, s_beside, top, stud)
    t_pair = jnp.stack(choose(low_x, t_half, t_beside))
    s_pair = jnp.stack(choose(low_x, s_half, s_beside))
    top = jnp.maximum(top, swap(top, "c"))

    t_pair, s_pair, top, stud = tie(t_pair, s_pair, top, stud)
    mine = gather_along(t_pair)
    far = swap(top, "xh")
    soft = row_soft(stud, table, rows, 0, 2)
    mine, far, soft, top, stud, s_pair = tie(mine, far, soft, top, stud, s_pair)

    top = jnp.maximum(top, far)
    other = [swap(piece, "c") for piece in mine]
    beside = swap(top, "xl")
    mine, other, top, beside, soft, stud, s_pair = tie(mine, other, top, beside, soft, stud, s_pair)

    tops = gather_along(jnp.stack(choose(low_x, top, beside)))
    soft_two = row_soft(stud, table, rows, 1, 2)
    mine, other, tops, soft, soft_two, s_pair, place = tie(mine, other, tops, soft, soft_two, s_pair, place)

    s_mine = gather_along(s_pair)
    soft = jnp.stack(merged(soft, soft_two))
    soft = jnp.stack(merged(soft, swap(soft, "c")))
    soft_far = swap(soft, "xh")
    expo, col, valid, meta = expo_step(place, ordered(mine) + ordered(other), ordered(tops), prototypes)
    s_mine, col, soft, soft_far = tie(s_mine, col, soft, soft_far)

    got = ring(col, "z")
    soft = merged(soft, soft_far)
    got, s_mine, col, soft = tie(got, s_mine, col, soft)
    col = total_of(col, got)
    mask_total = col[0, count]
    row = row_step(place, meta, col, expo, proto_total, soft[0] / student_temp + jnp.log(soft[1]))
    row = row + swap(row, "c")
    row, s_mine = tie(row, s_mine)
    got = ring(row, "x")
    s_other = [swap(piece, "c") for piece in s_mine]
    row, got, s_mine, s_other = tie(row, got, s_mine, s_other)
    row = total_of(row, got)
    got = ring(row, "y")
    loaded = load_step(place, meta, ordered(s_mine) + ordered(s_other), prototypes)
    row, got, loaded = tie(row, got, loaded)
    stud_rows, rank, protos, turned = loaded
    row = total_of(row, got)
    col = col_step(meta, row, valid, expo)

    col, stud_rows, line = tie(col, stud_rows, row)
    got = ring(col, "z")
    one = student_step(0, place, meta, stud_rows, line, protos, turned)
    col, got, one = tie(col, got, one)
    row = row_step(place, meta, total_of(col, got), expo, proto_total)
    row = row + swap(row, "c")
    row, one = tie(row, one)
    got = ring(row, "x")
    two = student_step(1, place, meta, stud_rows, line, protos, turned, one[2])
    row, got, two = tie(row, got, two)
    row = total_of(row, got)
    got = ring(row, "y")
    row, got = tie(row, got)
    col = col_step(meta, total_of(row, got), valid, expo)

    got = ring(col, "z")
    col, got = tie(col, got)
    col = total_of(col, got)
    row = row_step(place, meta, col, expo, proto_total)
    row = row + swap(row, "c")
    row, turned = tie(row, turned)
    got = ring(row, "x")
    plan_sums = feature_step(meta, col, expo, turned, proto_total)
    row, got, plan_sums = tie(row, got, plan_sums)
    row = total_of(row, got)
    got = ring(row, "y")
    row, got = tie(row, got)
    row = total_of(row, got)

    keep, give = join_step(place, meta, row, valid, rank, two[2], plan_sums)
    keep, give, row = tie(keep, give, row)
    got = swap(give, "c")
    grads = grad_step(
        place, meta, row, valid, stud_rows, expo, col, tuple(one[:2]) + tuple(two[:2]), proto_total
    )
    keep, got, grads = tie(keep, got, grads)
    keep = (keep.astype(F32) + got.astype(F32)).astype(BF16)
    parts = exchange(keep, ("y", "xl", "xh"))
    pieces = scatter_protos(grads)
    parts, pieces = tie(parts, pieces)
    feature_grad = (
        jnp.sum(parts.astype(F32), axis=0) * (math.sqrt(proto_total) / student_temp)
    ).astype(BF16)
    proto_grad = (
        sum(piece.astype(F32) for piece in pieces) * (proto_total / jnp.sqrt(mask_total))
    ).astype(BF16)
    return feature_grad, proto_grad


def solution(mesh):
    fine = Mesh(mesh.devices.reshape(4, 2, 4, 2, 2), ("y", "xl", "z", "xh", "c"))
    rows, protos = ("y", "xl", "z"), ("xh", "c")
    in_specs = (P(rows, None), P(rows, None), P(protos, None), P(rows))
    out_specs = (P(rows + protos, None), P(protos + rows, None))
    return jax.shard_map(local, mesh=fine, in_specs=in_specs, out_specs=out_specs, check_vma=False)
```

```python
import functools
import math

import jax
import jax.numpy as jnp
from jax import lax
from jax.experimental import pallas as pl
from jax.experimental.pallas import tpu as pltpu
from jax.sharding import Mesh
from jax.sharding import PartitionSpec as P

ITERS = 3
student_temp = 0.1
teacher_temp = 0.05

F32 = jnp.float32
BF16 = jnp.bfloat16
TILE = 512
LANES = 128
ALIGN = 16
FAR = 1e30
INFO = 16
SPAN = 3
BLOCKS = 8
END, TILES = 2 * BLOCKS, 2 * BLOCKS + 1
MIB = 2**20

LOG2E = math.log2(math.e)


def params(mib):
    return pltpu.CompilerParams(vmem_limit_bytes=mib * MIB)


def vmem():
    return pl.BlockSpec(memory_space=pltpu.VMEM)


def smem():
    return pl.BlockSpec(memory_space=pltpu.SMEM)


def hbm():
    return pl.BlockSpec(memory_space=pltpu.HBM)


def pinned(value):
    return pltpu.with_memory_space_constraint(value, pltpu.VMEM)


def streamed(value):
    return pltpu.with_memory_space_constraint(value, pltpu.HBM)


def own_protos(place, proto_ref, own_ref, sem):
    count = own_ref.shape[0]
    start = pl.multiple_of(place[3] * count, count)
    return pltpu.make_async_copy(proto_ref.at[pl.ds(start, count)], own_ref, sem)


def turn(own_ref):
    chunk = 512
    return jnp.concatenate(
        [jnp.transpose(own_ref[k : k + chunk]) for k in range(0, own_ref.shape[0], chunk)], axis=1
    )


def split(value):
    high = value.astype(BF16)
    low = (value - high.astype(F32)).astype(BF16)
    return high, low


def as_row(block):
    pieces = []
    for start in range(0, block.shape[0], LANES):
        part = block[start : start + LANES]
        total = part[:, :LANES]
        for lane in range(LANES, block.shape[1], LANES):
            total = total + part[:, lane : lane + LANES]
        pieces.append(jnp.sum(jnp.transpose(total), axis=0, keepdims=True))
    return jnp.concatenate(pieces, axis=1)


def compact_kernel(mask_ref, teach_ref, stud_ref, teach_out, stud_out):
    rows, width = teach_ref.shape
    mask = mask_ref[...].reshape(1, rows).astype(F32)
    down = lax.broadcasted_iota(jnp.int32, (rows, rows), 0)
    along = lax.broadcasted_iota(jnp.int32, (rows, rows), 1)
    upper = jnp.where(down <= along, 1.0, 0.0).astype(BF16)
    many = jnp.broadcast_to(mask, (16, rows)).astype(BF16)
    rank = jnp.dot(many, upper, preferred_element_type=F32)[:1]
    place = jnp.where(mask > 0, rank - 1.0, -1.0)
    onehot = jnp.where(down.astype(F32) == place, 1.0, 0.0).astype(BF16)
    teach_out[:rows] = jnp.dot(onehot, teach_ref[...], preferred_element_type=F32).astype(BF16)
    stud_out[:rows] = jnp.dot(onehot, stud_ref[...], preferred_element_type=F32).astype(BF16)
    which = lax.broadcasted_iota(jnp.int32, (INFO, width), 0)
    info = jnp.zeros((INFO, width), F32)
    for piece in range(rows // width):
        info = jnp.where(which == piece, mask[:, piece * width : (piece + 1) * width], info)
    teach_out[rows:] = info.astype(BF16)
    stud_out[rows:] = info.astype(BF16)


def compact(masked, teacher, student):
    rows, width = teacher.shape
    return pl.pallas_call(
        compact_kernel,
        out_shape=(jax.ShapeDtypeStruct((rows + INFO, width), BF16),) * 2,
        in_specs=[vmem()] * 3,
        out_specs=(vmem(), vmem()),
        compiler_params=params(12),
        name="compact",
    )(masked, teacher, student)


def max_kernel(teach_ref, proto_ref, out_ref, turned_ref):
    rows = out_ref.shape[1]
    chunk = 512

    @pl.when(pl.program_id(0) == 0)
    def _():
        out_ref[...] = jnp.full_like(out_ref, -FAR)
        turned_ref[...] = jnp.transpose(teach_ref[:rows])

    best = out_ref[...]
    for start in range(0, proto_ref.shape[0], chunk):
        logit = jnp.dot(proto_ref[start : start + chunk], turned_ref[...], preferred_element_type=F32)
        best = jnp.maximum(best, jnp.max(logit, axis=0, keepdims=True))
    out_ref[...] = best


def row_max(feats, protos, rows, part, parts):
    count, width = protos.shape
    block = 2048
    steps = count // block // parts
    return pl.pallas_call(
        max_kernel,
        grid=(steps,),
        out_shape=jax.ShapeDtypeStruct((1, rows), F32),
        in_specs=[
            pl.BlockSpec(feats.shape, lambda i: (0, 0)),
            pl.BlockSpec((block, width), lambda i: (i + part * steps, 0)),
        ],
        out_specs=pl.BlockSpec((1, rows), lambda i: (0, 0)),
        scratch_shapes=[pltpu.VMEM((width, rows), BF16)],
        compiler_params=params(14),
        cost_estimate=cost(2 * count * width * rows // parts),
        name="row_max",
    )(feats, protos)


def soft_kernel(feat_ref, proto_ref, top_ref, sum_ref, turned_ref):
    chunk = 512

    @pl.when(pl.program_id(0) == 0)
    def _():
        top_ref[...] = jnp.full_like(top_ref, -FAR)
        sum_ref[...] = jnp.zeros_like(sum_ref)
        turned_ref[...] = jnp.transpose(feat_ref[: turned_ref.shape[1]])

    top = top_ref[...]
    total = sum_ref[...]
    for start in range(0, proto_ref.shape[0], chunk):
        logit = jnp.dot(proto_ref[start : start + chunk], turned_ref[...], preferred_element_type=F32)
        higher = jnp.maximum(top, jnp.max(logit, axis=0, keepdims=True))
        total = total * jnp.exp((top - higher) * (1 / student_temp)) + jnp.sum(
            jnp.exp2((logit - higher) * (LOG2E / student_temp)), axis=0, keepdims=True
        )
        top = higher
    top_ref[...] = top
    sum_ref[...] = total


def row_soft(feats, protos, rows, part, parts):
    count, width = protos.shape
    block = 2048
    steps = count // block // parts
    row = pl.BlockSpec((1, rows), lambda i: (0, 0))
    return pl.pallas_call(
        soft_kernel,
        grid=(steps,),
        out_shape=(jax.ShapeDtypeStruct((1, rows), F32),) * 2,
        in_specs=[
            pl.BlockSpec(feats.shape, lambda i: (0, 0)),
            pl.BlockSpec((block, width), lambda i: (i + part * steps, 0)),
        ],
        out_specs=(row, row),
        scratch_shapes=[pltpu.VMEM((width, rows), BF16)],
        compiler_params=params(14),
        cost_estimate=cost(3 * count * width * rows // parts),
        name="row_soft",
    )(feats, protos)


def cost(flops):
    return pl.CostEstimate(flops=flops, bytes_accessed=2**20, transcendentals=0)


def joined(place, refs, block, rows):
    piece, side = block // 2, block % 2
    mine = refs[piece][side, :rows]
    other = refs[4 + piece][side, :rows]
    first = place[1] == 0
    return jnp.where(first, mine, other), jnp.where(first, other, mine)


def true_block(place, block):
    return (place[0] ^ (block // 2)) * 2 + block % 2


def load_rows(place, meta, refs, rows_ref, rows):
    for true in range(BLOCKS):

        def fill(block, true=true):
            @pl.when(place[0] == (true // 2) ^ (block // 2))
            def _():
                offset = pl.multiple_of(meta[true], ALIGN)
                low, high = joined(place, refs, block, rows)
                rows_ref[pl.ds(offset, rows), :LANES] = low
                rows_ref[pl.ds(offset, rows), LANES:] = high

        for piece in range(4):
            fill(piece * 2 + true % 2)
    tail = pl.multiple_of(meta[END], ALIGN)
    rows_ref[pl.ds(tail, TILE), :] = jnp.zeros((TILE, rows_ref.shape[1]), BF16)


def load_line(meta, lines, out_ref, fill):
    rows = lines[0].shape[1]
    out_ref[...] = jnp.full_like(out_ref, fill)
    lane = lax.broadcasted_iota(jnp.int32, (1, rows + LANES), 1)
    for block in range(BLOCKS):
        offset = meta[block]
        shift = lax.rem(offset, LANES)
        base = pl.multiple_of(offset - shift, LANES)
        wide = jnp.concatenate([lines[block], jnp.zeros((1, LANES), F32)], axis=1)
        wide = pltpu.roll(jnp.broadcast_to(wide, (8, rows + LANES)), shift, axis=1)[:1]
        there = (lane >= shift) & (lane < shift + meta[BLOCKS + block])
        out_ref[:, pl.ds(base, rows + LANES)] = jnp.where(
            there, wide, out_ref[:, pl.ds(base, rows + LANES)]
        )


def place_blocks(place, meta, refs, rows):
    for block in range(BLOCKS):
        piece, side = block // 2, block % 2
        info = refs[piece][side, rows:].astype(F32) + refs[4 + piece][side, rows:].astype(F32)
        meta[BLOCKS + true_block(place, block)] = jnp.sum(info).astype(jnp.int32)
    end = jnp.int32(0)
    for block in range(BLOCKS):
        meta[block] = end
        end = end + (meta[BLOCKS + block] + (ALIGN - 1)) // ALIGN * ALIGN
    meta[END] = end
    meta[TILES] = (end + (TILE - 1)) // TILE


def expo_kernel(place, *refs):
    pieces, tops, proto_ref, refs = refs[:8], refs[8:12], refs[12], refs[13:]
    expo_ref, col_ref, valid_ref, meta, rows_ref, line_ref, acc_ref, own_ref, sem = refs
    rows = tops[0].shape[2]
    protos = own_protos(place, proto_ref, own_ref, sem)
    protos.start()
    place_blocks(place, meta, pieces, rows)
    load_rows(place, meta, pieces, rows_ref, rows)
    lines = []
    for block in range(BLOCKS):
        line = tops[0][block % 2]
        for piece in range(1, 4):
            line = jnp.where((place[0] ^ piece) == block // 2, tops[piece][block % 2], line)
        lines.append(line)
    load_line(meta, lines, line_ref, FAR)
    valid_ref[...] = jnp.where(line_ref[:, : valid_ref.shape[1]] < 0.5 * FAR, 1.0, 0.0)
    acc_ref[...] = jnp.zeros_like(acc_ref)
    protos.wait()
    chunk = 512
    count = own_ref.shape[0]

    @pl.loop(0, meta[TILES])
    def _(tile):
        start = pl.multiple_of(tile * TILE, TILE)
        feats = jnp.transpose(rows_ref[pl.ds(start, TILE), :])
        top = line_ref[:, pl.ds(start, TILE)]
        for k in range(0, count, chunk):
            logit = jnp.dot(own_ref[k : k + chunk], feats, preferred_element_type=F32)
            expo = jnp.exp2((logit - top) * (LOG2E / teacher_temp))
            expo_ref[tile, k : k + chunk] = expo.astype(BF16)
            acc_ref[k : k + chunk] += fold(expo)

    col_ref[:, :count] = as_row(acc_ref[...])
    col_ref[:, count:] = jnp.zeros((1, LANES), F32) + jnp.sum(valid_ref[...])


def fold(block):
    total = block[:, :LANES]
    for lane in range(LANES, block.shape[1], LANES):
        total = total + block[:, lane : lane + LANES]
    return total


def expo_step(place, pieces, tops, protos):
    rows = tops[0].shape[2]
    width = protos.shape[1]
    count = protos.shape[0] // BLOCKS
    total = BLOCKS * rows
    return pl.pallas_call(
        expo_kernel,
        out_shape=(
            pltpu.VMEM((total // TILE, count, TILE), BF16),
            jax.ShapeDtypeStruct((1, count + LANES), F32),
            jax.ShapeDtypeStruct((1, total), F32),
            jax.ShapeDtypeStruct((24,), jnp.int32),
        ),
        in_specs=[smem()] + [vmem()] * 12 + [hbm()],
        out_specs=(vmem(), vmem(), vmem(), smem()),
        scratch_shapes=[
            pltpu.VMEM((total + TILE, width), BF16),
            pltpu.VMEM((1, total + LANES), F32),
            pltpu.VMEM((count, LANES), F32),
            pltpu.VMEM((count, width), BF16),
            pltpu.SemaphoreType.DMA,
        ],
        compiler_params=params(26),
        cost_estimate=cost(count * total * width * 2),
        name="expo",
    )(place, *pieces, *tops, streamed(protos))


def col_scale_of(total_ref, count, proto_total):
    return 1.0 / (proto_total * total_ref[:, :count])


def two_rows(value):
    high, low = split(value)
    which = lax.broadcasted_iota(jnp.int32, (16, value.shape[1]), 0)
    return jnp.where(which == 0, high.astype(F32), jnp.where(which == 1, low.astype(F32), 0.0)).astype(BF16)


def row_kernel(proto_total, with_lse, place, meta, total_ref, expo_ref, *refs):
    out_ref = refs[-1]
    lhs = two_rows(col_scale_of(total_ref, expo_ref.shape[1], proto_total))
    out_ref[...] = jnp.zeros_like(out_ref)
    if with_lse:
        lse_ref = refs[0]
        rows = lse_ref.shape[1]
        start = pl.multiple_of(rows * BLOCKS + place[3] * rows, rows)
        out_ref[:, pl.ds(start, rows)] = lse_ref[...] * 0.25

    @pl.loop(0, meta[TILES])
    def _(tile):
        start = pl.multiple_of(tile * TILE, TILE)
        both = jnp.dot(lhs, expo_ref[tile], preferred_element_type=F32)
        out_ref[:, pl.ds(start, TILE)] = both[:1] + both[1:2]


def row_step(place, meta, total, expo, proto_total, lse=None):
    tiles, count, _ = expo.shape
    more = () if lse is None else (lse,)
    return pl.pallas_call(
        functools.partial(row_kernel, proto_total, lse is not None),
        out_shape=jax.ShapeDtypeStruct((1, (1 + len(more)) * tiles * TILE), F32),
        in_specs=[smem()] * 2 + [vmem()] * (2 + len(more)),
        out_specs=vmem(),
        compiler_params=params(10),
        cost_estimate=cost(count * tiles * TILE * 400),
        name="row_step",
    )(place, meta, total, pinned(expo), *more)


def weights_of(total_ref, valid_ref):
    valid = valid_ref[...]
    return valid / jnp.where(valid > 0, total_ref[:, : valid.shape[1]], 1.0)


def col_kernel(meta, total_ref, valid_ref, expo_ref, out_ref, line_ref, acc_ref):
    line_ref[...] = weights_of(total_ref, valid_ref)
    acc_ref[...] = jnp.zeros_like(acc_ref)
    chunk = 64

    @pl.loop(0, meta[TILES])
    def _(tile):
        start = pl.multiple_of(tile * TILE, TILE)
        weight = line_ref[:, pl.ds(start, TILE)]
        for k in range(0, acc_ref.shape[0], chunk):
            acc_ref[k : k + chunk] += fold(expo_ref[tile, k : k + chunk].astype(F32) * weight)

    out_ref[...] = as_row(acc_ref[...])


def col_step(meta, total, valid, expo):
    tiles, count, _ = expo.shape
    return pl.pallas_call(
        col_kernel,
        out_shape=jax.ShapeDtypeStruct((1, count), F32),
        in_specs=[smem()] + [vmem()] * 3,
        out_specs=vmem(),
        scratch_shapes=[pltpu.VMEM((1, tiles * TILE), F32), pltpu.VMEM((count, LANES), F32)],
        compiler_params=params(10),
        cost_estimate=cost(count * tiles * TILE * 400),
        name="col_step",
    )(meta, total, valid, pinned(expo))


def load_kernel(place, meta, *refs):
    pieces, proto_ref, refs = refs[:8], refs[8], refs[9:]
    out_ref, rank_ref, own_out, turned_ref, rows_ref, own_ref, sem = refs
    protos = own_protos(place, proto_ref, own_ref, sem)
    protos.start()
    rows = pieces[0].shape[1] - INFO
    load_rows(place, meta, pieces, rows_ref, rows)
    out_ref[...] = rows_ref[...]
    masks = [jnp.zeros((1, rows), F32)] * BLOCKS
    for block in range(BLOCKS):
        low, high = joined(place, pieces, block, rows + INFO)
        low, high = low[rows:].astype(F32), high[rows:].astype(F32)
        line = []
        for index in range(rows // (2 * LANES)):
            line += [low[index : index + 1], high[index : index + 1]]
        line = jnp.concatenate(line, axis=1)
        for true in range(block % 2, BLOCKS, 2):
            masks[true] = jnp.where(true_block(place, block) == true, line, masks[true])
    masks = jnp.concatenate(masks, axis=0)
    down = lax.broadcasted_iota(jnp.int32, (rows, rows), 0)
    along = lax.broadcasted_iota(jnp.int32, (rows, rows), 1)
    upper = jnp.where(down <= along, 1.0, 0.0).astype(BF16)
    many = jnp.concatenate([masks, masks], axis=0).astype(BF16)
    rank = jnp.dot(many, upper, preferred_element_type=F32)[:BLOCKS]
    rank_ref[...] = jnp.where(masks > 0, rank - 1.0, -1.0)
    protos.wait()
    own_out[...] = own_ref[...]
    turned_ref[...] = turn(own_ref)


def load_step(place, meta, pieces, protos):
    rows = pieces[0].shape[1] - INFO
    width = protos.shape[1]
    count = protos.shape[0] // BLOCKS
    total = BLOCKS * rows
    return pl.pallas_call(
        load_kernel,
        out_shape=(
            jax.ShapeDtypeStruct((total + TILE, width), BF16),
            jax.ShapeDtypeStruct((BLOCKS, rows), F32),
            jax.ShapeDtypeStruct((count, width), BF16),
            jax.ShapeDtypeStruct((width, count), BF16),
        ),
        in_specs=[smem()] * 2 + [vmem()] * 8 + [hbm()],
        out_specs=(vmem(),) * 4,
        scratch_shapes=[
            pltpu.VMEM((total + TILE, width), BF16),
            pltpu.VMEM((count, width), BF16),
            pltpu.SemaphoreType.DMA,
        ],
        compiler_params=params(18),
        cost_estimate=cost(2**31),
        name="load_student",
    )(place, meta, *pieces, streamed(protos))


def student_kernel(part, place, meta, rows_ref, all_ref, own_ref, turned_ref, *refs):
    if part == 1:
        sums_in, refs = refs[0], refs[1:]
    grads, (sums_out, acc_ref, line_ref) = refs[:2], refs[2:]
    total = sums_out.shape[0]
    rows = total // BLOCKS
    load_line(
        meta, [all_ref[:, total + block * rows : total + (block + 1) * rows] for block in range(BLOCKS)], line_ref, FAR
    )
    acc_ref[...] = jnp.zeros_like(acc_ref)
    sums_out[...] = jnp.zeros_like(sums_out)
    chunk = grads[0].shape[0]

    @pl.loop(0, meta[TILES])
    def _(tile):
        start = pl.multiple_of(tile * TILE, TILE)
        feats = rows_ref[pl.ds(start, TILE), :]
        across = jnp.transpose(feats)
        lse = line_ref[:, pl.ds(start, TILE)]
        turned = jnp.zeros((turned_ref.shape[0], TILE), F32)
        for piece in range(2):
            k = pl.multiple_of((place[2] ^ (2 * part + piece)) * chunk, chunk)
            logit = jnp.dot(own_ref[pl.ds(k, chunk), :], across, preferred_element_type=F32)
            probs = jnp.exp2((logit - lse) * (LOG2E / student_temp)).astype(BF16)
            acc_ref[piece] += jnp.dot(probs, feats, preferred_element_type=F32)
            turned += jnp.dot(turned_ref[:, pl.ds(k, chunk)], probs, preferred_element_type=F32)
        sums = jnp.transpose(turned)
        if part == 1:
            sums = sums + sums_in[pl.ds(start, TILE), :].astype(F32)
        sums_out[pl.ds(start, TILE), :] = sums.astype(BF16)

    for piece in range(2):
        grads[piece][...] = acc_ref[piece].astype(BF16)


def student_step(part, place, meta, rows, line, own, turned, *sums):
    width, count = turned.shape
    total = line.shape[1] // 2
    outs = (jax.ShapeDtypeStruct((count // 4, width), BF16),) * 2 + (jax.ShapeDtypeStruct((total, width), BF16),)
    return pl.pallas_call(
        functools.partial(student_kernel, part),
        out_shape=outs,
        in_specs=[smem()] * 2 + [vmem()] * (4 + len(sums)),
        out_specs=(vmem(),) * len(outs),
        scratch_shapes=[pltpu.VMEM((2, count // 4, width), F32), pltpu.VMEM((1, total + LANES), F32)],
        compiler_params=params(20),
        cost_estimate=cost(count * total * width * 3),
        name="student",
    )(place, meta, rows, line, own, turned, *sums)


def scaled_rows(feats, factor):
    parts = []
    for start in range(0, feats.shape[0], LANES):
        column = jnp.transpose(jnp.broadcast_to(factor[:, start : start + LANES], (LANES, LANES)))
        part = feats[start : start + LANES].astype(F32)
        parts.append(
            jnp.concatenate([part[:, d : d + LANES] * column for d in range(0, part.shape[1], LANES)], axis=1)
        )
    return jnp.concatenate(parts, axis=0)


def feature_kernel(proto_total, first, meta, total_ref, expo_ref, turned_ref, *refs):
    sums_ref = refs[-1]
    scale = col_scale_of(total_ref, expo_ref.shape[1], proto_total)
    scaled = (turned_ref[...].astype(F32) * scale).astype(BF16)
    if first == 0:
        sums_ref[...] = jnp.zeros_like(sums_ref)
        span = (0, jnp.minimum(meta[TILES], SPAN))
    else:
        span = (SPAN, meta[TILES])

    @pl.loop(*span)
    def _(tile):
        start = pl.multiple_of(tile * TILE, TILE)
        turned = jnp.dot(scaled, expo_ref[tile], preferred_element_type=F32)
        sums_ref[pl.ds(start, TILE), :] = jnp.transpose(turned).astype(BF16)


def feature_step(first, meta, total, expo, turned, proto_total, *sums):
    tiles, count, _ = expo.shape
    width = turned.shape[0]
    return pl.pallas_call(
        functools.partial(feature_kernel, proto_total, first),
        out_shape=pltpu.VMEM((tiles * TILE, width), BF16),
        in_specs=[smem()] + [vmem()] * (3 + len(sums)),
        out_specs=vmem(),
        input_output_aliases={4: 0} if sums else {},
        compiler_params=params(14),
        cost_estimate=cost(count * tiles * TILE * width),
        name="feature_step",
    )(meta, total, pinned(expo), turned, *[pinned(value) for value in sums])


def join_kernel(place, meta, total_ref, valid_ref, rank_ref, stud_ref, plan_ref, keep_ref, give_ref, weight_ref, sums_ref):
    weight_ref[...] = weights_of(total_ref, valid_ref)

    @pl.loop(0, meta[TILES])
    def _(tile):
        start = pl.multiple_of(tile * TILE, TILE)
        plan = scaled_rows(plan_ref[pl.ds(start, TILE), :], weight_ref[:, pl.ds(start, TILE)])
        sums_ref[pl.ds(start, TILE), :] = (stud_ref[pl.ds(start, TILE), :].astype(F32) - plan).astype(BF16)

    tail = pl.multiple_of(meta[TILES] * TILE, TILE)
    rows = rank_ref.shape[1]
    sums_ref[pl.ds(tail, rows), :] = jnp.zeros((rows, sums_ref.shape[1]), BF16)
    along = lax.broadcasted_iota(jnp.int32, (LANES, rows), 1).astype(F32)
    first = place[1] == 0
    for block in range(BLOCKS):
        offset = pl.multiple_of(meta[block], ALIGN)
        sums = sums_ref[pl.ds(offset, rows), :]
        pieces = []
        for start in range(0, rows, LANES):
            column = jnp.transpose(jnp.broadcast_to(rank_ref[block : block + 1, start : start + LANES], (LANES, LANES)))
            column = jnp.concatenate([column] * (rows // LANES), axis=1)
            onehot = jnp.where(column == along, 1.0, 0.0).astype(BF16)
            pieces.append(jnp.dot(onehot, sums, preferred_element_type=F32).astype(BF16))
        for half in range(2):
            low, high = pieces[2 * half], pieces[2 * half + 1]
            keep_ref[2 * block + half] = jnp.where(first, low, high)
            give_ref[2 * block + half] = jnp.where(first, high, low)


def join_step(place, meta, total, valid, rank, stud, plan):
    all_rows, width = stud.shape
    out = jax.ShapeDtypeStruct((2 * BLOCKS, LANES, width), BF16)
    return pl.pallas_call(
        join_kernel,
        out_shape=(out, out),
        in_specs=[smem()] * 2 + [vmem()] * 5,
        out_specs=(vmem(),) * 2,
        scratch_shapes=[
            pltpu.VMEM((1, all_rows), F32),
            pltpu.VMEM((all_rows + rank.shape[1], width), BF16),
        ],
        compiler_params=params(14),
        cost_estimate=cost(2**31),
        name="join_step",
    )(place, meta, total, valid, rank, stud, plan)


def grad_kernel(proto_total, place, meta, total_ref, valid_ref, rows_ref, expo_ref, col_ref, *refs):
    studs, grads, (weight_ref, acc_ref) = refs[:4], refs[4:8], refs[8:]
    weight_ref[...] = weights_of(total_ref, valid_ref)
    acc_ref[...] = jnp.zeros_like(acc_ref)
    chunk = 512

    @pl.loop(0, meta[TILES])
    def _(tile):
        start = pl.multiple_of(tile * TILE, TILE)
        scaled = scaled_rows(rows_ref[pl.ds(start, TILE), :], weight_ref[:, pl.ds(start, TILE)]).astype(BF16)
        for k in range(0, acc_ref.shape[0], chunk):
            acc_ref[k : k + chunk] += jnp.dot(
                expo_ref[tile, k : k + chunk], scaled, preferred_element_type=F32
            )

    rows = grads[0].shape[0]
    for piece in range(len(grads)):
        start = pl.multiple_of((place[2] ^ piece) * rows, rows)
        scale = 1.0 / (proto_total * col_ref[:, pl.ds(start, rows)])
        plan = scaled_rows(acc_ref[pl.ds(start, rows), :], scale)
        grads[piece][...] = (studs[piece][...].astype(F32) - plan).astype(BF16)


def grad_step(place, meta, total, valid, rows, expo, col, studs, proto_total):
    tiles, count, _ = expo.shape
    width = rows.shape[1]
    return pl.pallas_call(
        functools.partial(grad_kernel, proto_total),
        out_shape=(jax.ShapeDtypeStruct((count // 4, width), BF16),) * 4,
        in_specs=[smem()] * 2 + [vmem()] * 9,
        out_specs=(vmem(),) * 4,
        scratch_shapes=[pltpu.VMEM((1, tiles * TILE), F32), pltpu.VMEM((count, width), F32)],
        compiler_params=params(18),
        cost_estimate=cost(count * tiles * TILE * width * 2),
        name="grad_step",
    )(place, meta, total, valid, rows, pinned(expo), col, *studs)


def swap(value, axis):
    return lax.ppermute(value, axis, [(0, 1), (1, 0)])


def from_xor(value, axis, mask):
    return lax.ppermute(value, axis, [(i, i ^ mask) for i in range(4)])


def exchange(many, axes):
    return lax.all_to_all(many, axes, 0, 0, tiled=True)


def spread(value, axes, size):
    return exchange(jnp.broadcast_to(value[None], (size,) + value.shape), axes)


def tie(*values):
    return lax.optimization_barrier(values)


def pair_of(half, low):
    return jnp.stack(choose(low, half, swap(half, "xl")))


def double(value, mask):
    return jnp.stack([value, from_xor(value, "y", mask)])


def gather_along(pair):
    return [pair] + [from_xor(pair, "y", mask) for mask in (1, 3, 2)]


def ordered(pieces):
    own, one, three, two = pieces
    return [own, one, two, three]


def scatter_protos(pieces):
    return [pieces[0]] + [from_xor(pieces[mask], "z", mask) for mask in (1, 3, 2)]


def choose(first, one, two):
    return jnp.where(first, one, two), jnp.where(first, two, one)


RINGS = {"x": (("xl", "xh"), (1, 2, 3)), "y": ("y", (2, 1, 3)), "z": ("z", (2, 1, 3))}


def ring(value, name):
    axes, masks = RINGS[name]
    return [lax.ppermute(value, axes, [(i, i ^ mask) for i in range(4)]) for mask in masks]


def total_of(value, got):
    return value + got[0] + got[1] + got[2]


def merged(one, two):
    high = jnp.maximum(one[0], two[0])
    return high, one[1] * jnp.exp((one[0] - high) / student_temp) + two[1] * jnp.exp(
        (two[0] - high) / student_temp
    )


def local(student, teacher, prototypes, masked):
    rows, width = student.shape
    y, xl, z = lax.axis_index("y"), lax.axis_index("xl"), lax.axis_index("z")
    core = lax.axis_index("c")
    block_id = y * 2 + xl
    count = prototypes.shape[0] // BLOCKS
    proto_total = prototypes.shape[0] * 4
    place = jnp.stack([y, core, z, block_id]).astype(jnp.int32)
    low_x, low_c = xl == 0, core == 0
    table = streamed(prototypes)

    teach, stud = compact(masked, streamed(teacher), streamed(student))
    t_half, _ = choose(low_c, teach[:, :LANES], teach[:, LANES:])
    s_half, _ = choose(low_c, stud[:, :LANES], stud[:, LANES:])
    t_half, s_half, teach, stud = tie(t_half, s_half, teach, stud)
    t_beside, s_beside = swap(t_half, "xl"), swap(s_half, "xl")
    top = row_max(teach, table, rows, 0, 1)
    t_beside, s_beside, top, stud = tie(t_beside, s_beside, top, stud)
    t_pair = jnp.stack(choose(low_x, t_half, t_beside))
    s_pair = jnp.stack(choose(low_x, s_half, s_beside))
    top = jnp.maximum(top, swap(top, "c"))

    t_pair, s_pair, top, stud = tie(t_pair, s_pair, top, stud)
    mine = gather_along(t_pair)
    far = swap(top, "xh")
    soft = row_soft(stud, table, rows, 0, 2)
    mine, far, soft, top, stud, s_pair = tie(mine, far, soft, top, stud, s_pair)

    top = jnp.maximum(top, far)
    other = [swap(piece, "c") for piece in mine]
    beside = swap(top, "xl")
    mine, other, top, beside, soft, stud, s_pair = tie(mine, other, top, beside, soft, stud, s_pair)

    tops = gather_along(jnp.stack(choose(low_x, top, beside)))
    s_mine = double(s_pair, 1)
    soft_two = row_soft(stud, table, rows, 1, 2)
    mine, other, tops, soft, soft_two, s_mine, place = tie(mine, other, tops, soft, soft_two, s_mine, place)
    soft = jnp.stack(merged(soft, soft_two))
    soft = jnp.stack(merged(soft, swap(soft, "c")))
    soft, tops, s_mine = tie(soft, tops, s_mine)

    s_mine = [s_mine[0], s_mine[1], from_xor(s_mine, "y", 3)]
    soft_far = swap(soft, "xh")
    expo, col, valid, meta = expo_step(place, ordered(mine) + ordered(other), ordered(tops), prototypes)
    col, soft, soft_far = tie(col, soft, soft_far)

    got = ring(col, "z")
    soft = merged(soft, soft_far)
    got, s_mine, col, soft = tie(got, s_mine, col, soft)
    s_mine = [s_mine[0], s_mine[1], s_mine[2][0], s_mine[2][1]]
    col = total_of(col, got)
    mask_total = col[0, count]
    col, s_mine = tie(col, s_mine)
    s_other = [swap(piece, "c") for piece in s_mine]
    row = row_step(place, meta, col, expo, proto_total, soft[0] + student_temp * jnp.log(soft[1]))
    row, s_mine, s_other = tie(row, s_mine, s_other)
    row = row + swap(row, "c")
    got = ring(row, "x")
    row, got, s_mine, s_other = tie(row, got, s_mine, s_other)
    row = total_of(row, got)
    got = ring(row, "y")
    loaded = load_step(place, meta, ordered(s_mine) + ordered(s_other), prototypes)
    row, got, loaded = tie(row, got, loaded)
    stud_rows, rank, protos, turned = loaded
    row = total_of(row, got)
    col = col_step(meta, row, valid, expo)

    col, stud_rows, line = tie(col, stud_rows, row)
    got = ring(col, "z")
    one = student_step(0, place, meta, stud_rows, line, protos, turned)
    col, got, one = tie(col, got, one)
    row = row_step(place, meta, total_of(col, got), expo, proto_total)
    row = row + swap(row, "c")
    row, one = tie(row, one)
    got = ring(row, "x")
    two = student_step(1, place, meta, stud_rows, line, protos, turned, one[2])
    row, got, two = tie(row, got, two)
    row = total_of(row, got)
    got = ring(row, "y")
    row, got = tie(row, got)
    col = col_step(meta, total_of(row, got), valid, expo)

    got = ring(col, "z")
    col, got = tie(col, got)
    col = total_of(col, got)
    row = row_step(place, meta, col, expo, proto_total)
    row = row + swap(row, "c")
    row, turned = tie(row, turned)
    got = ring(row, "x")
    plan_sums = feature_step(0, meta, col, expo, turned, proto_total)
    row, got, plan_sums = tie(row, got, plan_sums)
    row = total_of(row, got)
    got = ring(row, "y")
    plan_sums = feature_step(1, meta, col, expo, turned, proto_total, plan_sums)
    row, got, plan_sums = tie(row, got, plan_sums)
    row = total_of(row, got)

    keep, give = join_step(place, meta, row, valid, rank, two[2], pinned(plan_sums))
    keep, give, row = tie(keep, give, row)
    got = swap(give, "c")
    grads = grad_step(
        place, meta, row, valid, stud_rows, expo, col, tuple(one[:2]) + tuple(two[:2]), proto_total
    )
    keep, got, grads = tie(keep, got, grads)
    pieces = scatter_protos(grads)
    keep = (keep.astype(F32) + got.astype(F32)).astype(BF16)
    parts = exchange(keep, ("y", "xl", "xh"))
    proto_grad = (
        sum(piece.astype(F32) for piece in pieces) * (proto_total / jnp.sqrt(mask_total))
    ).astype(BF16)
    parts, proto_grad = tie(parts, proto_grad)
    feature_grad = (
        jnp.sum(parts.astype(F32), axis=0) * (math.sqrt(proto_total) / student_temp)
    ).astype(BF16)
    return feature_grad, proto_grad


def solution(mesh):
    fine = Mesh(mesh.devices.reshape(4, 2, 4, 2, 2), ("y", "xl", "z", "xh", "c"))
    rows, protos = ("y", "xl", "z"), ("xh", "c")
    in_specs = (P(rows, None), P(rows, None), P(protos, None), P(rows))
    out_specs = (P(rows + protos, None), P(protos + rows, None))
    return jax.shard_map(local, mesh=fine, in_specs=in_specs, out_specs=out_specs, check_vma=False)
```

```python
import functools
import math

import jax
import jax.numpy as jnp
from jax import lax
from jax.experimental import pallas as pl
from jax.experimental.pallas import tpu as pltpu
from jax.sharding import Mesh
from jax.sharding import PartitionSpec as P

ITERS = 3
student_temp = 0.1
teacher_temp = 0.05

F32 = jnp.float32
BF16 = jnp.bfloat16
TILE = 512
LANES = 128
ALIGN = 16
FAR = 1e30
INFO = 16
SPAN = 3
BLOCKS = 8
END, TILES = 2 * BLOCKS, 2 * BLOCKS + 1
MIB = 2**20

LOG2E = math.log2(math.e)


def params(mib):
    return pltpu.CompilerParams(vmem_limit_bytes=mib * MIB)


def vmem():
    return pl.BlockSpec(memory_space=pltpu.VMEM)


def smem():
    return pl.BlockSpec(memory_space=pltpu.SMEM)


def hbm():
    return pl.BlockSpec(memory_space=pltpu.HBM)


def pinned(value):
    return pltpu.with_memory_space_constraint(value, pltpu.VMEM)


def streamed(value):
    return pltpu.with_memory_space_constraint(value, pltpu.HBM)


def own_protos(place, proto_ref, own_ref, sem):
    count = own_ref.shape[0]
    start = pl.multiple_of(place[3] * count, count)
    return pltpu.make_async_copy(proto_ref.at[pl.ds(start, count)], own_ref, sem)


def turn(own_ref):
    chunk = 512
    return jnp.concatenate(
        [jnp.transpose(own_ref[k : k + chunk]) for k in range(0, own_ref.shape[0], chunk)], axis=1
    )


def split(value):
    high = value.astype(BF16)
    low = (value - high.astype(F32)).astype(BF16)
    return high, low


def as_row(block):
    pieces = []
    for start in range(0, block.shape[0], LANES):
        part = block[start : start + LANES]
        total = part[:, :LANES]
        for lane in range(LANES, block.shape[1], LANES):
            total = total + part[:, lane : lane + LANES]
        pieces.append(jnp.sum(jnp.transpose(total), axis=0, keepdims=True))
    return jnp.concatenate(pieces, axis=1)


def compact_kernel(mask_ref, teach_ref, stud_ref, teach_out, stud_out):
    rows, width = teach_ref.shape
    mask = mask_ref[...].reshape(1, rows).astype(F32)
    down = lax.broadcasted_iota(jnp.int32, (rows, rows), 0)
    along = lax.broadcasted_iota(jnp.int32, (rows, rows), 1)
    upper = jnp.where(down <= along, 1.0, 0.0).astype(BF16)
    many = jnp.broadcast_to(mask, (16, rows)).astype(BF16)
    rank = jnp.dot(many, upper, preferred_element_type=F32)[:1]
    place = jnp.where(mask > 0, rank - 1.0, -1.0)
    onehot = jnp.where(down.astype(F32) == place, 1.0, 0.0).astype(BF16)
    teach_out[:rows] = jnp.dot(onehot, teach_ref[...], preferred_element_type=F32).astype(BF16)
    stud_out[:rows] = jnp.dot(onehot, stud_ref[...], preferred_element_type=F32).astype(BF16)
    which = lax.broadcasted_iota(jnp.int32, (INFO, width), 0)
    info = jnp.zeros((INFO, width), F32)
    for piece in range(rows // width):
        info = jnp.where(which == piece, mask[:, piece * width : (piece + 1) * width], info)
    teach_out[rows:] = info.astype(BF16)
    stud_out[rows:] = info.astype(BF16)


def compact(masked, teacher, student):
    rows, width = teacher.shape
    return pl.pallas_call(
        compact_kernel,
        out_shape=(jax.ShapeDtypeStruct((rows + INFO, width), BF16),) * 2,
        in_specs=[vmem()] * 3,
        out_specs=(vmem(), vmem()),
        compiler_params=params(12),
        name="compact",
    )(masked, teacher, student)


def max_kernel(teach_ref, proto_ref, out_ref, turned_ref):
    rows = out_ref.shape[1]
    chunk = 512

    @pl.when(pl.program_id(0) == 0)
    def _():
        out_ref[...] = jnp.full_like(out_ref, -FAR)
        turned_ref[...] = jnp.transpose(teach_ref[:rows])

    best = out_ref[...]
    for start in range(0, proto_ref.shape[0], chunk):
        logit = jnp.dot(proto_ref[start : start + chunk], turned_ref[...], preferred_element_type=F32)
        best = jnp.maximum(best, jnp.max(logit, axis=0, keepdims=True))
    out_ref[...] = best


def row_max(feats, protos, rows, part, parts):
    count, width = protos.shape
    block = 2048
    steps = count // block // parts
    return pl.pallas_call(
        max_kernel,
        grid=(steps,),
        out_shape=jax.ShapeDtypeStruct((1, rows), F32),
        in_specs=[
            pl.BlockSpec(feats.shape, lambda i: (0, 0)),
            pl.BlockSpec((block, width), lambda i: (i + part * steps, 0)),
        ],
        out_specs=pl.BlockSpec((1, rows), lambda i: (0, 0)),
        scratch_shapes=[pltpu.VMEM((width, rows), BF16)],
        compiler_params=params(14),
        cost_estimate=cost(2 * count * width * rows // parts),
        name="row_max",
    )(feats, protos)


def soft_kernel(feat_ref, proto_ref, top_ref, sum_ref, turned_ref):
    chunk = 512

    @pl.when(pl.program_id(0) == 0)
    def _():
        top_ref[...] = jnp.full_like(top_ref, -FAR)
        sum_ref[...] = jnp.zeros_like(sum_ref)
        turned_ref[...] = jnp.transpose(feat_ref[: turned_ref.shape[1]])

    top = top_ref[...]
    total = sum_ref[...]
    for start in range(0, proto_ref.shape[0], chunk):
        logit = jnp.dot(proto_ref[start : start + chunk], turned_ref[...], preferred_element_type=F32)
        higher = jnp.maximum(top, jnp.max(logit, axis=0, keepdims=True))
        total = total * jnp.exp((top - higher) * (1 / student_temp)) + jnp.sum(
            jnp.exp2((logit - higher) * (LOG2E / student_temp)), axis=0, keepdims=True
        )
        top = higher
    top_ref[...] = top
    sum_ref[...] = total


def row_soft(feats, protos, rows, part, parts):
    count, width = protos.shape
    block = 2048
    steps = count // block // parts
    row = pl.BlockSpec((1, rows), lambda i: (0, 0))
    return pl.pallas_call(
        soft_kernel,
        grid=(steps,),
        out_shape=(jax.ShapeDtypeStruct((1, rows), F32),) * 2,
        in_specs=[
            pl.BlockSpec(feats.shape, lambda i: (0, 0)),
            pl.BlockSpec((block, width), lambda i: (i + part * steps, 0)),
        ],
        out_specs=(row, row),
        scratch_shapes=[pltpu.VMEM((width, rows), BF16)],
        compiler_params=params(14),
        cost_estimate=cost(3 * count * width * rows // parts),
        name="row_soft",
    )(feats, protos)


def cost(flops):
    return pl.CostEstimate(flops=flops, bytes_accessed=2**20, transcendentals=0)


def joined(place, refs, block, rows):
    piece, side = block // 2, block % 2
    mine = refs[piece][side, :rows]
    other = refs[4 + piece][side, :rows]
    first = place[1] == 0
    return jnp.where(first, mine, other), jnp.where(first, other, mine)


def true_block(place, block):
    return (place[0] ^ (block // 2)) * 2 + block % 2


def load_rows(place, meta, refs, rows_ref, rows):
    for true in range(BLOCKS):

        def fill(block, true=true):
            @pl.when(place[0] == (true // 2) ^ (block // 2))
            def _():
                offset = pl.multiple_of(meta[true], ALIGN)
                low, high = joined(place, refs, block, rows)
                rows_ref[pl.ds(offset, rows), :LANES] = low
                rows_ref[pl.ds(offset, rows), LANES:] = high

        for piece in range(4):
            fill(piece * 2 + true % 2)
    tail = pl.multiple_of(meta[END], ALIGN)
    rows_ref[pl.ds(tail, TILE), :] = jnp.zeros((TILE, rows_ref.shape[1]), BF16)


def load_line(meta, lines, out_ref, fill):
    rows = lines[0].shape[1]
    out_ref[...] = jnp.full_like(out_ref, fill)
    lane = lax.broadcasted_iota(jnp.int32, (1, rows + LANES), 1)
    for block in range(BLOCKS):
        offset = meta[block]
        shift = lax.rem(offset, LANES)
        base = pl.multiple_of(offset - shift, LANES)
        wide = jnp.concatenate([lines[block], jnp.zeros((1, LANES), F32)], axis=1)
        wide = pltpu.roll(jnp.broadcast_to(wide, (8, rows + LANES)), shift, axis=1)[:1]
        there = (lane >= shift) & (lane < shift + meta[BLOCKS + block])
        out_ref[:, pl.ds(base, rows + LANES)] = jnp.where(
            there, wide, out_ref[:, pl.ds(base, rows + LANES)]
        )


def place_blocks(place, meta, refs, rows):
    for block in range(BLOCKS):
        piece, side = block // 2, block % 2
        info = refs[piece][side, rows:].astype(F32) + refs[4 + piece][side, rows:].astype(F32)
        meta[BLOCKS + true_block(place, block)] = jnp.sum(info).astype(jnp.int32)
    end = jnp.int32(0)
    for block in range(BLOCKS):
        meta[block] = end
        end = end + (meta[BLOCKS + block] + (ALIGN - 1)) // ALIGN * ALIGN
    meta[END] = end
    meta[TILES] = (end + (TILE - 1)) // TILE


def expo_kernel(place, *refs):
    pieces, tops, proto_ref, refs = refs[:8], refs[8:12], refs[12], refs[13:]
    expo_ref, col_ref, valid_ref, meta, rows_ref, line_ref, acc_ref, own_ref, sem = refs
    rows = tops[0].shape[2]
    protos = own_protos(place, proto_ref, own_ref, sem)
    protos.start()
    place_blocks(place, meta, pieces, rows)
    load_rows(place, meta, pieces, rows_ref, rows)
    lines = []
    for block in range(BLOCKS):
        line = tops[0][block % 2]
        for piece in range(1, 4):
            line = jnp.where((place[0] ^ piece) == block // 2, tops[piece][block % 2], line)
        lines.append(line)
    load_line(meta, lines, line_ref, FAR)
    valid_ref[...] = jnp.where(line_ref[:, : valid_ref.shape[1]] < 0.5 * FAR, 1.0, 0.0)
    acc_ref[...] = jnp.zeros_like(acc_ref)
    protos.wait()
    chunk = 512
    count = own_ref.shape[0]

    @pl.loop(0, meta[TILES])
    def _(tile):
        start = pl.multiple_of(tile * TILE, TILE)
        feats = jnp.transpose(rows_ref[pl.ds(start, TILE), :])
        top = line_ref[:, pl.ds(start, TILE)]
        for k in range(0, count, chunk):
            logit = jnp.dot(own_ref[k : k + chunk], feats, preferred_element_type=F32)
            expo = jnp.exp2((logit - top) * (LOG2E / teacher_temp))
            expo_ref[tile, k : k + chunk] = expo.astype(BF16)
            acc_ref[k : k + chunk] += fold(expo)

    col_ref[:, :count] = as_row(acc_ref[...])
    col_ref[:, count:] = jnp.zeros((1, LANES), F32) + jnp.sum(valid_ref[...])


def fold(block):
    total = block[:, :LANES]
    for lane in range(LANES, block.shape[1], LANES):
        total = total + block[:, lane : lane + LANES]
    return total


def expo_step(place, pieces, tops, protos):
    rows = tops[0].shape[2]
    width = protos.shape[1]
    count = protos.shape[0] // BLOCKS
    total = BLOCKS * rows
    return pl.pallas_call(
        expo_kernel,
        out_shape=(
            pltpu.VMEM((total // TILE, count, TILE), BF16),
            jax.ShapeDtypeStruct((1, count + LANES), F32),
            jax.ShapeDtypeStruct((1, total), F32),
            jax.ShapeDtypeStruct((24,), jnp.int32),
        ),
        in_specs=[smem()] + [vmem()] * 12 + [hbm()],
        out_specs=(vmem(), vmem(), vmem(), smem()),
        scratch_shapes=[
            pltpu.VMEM((total + TILE, width), BF16),
            pltpu.VMEM((1, total + LANES), F32),
            pltpu.VMEM((count, LANES), F32),
            pltpu.VMEM((count, width), BF16),
            pltpu.SemaphoreType.DMA,
        ],
        compiler_params=params(26),
        cost_estimate=cost(count * total * width * 2),
        name="expo",
    )(place, *pieces, *tops, streamed(protos))


def col_scale_of(total_ref, count, proto_total):
    return 1.0 / (proto_total * total_ref[:, :count])


def two_rows(value):
    high, low = split(value)
    which = lax.broadcasted_iota(jnp.int32, (16, value.shape[1]), 0)
    return jnp.where(which == 0, high.astype(F32), jnp.where(which == 1, low.astype(F32), 0.0)).astype(BF16)


def row_kernel(proto_total, with_lse, place, meta, total_ref, expo_ref, *refs):
    out_ref = refs[-1]
    lhs = two_rows(col_scale_of(total_ref, expo_ref.shape[1], proto_total))
    out_ref[...] = jnp.zeros_like(out_ref)
    if with_lse:
        lse_ref = refs[0]
        rows = lse_ref.shape[1]
        start = pl.multiple_of(rows * BLOCKS + place[3] * rows, rows)
        out_ref[:, pl.ds(start, rows)] = lse_ref[...] * 0.25

    @pl.loop(0, meta[TILES])
    def _(tile):
        start = pl.multiple_of(tile * TILE, TILE)
        both = jnp.dot(lhs, expo_ref[tile], preferred_element_type=F32)
        out_ref[:, pl.ds(start, TILE)] = both[:1] + both[1:2]


def row_step(place, meta, total, expo, proto_total, lse=None):
    tiles, count, _ = expo.shape
    more = () if lse is None else (lse,)
    return pl.pallas_call(
        functools.partial(row_kernel, proto_total, lse is not None),
        out_shape=jax.ShapeDtypeStruct((1, (1 + len(more)) * tiles * TILE), F32),
        in_specs=[smem()] * 2 + [vmem()] * (2 + len(more)),
        out_specs=vmem(),
        compiler_params=params(10),
        cost_estimate=cost(count * tiles * TILE * 400),
        name="row_step",
    )(place, meta, total, pinned(expo), *more)


def weights_of(total_ref, valid_ref):
    valid = valid_ref[...]
    return valid / jnp.where(valid > 0, total_ref[:, : valid.shape[1]], 1.0)


def col_kernel(meta, total_ref, valid_ref, expo_ref, out_ref, line_ref, acc_ref):
    line_ref[...] = weights_of(total_ref, valid_ref)
    acc_ref[...] = jnp.zeros_like(acc_ref)
    chunk = 64

    @pl.loop(0, meta[TILES])
    def _(tile):
        start = pl.multiple_of(tile * TILE, TILE)
        weight = line_ref[:, pl.ds(start, TILE)]
        for k in range(0, acc_ref.shape[0], chunk):
            acc_ref[k : k + chunk] += fold(expo_ref[tile, k : k + chunk].astype(F32) * weight)

    out_ref[...] = as_row(acc_ref[...])


def col_step(meta, total, valid, expo):
    tiles, count, _ = expo.shape
    return pl.pallas_call(
        col_kernel,
        out_shape=jax.ShapeDtypeStruct((1, count), F32),
        in_specs=[smem()] + [vmem()] * 3,
        out_specs=vmem(),
        scratch_shapes=[pltpu.VMEM((1, tiles * TILE), F32), pltpu.VMEM((count, LANES), F32)],
        compiler_params=params(10),
        cost_estimate=cost(count * tiles * TILE * 400),
        name="col_step",
    )(meta, total, valid, pinned(expo))


def load_kernel(place, meta, *refs):
    pieces, proto_ref, refs = refs[:8], refs[8], refs[9:]
    out_ref, rank_ref, own_out, turned_ref, rows_ref, own_ref, sem = refs
    protos = own_protos(place, proto_ref, own_ref, sem)
    protos.start()
    rows = pieces[0].shape[1] - INFO
    load_rows(place, meta, pieces, rows_ref, rows)
    out_ref[...] = rows_ref[...]
    masks = [jnp.zeros((1, rows), F32)] * BLOCKS
    for block in range(BLOCKS):
        low, high = joined(place, pieces, block, rows + INFO)
        low, high = low[rows:].astype(F32), high[rows:].astype(F32)
        line = []
        for index in range(rows // (2 * LANES)):
            line += [low[index : index + 1], high[index : index + 1]]
        line = jnp.concatenate(line, axis=1)
        for true in range(block % 2, BLOCKS, 2):
            masks[true] = jnp.where(true_block(place, block) == true, line, masks[true])
    masks = jnp.concatenate(masks, axis=0)
    down = lax.broadcasted_iota(jnp.int32, (rows, rows), 0)
    along = lax.broadcasted_iota(jnp.int32, (rows, rows), 1)
    upper = jnp.where(down <= along, 1.0, 0.0).astype(BF16)
    many = jnp.concatenate([masks, masks], axis=0).astype(BF16)
    rank = jnp.dot(many, upper, preferred_element_type=F32)[:BLOCKS]
    rank_ref[...] = jnp.where(masks > 0, rank - 1.0, -1.0)
    protos.wait()
    own_out[...] = own_ref[...]
    turned_ref[...] = turn(own_ref)


def load_step(place, meta, pieces, protos):
    rows = pieces[0].shape[1] - INFO
    width = protos.shape[1]
    count = protos.shape[0] // BLOCKS
    total = BLOCKS * rows
    return pl.pallas_call(
        load_kernel,
        out_shape=(
            jax.ShapeDtypeStruct((total + TILE, width), BF16),
            jax.ShapeDtypeStruct((BLOCKS, rows), F32),
            jax.ShapeDtypeStruct((count, width), BF16),
            jax.ShapeDtypeStruct((width, count), BF16),
        ),
        in_specs=[smem()] * 2 + [vmem()] * 8 + [hbm()],
        out_specs=(vmem(),) * 4,
        scratch_shapes=[
            pltpu.VMEM((total + TILE, width), BF16),
            pltpu.VMEM((count, width), BF16),
            pltpu.SemaphoreType.DMA,
        ],
        compiler_params=params(18),
        cost_estimate=cost(2**31),
        name="load_student",
    )(place, meta, *pieces, streamed(protos))


def student_kernel(part, place, meta, rows_ref, all_ref, own_ref, turned_ref, *refs):
    if part == 1:
        sums_in, refs = refs[0], refs[1:]
    grads, (sums_out, acc_ref, line_ref) = refs[:2], refs[2:]
    total = sums_out.shape[0]
    rows = total // BLOCKS
    load_line(
        meta, [all_ref[:, total + block * rows : total + (block + 1) * rows] for block in range(BLOCKS)], line_ref, FAR
    )
    acc_ref[...] = jnp.zeros_like(acc_ref)
    sums_out[...] = jnp.zeros_like(sums_out)
    chunk = grads[0].shape[0]

    @pl.loop(0, meta[TILES])
    def _(tile):
        start = pl.multiple_of(tile * TILE, TILE)
        feats = rows_ref[pl.ds(start, TILE), :]
        across = jnp.transpose(feats)
        lse = line_ref[:, pl.ds(start, TILE)]
        turned = jnp.zeros((turned_ref.shape[0], TILE), F32)
        for piece in range(2):
            k = pl.multiple_of((place[2] ^ (2 * part + piece)) * chunk, chunk)
            logit = jnp.dot(own_ref[pl.ds(k, chunk), :], across, preferred_element_type=F32)
            probs = jnp.exp2((logit - lse) * (LOG2E / student_temp)).astype(BF16)
            acc_ref[piece] += jnp.dot(probs, feats, preferred_element_type=F32)
            turned += jnp.dot(turned_ref[:, pl.ds(k, chunk)], probs, preferred_element_type=F32)
        sums = jnp.transpose(turned)
        if part == 1:
            sums = sums + sums_in[pl.ds(start, TILE), :].astype(F32)
        sums_out[pl.ds(start, TILE), :] = sums.astype(BF16)

    for piece in range(2):
        grads[piece][...] = acc_ref[piece].astype(BF16)


def student_step(part, place, meta, rows, line, own, turned, *sums):
    width, count = turned.shape
    total = line.shape[1] // 2
    outs = (jax.ShapeDtypeStruct((count // 4, width), BF16),) * 2 + (jax.ShapeDtypeStruct((total, width), BF16),)
    return pl.pallas_call(
        functools.partial(student_kernel, part),
        out_shape=outs,
        in_specs=[smem()] * 2 + [vmem()] * (4 + len(sums)),
        out_specs=(vmem(),) * len(outs),
        scratch_shapes=[pltpu.VMEM((2, count // 4, width), F32), pltpu.VMEM((1, total + LANES), F32)],
        compiler_params=params(20),
        cost_estimate=cost(count * total * width * 3),
        name="student",
    )(place, meta, rows, line, own, turned, *sums)


def scaled_rows(feats, factor):
    parts = []
    for start in range(0, feats.shape[0], LANES):
        column = jnp.transpose(jnp.broadcast_to(factor[:, start : start + LANES], (LANES, LANES)))
        part = feats[start : start + LANES].astype(F32)
        parts.append(
            jnp.concatenate([part[:, d : d + LANES] * column for d in range(0, part.shape[1], LANES)], axis=1)
        )
    return jnp.concatenate(parts, axis=0)


def feature_kernel(proto_total, first, meta, total_ref, expo_ref, turned_ref, *refs):
    sums_ref = refs[-1]
    scale = col_scale_of(total_ref, expo_ref.shape[1], proto_total)
    scaled = (turned_ref[...].astype(F32) * scale).astype(BF16)
    if first == 0:
        sums_ref[...] = jnp.zeros_like(sums_ref)
        span = (0, jnp.minimum(meta[TILES], SPAN))
    else:
        span = (SPAN, meta[TILES])

    @pl.loop(*span)
    def _(tile):
        start = pl.multiple_of(tile * TILE, TILE)
        turned = jnp.dot(scaled, expo_ref[tile], preferred_element_type=F32)
        sums_ref[pl.ds(start, TILE), :] = jnp.transpose(turned).astype(BF16)


def feature_step(first, meta, total, expo, turned, proto_total, *sums):
    tiles, count, _ = expo.shape
    width = turned.shape[0]
    return pl.pallas_call(
        functools.partial(feature_kernel, proto_total, first),
        out_shape=pltpu.VMEM((tiles * TILE, width), BF16),
        in_specs=[smem()] + [vmem()] * (3 + len(sums)),
        out_specs=vmem(),
        input_output_aliases={4: 0} if sums else {},
        compiler_params=params(14),
        cost_estimate=cost(count * tiles * TILE * width),
        name="feature_step",
    )(meta, total, pinned(expo), turned, *[pinned(value) for value in sums])


def join_kernel(place, meta, total_ref, valid_ref, rank_ref, stud_ref, plan_ref, keep_ref, give_ref, weight_ref, sums_ref):
    weight_ref[...] = weights_of(total_ref, valid_ref)

    @pl.loop(0, meta[TILES])
    def _(tile):
        start = pl.multiple_of(tile * TILE, TILE)
        plan = scaled_rows(plan_ref[pl.ds(start, TILE), :], weight_ref[:, pl.ds(start, TILE)])
        sums_ref[pl.ds(start, TILE), :] = (stud_ref[pl.ds(start, TILE), :].astype(F32) - plan).astype(BF16)

    tail = pl.multiple_of(meta[TILES] * TILE, TILE)
    rows = rank_ref.shape[1]
    sums_ref[pl.ds(tail, rows), :] = jnp.zeros((rows, sums_ref.shape[1]), BF16)
    along = lax.broadcasted_iota(jnp.int32, (LANES, rows), 1).astype(F32)
    first = place[1] == 0
    for block in range(BLOCKS):
        offset = pl.multiple_of(meta[block], ALIGN)
        sums = sums_ref[pl.ds(offset, rows), :]
        pieces = []
        for start in range(0, rows, LANES):
            column = jnp.transpose(jnp.broadcast_to(rank_ref[block : block + 1, start : start + LANES], (LANES, LANES)))
            column = jnp.concatenate([column] * (rows // LANES), axis=1)
            onehot = jnp.where(column == along, 1.0, 0.0).astype(BF16)
            pieces.append(jnp.dot(onehot, sums, preferred_element_type=F32).astype(BF16))
        for half in range(2):
            low, high = pieces[2 * half], pieces[2 * half + 1]
            keep_ref[2 * block + half] = jnp.where(first, low, high)
            give_ref[2 * block + half] = jnp.where(first, high, low)


def join_step(place, meta, total, valid, rank, stud, plan):
    all_rows, width = stud.shape
    out = jax.ShapeDtypeStruct((2 * BLOCKS, LANES, width), BF16)
    return pl.pallas_call(
        join_kernel,
        out_shape=(out, out),
        in_specs=[smem()] * 2 + [vmem()] * 5,
        out_specs=(vmem(),) * 2,
        scratch_shapes=[
            pltpu.VMEM((1, all_rows), F32),
            pltpu.VMEM((all_rows + rank.shape[1], width), BF16),
        ],
        compiler_params=params(14),
        cost_estimate=cost(2**31),
        name="join_step",
    )(place, meta, total, valid, rank, stud, plan)


def grad_kernel(proto_total, place, meta, total_ref, valid_ref, rows_ref, expo_ref, col_ref, *refs):
    studs, grads, (weight_ref, acc_ref) = refs[:4], refs[4:8], refs[8:]
    weight_ref[...] = weights_of(total_ref, valid_ref)
    acc_ref[...] = jnp.zeros_like(acc_ref)
    chunk = 512

    @pl.loop(0, meta[TILES])
    def _(tile):
        start = pl.multiple_of(tile * TILE, TILE)
        scaled = scaled_rows(rows_ref[pl.ds(start, TILE), :], weight_ref[:, pl.ds(start, TILE)]).astype(BF16)
        for k in range(0, acc_ref.shape[0], chunk):
            acc_ref[k : k + chunk] += jnp.dot(
                expo_ref[tile, k : k + chunk], scaled, preferred_element_type=F32
            )

    rows = grads[0].shape[0]
    for piece in range(len(grads)):
        start = pl.multiple_of((place[2] ^ piece) * rows, rows)
        scale = 1.0 / (proto_total * col_ref[:, pl.ds(start, rows)])
        plan = scaled_rows(acc_ref[pl.ds(start, rows), :], scale)
        grads[piece][...] = (studs[piece][...].astype(F32) - plan).astype(BF16)


def grad_step(place, meta, total, valid, rows, expo, col, studs, proto_total):
    tiles, count, _ = expo.shape
    width = rows.shape[1]
    return pl.pallas_call(
        functools.partial(grad_kernel, proto_total),
        out_shape=(jax.ShapeDtypeStruct((count // 4, width), BF16),) * 4,
        in_specs=[smem()] * 2 + [vmem()] * 9,
        out_specs=(vmem(),) * 4,
        scratch_shapes=[pltpu.VMEM((1, tiles * TILE), F32), pltpu.VMEM((count, width), F32)],
        compiler_params=params(18),
        cost_estimate=cost(count * tiles * TILE * width * 2),
        name="grad_step",
    )(place, meta, total, valid, rows, pinned(expo), col, *studs)


def swap(value, axis):
    return lax.ppermute(value, axis, [(0, 1), (1, 0)])


def from_xor(value, axis, mask):
    return lax.ppermute(value, axis, [(i, i ^ mask) for i in range(4)])


def exchange(many, axes):
    return lax.all_to_all(many, axes, 0, 0, tiled=True)


def spread(value, axes, size):
    return exchange(jnp.broadcast_to(value[None], (size,) + value.shape), axes)


def tie(*values):
    return lax.optimization_barrier(values)


def pair_of(half, low):
    return jnp.stack(choose(low, half, swap(half, "xl")))


def double(value, mask):
    return jnp.stack([value, from_xor(value, "y", mask)])


def gather_along(pair):
    return [pair] + [from_xor(pair, "y", mask) for mask in (1, 3, 2)]


def ordered(pieces):
    own, one, three, two = pieces
    return [own, one, two, three]


def scatter_protos(pieces):
    return [pieces[0]] + [from_xor(pieces[mask], "z", mask) for mask in (1, 3, 2)]


def choose(first, one, two):
    return jnp.where(first, one, two), jnp.where(first, two, one)


RINGS = {"x": (("xl", "xh"), (2, 3, 1)), "y": ("y", (1, 3, 2)), "z": ("z", (1, 3, 2))}


def ring(value, name):
    axes, masks = RINGS[name]
    return [lax.ppermute(value, axes, [(i, i ^ mask) for i in range(4)]) for mask in masks]


def total_of(value, got):
    return value + got[0] + got[1] + got[2]


def merged(one, two):
    high = jnp.maximum(one[0], two[0])
    return high, one[1] * jnp.exp((one[0] - high) / student_temp) + two[1] * jnp.exp(
        (two[0] - high) / student_temp
    )


def local(student, teacher, prototypes, masked):
    rows, width = student.shape
    y, xl, z = lax.axis_index("y"), lax.axis_index("xl"), lax.axis_index("z")
    core = lax.axis_index("c")
    block_id = y * 2 + xl
    count = prototypes.shape[0] // BLOCKS
    proto_total = prototypes.shape[0] * 4
    place = jnp.stack([y, core, z, block_id]).astype(jnp.int32)
    low_x, low_c = xl == 0, core == 0
    table = streamed(prototypes)

    teach, stud = compact(masked, streamed(teacher), streamed(student))
    t_half, _ = choose(low_c, teach[:, :LANES], teach[:, LANES:])
    s_half, _ = choose(low_c, stud[:, :LANES], stud[:, LANES:])
    t_half, s_half, teach, stud = tie(t_half, s_half, teach, stud)
    t_beside, s_beside = swap(t_half, "xl"), swap(s_half, "xl")
    top = row_max(teach, table, rows, 0, 1)
    t_beside, s_beside, top, stud = tie(t_beside, s_beside, top, stud)
    t_pair = jnp.stack(choose(low_x, t_half, t_beside))
    s_pair = jnp.stack(choose(low_x, s_half, s_beside))
    top = jnp.maximum(top, swap(top, "c"))

    t_pair, s_pair, top, stud = tie(t_pair, s_pair, top, stud)
    mine = gather_along(t_pair)
    far = swap(top, "xh")
    soft = row_soft(stud, table, rows, 0, 2)
    mine, far, soft, top, stud, s_pair = tie(mine, far, soft, top, stud, s_pair)

    top = jnp.maximum(top, far)
    other = [swap(piece, "c") for piece in mine]
    beside = swap(top, "xl")
    mine, other, top, beside, soft, stud, s_pair = tie(mine, other, top, beside, soft, stud, s_pair)

    tops = gather_along(jnp.stack(choose(low_x, top, beside)))
    s_mine = double(s_pair, 1)
    soft_two = row_soft(stud, table, rows, 1, 2)
    mine, other, tops, soft, soft_two, s_mine, place = tie(mine, other, tops, soft, soft_two, s_mine, place)
    soft = jnp.stack(merged(soft, soft_two))
    soft = jnp.stack(merged(soft, swap(soft, "c")))
    soft, tops, s_mine = tie(soft, tops, s_mine)

    s_mine = [s_mine[0], s_mine[1], from_xor(s_mine, "y", 3)]
    soft_far = swap(soft, "xh")
    expo, col, valid, meta = expo_step(place, ordered(mine) + ordered(other), ordered(tops), prototypes)
    col, soft, soft_far = tie(col, soft, soft_far)

    got = ring(col, "z")
    soft = merged(soft, soft_far)
    got, s_mine, col, soft = tie(got, s_mine, col, soft)
    s_mine = [s_mine[0], s_mine[1], s_mine[2][0], s_mine[2][1]]
    col = total_of(col, got)
    mask_total = col[0, count]
    col, s_mine = tie(col, s_mine)
    s_other = [swap(piece, "c") for piece in s_mine]
    row = row_step(place, meta, col, expo, proto_total, soft[0] + student_temp * jnp.log(soft[1]))
    row, s_mine, s_other = tie(row, s_mine, s_other)
    row = row + swap(row, "c")
    got = ring(row, "x")
    row, got, s_mine, s_other = tie(row, got, s_mine, s_other)
    row = total_of(row, got)
    got = ring(row, "y")
    loaded = load_step(place, meta, ordered(s_mine) + ordered(s_other), prototypes)
    row, got, loaded = tie(row, got, loaded)
    stud_rows, rank, protos, turned = loaded
    row = total_of(row, got)
    col = col_step(meta, row, valid, expo)

    col, stud_rows, line = tie(col, stud_rows, row)
    got = ring(col, "z")
    one = student_step(0, place, meta, stud_rows, line, protos, turned)
    col, got, one = tie(col, got, one)
    row = row_step(place, meta, total_of(col, got), expo, proto_total)
    row = row + swap(row, "c")
    row, one = tie(row, one)
    got = ring(row, "x")
    two = student_step(1, place, meta, stud_rows, line, protos, turned, one[2])
    row, got, two = tie(row, got, two)
    row = total_of(row, got)
    got = ring(row, "y")
    row, got = tie(row, got)
    col = col_step(meta, total_of(row, got), valid, expo)

    got = ring(col, "z")
    col, got = tie(col, got)
    col = total_of(col, got)
    row = row_step(place, meta, col, expo, proto_total)
    row = row + swap(row, "c")
    row, turned = tie(row, turned)
    got = ring(row, "x")
    plan_sums = feature_step(0, meta, col, expo, turned, proto_total)
    row, got, plan_sums = tie(row, got, plan_sums)
    row = total_of(row, got)
    got = ring(row, "y")
    plan_sums = feature_step(1, meta, col, expo, turned, proto_total, plan_sums)
    row, got, plan_sums = tie(row, got, plan_sums)
    row = total_of(row, got)

    keep, give = join_step(place, meta, row, valid, rank, two[2], pinned(plan_sums))
    keep, give, row = tie(keep, give, row)
    got = swap(give, "c")
    grads = grad_step(
        place, meta, row, valid, stud_rows, expo, col, tuple(one[:2]) + tuple(two[:2]), proto_total
    )
    keep, got, grads = tie(keep, got, grads)
    pieces = scatter_protos(grads)
    keep = (keep.astype(F32) + got.astype(F32)).astype(BF16)
    parts = exchange(keep, ("y", "xl", "xh"))
    proto_grad = (
        sum(piece.astype(F32) for piece in pieces) * (proto_total / jnp.sqrt(mask_total))
    ).astype(BF16)
    parts, proto_grad = tie(parts, proto_grad)
    feature_grad = (
        jnp.sum(parts.astype(F32), axis=0) * (math.sqrt(proto_total) / student_temp)
    ).astype(BF16)
    return feature_grad, proto_grad


def solution(mesh):
    fine = Mesh(mesh.devices.reshape(4, 2, 4, 2, 2), ("y", "xl", "z", "xh", "c"))
    rows, protos = ("y", "xl", "z"), ("xh", "c")
    in_specs = (P(rows, None), P(rows, None), P(protos, None), P(rows))
    out_specs = (P(rows + protos, None), P(protos + rows, None))
    return jax.shard_map(local, mesh=fine, in_specs=in_specs, out_specs=out_specs, check_vma=False)
```

```python
import functools
import math

import jax
import jax.numpy as jnp
from jax import lax
from jax.experimental import pallas as pl
from jax.experimental.pallas import tpu as pltpu
from jax.sharding import Mesh
from jax.sharding import PartitionSpec as P

ITERS = 3
student_temp = 0.1
teacher_temp = 0.05

F32 = jnp.float32
BF16 = jnp.bfloat16
TILE = 512
LANES = 128
ALIGN = 16
FAR = 1e30
INFO = 16
SPAN = 3
BLOCKS = 8
END, TILES = 2 * BLOCKS, 2 * BLOCKS + 1
MIB = 2**20

LOG2E = math.log2(math.e)


def params(mib):
    return pltpu.CompilerParams(vmem_limit_bytes=mib * MIB)


def vmem():
    return pl.BlockSpec(memory_space=pltpu.VMEM)


def smem():
    return pl.BlockSpec(memory_space=pltpu.SMEM)


def hbm():
    return pl.BlockSpec(memory_space=pltpu.HBM)


def pinned(value):
    return pltpu.with_memory_space_constraint(value, pltpu.VMEM)


def streamed(value):
    return pltpu.with_memory_space_constraint(value, pltpu.HBM)


def own_protos(place, proto_ref, own_ref, sem):
    count = own_ref.shape[0]
    start = pl.multiple_of(place[3] * count, count)
    return pltpu.make_async_copy(proto_ref.at[pl.ds(start, count)], own_ref, sem)


def turn(own_ref):
    chunk = 512
    return jnp.concatenate(
        [jnp.transpose(own_ref[k : k + chunk]) for k in range(0, own_ref.shape[0], chunk)], axis=1
    )


def split(value):
    high = value.astype(BF16)
    low = (value - high.astype(F32)).astype(BF16)
    return high, low


def as_row(block):
    pieces = []
    for start in range(0, block.shape[0], LANES):
        part = block[start : start + LANES]
        total = part[:, :LANES]
        for lane in range(LANES, block.shape[1], LANES):
            total = total + part[:, lane : lane + LANES]
        pieces.append(jnp.sum(jnp.transpose(total), axis=0, keepdims=True))
    return jnp.concatenate(pieces, axis=1)


def compact_kernel(mask_ref, teach_ref, stud_ref, teach_out, stud_out):
    rows, width = teach_ref.shape
    mask = mask_ref[...].reshape(1, rows).astype(F32)
    down = lax.broadcasted_iota(jnp.int32, (rows, rows), 0)
    along = lax.broadcasted_iota(jnp.int32, (rows, rows), 1)
    upper = jnp.where(down <= along, 1.0, 0.0).astype(BF16)
    many = jnp.broadcast_to(mask, (16, rows)).astype(BF16)
    rank = jnp.dot(many, upper, preferred_element_type=F32)[:1]
    place = jnp.where(mask > 0, rank - 1.0, -1.0)
    onehot = jnp.where(down.astype(F32) == place, 1.0, 0.0).astype(BF16)
    teach_out[:rows] = jnp.dot(onehot, teach_ref[...], preferred_element_type=F32).astype(BF16)
    stud_out[:rows] = jnp.dot(onehot, stud_ref[...], preferred_element_type=F32).astype(BF16)
    which = lax.broadcasted_iota(jnp.int32, (INFO, width), 0)
    info = jnp.zeros((INFO, width), F32)
    for piece in range(rows // width):
        info = jnp.where(which == piece, mask[:, piece * width : (piece + 1) * width], info)
    teach_out[rows:] = info.astype(BF16)
    stud_out[rows:] = info.astype(BF16)


def compact(masked, teacher, student):
    rows, width = teacher.shape
    return pl.pallas_call(
        compact_kernel,
        out_shape=(jax.ShapeDtypeStruct((rows + INFO, width), BF16),) * 2,
        in_specs=[vmem()] * 3,
        out_specs=(vmem(), vmem()),
        compiler_params=params(12),
        name="compact",
    )(masked, teacher, student)


def max_kernel(teach_ref, proto_ref, out_ref, turned_ref):
    rows = out_ref.shape[1]
    chunk = 512

    @pl.when(pl.program_id(0) == 0)
    def _():
        out_ref[...] = jnp.full_like(out_ref, -FAR)
        turned_ref[...] = jnp.transpose(teach_ref[:rows])

    best = out_ref[...]
    for start in range(0, proto_ref.shape[0], chunk):
        logit = jnp.dot(proto_ref[start : start + chunk], turned_ref[...], preferred_element_type=F32)
        best = jnp.maximum(best, jnp.max(logit, axis=0, keepdims=True))
    out_ref[...] = best


def row_max(feats, protos, rows, first, steps):
    count, width = protos.shape
    block = 2048
    return pl.pallas_call(
        max_kernel,
        grid=(steps,),
        out_shape=jax.ShapeDtypeStruct((1, rows), F32),
        in_specs=[
            pl.BlockSpec(feats.shape, lambda i: (0, 0)),
            pl.BlockSpec((block, width), lambda i: (i + first, 0)),
        ],
        out_specs=pl.BlockSpec((1, rows), lambda i: (0, 0)),
        scratch_shapes=[pltpu.VMEM((width, rows), BF16)],
        compiler_params=params(14),
        cost_estimate=cost(3 * steps * block * width * rows),
        name="row_max",
    )(feats, protos)


def soft_kernel(feat_ref, proto_ref, top_ref, sum_ref, turned_ref):
    chunk = 512

    @pl.when(pl.program_id(0) == 0)
    def _():
        top_ref[...] = jnp.full_like(top_ref, -FAR)
        sum_ref[...] = jnp.zeros_like(sum_ref)
        turned_ref[...] = jnp.transpose(feat_ref[: turned_ref.shape[1]])

    top = top_ref[...]
    total = sum_ref[...]
    for start in range(0, proto_ref.shape[0], chunk):
        logit = jnp.dot(proto_ref[start : start + chunk], turned_ref[...], preferred_element_type=F32)
        higher = jnp.maximum(top, jnp.max(logit, axis=0, keepdims=True))
        total = total * jnp.exp((top - higher) * (1 / student_temp)) + jnp.sum(
            jnp.exp2((logit - higher) * (LOG2E / student_temp)), axis=0, keepdims=True
        )
        top = higher
    top_ref[...] = top
    sum_ref[...] = total


def row_soft(feats, protos, rows, part, parts):
    count, width = protos.shape
    block = 2048
    steps = count // block // parts
    row = pl.BlockSpec((1, rows), lambda i: (0, 0))
    return pl.pallas_call(
        soft_kernel,
        grid=(steps,),
        out_shape=(jax.ShapeDtypeStruct((1, rows), F32),) * 2,
        in_specs=[
            pl.BlockSpec(feats.shape, lambda i: (0, 0)),
            pl.BlockSpec((block, width), lambda i: (i + part * steps, 0)),
        ],
        out_specs=(row, row),
        scratch_shapes=[pltpu.VMEM((width, rows), BF16)],
        compiler_params=params(14),
        cost_estimate=cost(3 * count * width * rows // parts),
        name="row_soft",
    )(feats, protos)


def cost(flops):
    return pl.CostEstimate(flops=flops, bytes_accessed=2**20, transcendentals=0)


def joined(place, refs, block, rows):
    piece, side = block // 2, block % 2
    mine = refs[piece][side, :rows]
    other = refs[4 + piece][side, :rows]
    first = place[1] == 0
    return jnp.where(first, mine, other), jnp.where(first, other, mine)


def true_block(place, block):
    return (place[0] ^ (block // 2)) * 2 + block % 2


def load_rows(place, meta, refs, rows_ref, rows):
    for true in range(BLOCKS):

        def fill(block, true=true):
            @pl.when(place[0] == (true // 2) ^ (block // 2))
            def _():
                offset = pl.multiple_of(meta[true], ALIGN)
                low, high = joined(place, refs, block, rows)
                rows_ref[pl.ds(offset, rows), :LANES] = low
                rows_ref[pl.ds(offset, rows), LANES:] = high

        for piece in range(4):
            fill(piece * 2 + true % 2)
    tail = pl.multiple_of(meta[END], ALIGN)
    rows_ref[pl.ds(tail, TILE), :] = jnp.zeros((TILE, rows_ref.shape[1]), BF16)


def load_line(meta, lines, out_ref, fill):
    rows = lines[0].shape[1]
    out_ref[...] = jnp.full_like(out_ref, fill)
    lane = lax.broadcasted_iota(jnp.int32, (1, rows + LANES), 1)
    for block in range(BLOCKS):
        offset = meta[block]
        shift = lax.rem(offset, LANES)
        base = pl.multiple_of(offset - shift, LANES)
        wide = jnp.concatenate([lines[block], jnp.zeros((1, LANES), F32)], axis=1)
        wide = pltpu.roll(jnp.broadcast_to(wide, (8, rows + LANES)), shift, axis=1)[:1]
        there = (lane >= shift) & (lane < shift + meta[BLOCKS + block])
        out_ref[:, pl.ds(base, rows + LANES)] = jnp.where(
            there, wide, out_ref[:, pl.ds(base, rows + LANES)]
        )


def place_blocks(place, meta, refs, rows):
    for block in range(BLOCKS):
        piece, side = block // 2, block % 2
        info = refs[piece][side, rows:].astype(F32) + refs[4 + piece][side, rows:].astype(F32)
        meta[BLOCKS + true_block(place, block)] = jnp.sum(info).astype(jnp.int32)
    end = jnp.int32(0)
    for block in range(BLOCKS):
        meta[block] = end
        end = end + (meta[BLOCKS + block] + (ALIGN - 1)) // ALIGN * ALIGN
    meta[END] = end
    meta[TILES] = (end + (TILE - 1)) // TILE


def expo_kernel(place, *refs):
    pieces, tops, proto_ref, refs = refs[:8], refs[8:12], refs[12], refs[13:]
    expo_ref, col_ref, valid_ref, meta, rows_ref, line_ref, acc_ref, own_ref, sem = refs
    rows = tops[0].shape[2]
    protos = own_protos(place, proto_ref, own_ref, sem)
    protos.start()
    place_blocks(place, meta, pieces, rows)
    load_rows(place, meta, pieces, rows_ref, rows)
    lines = []
    for block in range(BLOCKS):
        line = tops[0][block % 2]
        for piece in range(1, 4):
            line = jnp.where((place[0] ^ piece) == block // 2, tops[piece][block % 2], line)
        lines.append(line)
    load_line(meta, lines, line_ref, FAR)
    valid_ref[...] = jnp.where(line_ref[:, : valid_ref.shape[1]] < 0.5 * FAR, 1.0, 0.0)
    acc_ref[...] = jnp.zeros_like(acc_ref)
    protos.wait()
    chunk = 512
    count = own_ref.shape[0]

    @pl.loop(0, meta[TILES])
    def _(tile):
        start = pl.multiple_of(tile * TILE, TILE)
        feats = jnp.transpose(rows_ref[pl.ds(start, TILE), :])
        top = line_ref[:, pl.ds(start, TILE)]
        for k in range(0, count, chunk):
            logit = jnp.dot(own_ref[k : k + chunk], feats, preferred_element_type=F32)
            expo = jnp.exp2((logit - top) * (LOG2E / teacher_temp))
            expo_ref[tile, k : k + chunk] = expo.astype(BF16)
            acc_ref[k : k + chunk] += fold(expo)

    col_ref[:, :count] = as_row(acc_ref[...])
    col_ref[:, count:] = jnp.zeros((1, LANES), F32) + jnp.sum(valid_ref[...])


def fold(block):
    total = block[:, :LANES]
    for lane in range(LANES, block.shape[1], LANES):
        total = total + block[:, lane : lane + LANES]
    return total


def expo_step(place, pieces, tops, protos):
    rows = tops[0].shape[2]
    width = protos.shape[1]
    count = protos.shape[0] // BLOCKS
    total = BLOCKS * rows
    return pl.pallas_call(
        expo_kernel,
        out_shape=(
            pltpu.VMEM((total // TILE, count, TILE), BF16),
            jax.ShapeDtypeStruct((1, count + LANES), F32),
            jax.ShapeDtypeStruct((1, total), F32),
            jax.ShapeDtypeStruct((24,), jnp.int32),
        ),
        in_specs=[smem()] + [vmem()] * 12 + [hbm()],
        out_specs=(vmem(), vmem(), vmem(), smem()),
        scratch_shapes=[
            pltpu.VMEM((total + TILE, width), BF16),
            pltpu.VMEM((1, total + LANES), F32),
            pltpu.VMEM((count, LANES), F32),
            pltpu.VMEM((count, width), BF16),
            pltpu.SemaphoreType.DMA,
        ],
        compiler_params=params(26),
        cost_estimate=cost(count * total * width * 2),
        name="expo",
    )(place, *pieces, *tops, streamed(protos))


def col_scale_of(total_ref, count, proto_total):
    return 1.0 / (proto_total * total_ref[:, :count])


def two_rows(value):
    high, low = split(value)
    which = lax.broadcasted_iota(jnp.int32, (16, value.shape[1]), 0)
    return jnp.where(which == 0, high.astype(F32), jnp.where(which == 1, low.astype(F32), 0.0)).astype(BF16)


def row_kernel(proto_total, with_lse, place, meta, total_ref, expo_ref, *refs):
    out_ref = refs[-1]
    lhs = two_rows(col_scale_of(total_ref, expo_ref.shape[1], proto_total))
    out_ref[...] = jnp.zeros_like(out_ref)
    if with_lse:
        lse_ref = refs[0]
        rows = lse_ref.shape[1]
        start = pl.multiple_of(rows * BLOCKS + place[3] * rows, rows)
        out_ref[:, pl.ds(start, rows)] = lse_ref[...] * 0.25

    @pl.loop(0, meta[TILES])
    def _(tile):
        start = pl.multiple_of(tile * TILE, TILE)
        both = jnp.dot(lhs, expo_ref[tile], preferred_element_type=F32)
        out_ref[:, pl.ds(start, TILE)] = both[:1] + both[1:2]


def row_step(place, meta, total, expo, proto_total, lse=None):
    tiles, count, _ = expo.shape
    more = () if lse is None else (lse,)
    return pl.pallas_call(
        functools.partial(row_kernel, proto_total, lse is not None),
        out_shape=jax.ShapeDtypeStruct((1, (1 + len(more)) * tiles * TILE), F32),
        in_specs=[smem()] * 2 + [vmem()] * (2 + len(more)),
        out_specs=vmem(),
        compiler_params=params(10),
        cost_estimate=cost(count * tiles * TILE * 400),
        name="row_step",
    )(place, meta, total, pinned(expo), *more)


def weights_of(total_ref, valid_ref):
    valid = valid_ref[...]
    return valid / jnp.where(valid > 0, total_ref[:, : valid.shape[1]], 1.0)


def col_kernel(meta, total_ref, valid_ref, expo_ref, out_ref, line_ref, acc_ref):
    line_ref[...] = weights_of(total_ref, valid_ref)
    acc_ref[...] = jnp.zeros_like(acc_ref)
    chunk = 64

    @pl.loop(0, meta[TILES])
    def _(tile):
        start = pl.multiple_of(tile * TILE, TILE)
        weight = line_ref[:, pl.ds(start, TILE)]
        for k in range(0, acc_ref.shape[0], chunk):
            acc_ref[k : k + chunk] += fold(expo_ref[tile, k : k + chunk].astype(F32) * weight)

    out_ref[...] = as_row(acc_ref[...])


def col_step(meta, total, valid, expo):
    tiles, count, _ = expo.shape
    return pl.pallas_call(
        col_kernel,
        out_shape=jax.ShapeDtypeStruct((1, count), F32),
        in_specs=[smem()] + [vmem()] * 3,
        out_specs=vmem(),
        scratch_shapes=[pltpu.VMEM((1, tiles * TILE), F32), pltpu.VMEM((count, LANES), F32)],
        compiler_params=params(10),
        cost_estimate=cost(count * tiles * TILE * 400),
        name="col_step",
    )(meta, total, valid, pinned(expo))


def load_kernel(place, meta, *refs):
    pieces, proto_ref, refs = refs[:8], refs[8], refs[9:]
    out_ref, rank_ref, own_out, turned_ref, rows_ref, own_ref, sem = refs
    protos = own_protos(place, proto_ref, own_ref, sem)
    protos.start()
    rows = pieces[0].shape[1] - INFO
    load_rows(place, meta, pieces, rows_ref, rows)
    out_ref[...] = rows_ref[...]
    masks = [jnp.zeros((1, rows), F32)] * BLOCKS
    for block in range(BLOCKS):
        low, high = joined(place, pieces, block, rows + INFO)
        low, high = low[rows:].astype(F32), high[rows:].astype(F32)
        line = []
        for index in range(rows // (2 * LANES)):
            line += [low[index : index + 1], high[index : index + 1]]
        line = jnp.concatenate(line, axis=1)
        for true in range(block % 2, BLOCKS, 2):
            masks[true] = jnp.where(true_block(place, block) == true, line, masks[true])
    masks = jnp.concatenate(masks, axis=0)
    down = lax.broadcasted_iota(jnp.int32, (rows, rows), 0)
    along = lax.broadcasted_iota(jnp.int32, (rows, rows), 1)
    upper = jnp.where(down <= along, 1.0, 0.0).astype(BF16)
    many = jnp.concatenate([masks, masks], axis=0).astype(BF16)
    rank = jnp.dot(many, upper, preferred_element_type=F32)[:BLOCKS]
    rank_ref[...] = jnp.where(masks > 0, rank - 1.0, -1.0)
    protos.wait()
    own_out[...] = own_ref[...]
    turned_ref[...] = turn(own_ref)


def load_step(place, meta, pieces, protos):
    rows = pieces[0].shape[1] - INFO
    width = protos.shape[1]
    count = protos.shape[0] // BLOCKS
    total = BLOCKS * rows
    return pl.pallas_call(
        load_kernel,
        out_shape=(
            jax.ShapeDtypeStruct((total + TILE, width), BF16),
            jax.ShapeDtypeStruct((BLOCKS, rows), F32),
            jax.ShapeDtypeStruct((count, width), BF16),
            jax.ShapeDtypeStruct((width, count), BF16),
        ),
        in_specs=[smem()] * 2 + [vmem()] * 8 + [hbm()],
        out_specs=(vmem(),) * 4,
        scratch_shapes=[
            pltpu.VMEM((total + TILE, width), BF16),
            pltpu.VMEM((count, width), BF16),
            pltpu.SemaphoreType.DMA,
        ],
        compiler_params=params(18),
        cost_estimate=cost(2**31),
        name="load_student",
    )(place, meta, *pieces, streamed(protos))


def student_kernel(part, place, meta, rows_ref, all_ref, own_ref, turned_ref, *refs):
    if part == 1:
        sums_in, refs = refs[0], refs[1:]
    grads, (sums_out, acc_ref, line_ref) = refs[:2], refs[2:]
    total = sums_out.shape[0]
    rows = total // BLOCKS
    load_line(
        meta, [all_ref[:, total + block * rows : total + (block + 1) * rows] for block in range(BLOCKS)], line_ref, FAR
    )
    acc_ref[...] = jnp.zeros_like(acc_ref)
    sums_out[...] = jnp.zeros_like(sums_out)
    chunk = grads[0].shape[0]

    @pl.loop(0, meta[TILES])
    def _(tile):
        start = pl.multiple_of(tile * TILE, TILE)
        feats = rows_ref[pl.ds(start, TILE), :]
        across = jnp.transpose(feats)
        lse = line_ref[:, pl.ds(start, TILE)]
        turned = jnp.zeros((turned_ref.shape[0], TILE), F32)
        for piece in range(2):
            k = pl.multiple_of((place[2] ^ (2 * part + piece)) * chunk, chunk)
            logit = jnp.dot(own_ref[pl.ds(k, chunk), :], across, preferred_element_type=F32)
            probs = jnp.exp2((logit - lse) * (LOG2E / student_temp)).astype(BF16)
            acc_ref[piece] += jnp.dot(probs, feats, preferred_element_type=F32)
            turned += jnp.dot(turned_ref[:, pl.ds(k, chunk)], probs, preferred_element_type=F32)
        sums = jnp.transpose(turned)
        if part == 1:
            sums = sums + sums_in[pl.ds(start, TILE), :].astype(F32)
        sums_out[pl.ds(start, TILE), :] = sums.astype(BF16)

    for piece in range(2):
        grads[piece][...] = acc_ref[piece].astype(BF16)


def student_step(part, place, meta, rows, line, own, turned, *sums):
    width, count = turned.shape
    total = line.shape[1] // 2
    outs = (jax.ShapeDtypeStruct((count // 4, width), BF16),) * 2 + (jax.ShapeDtypeStruct((total, width), BF16),)
    return pl.pallas_call(
        functools.partial(student_kernel, part),
        out_shape=outs,
        in_specs=[smem()] * 2 + [vmem()] * (4 + len(sums)),
        out_specs=(vmem(),) * len(outs),
        scratch_shapes=[pltpu.VMEM((2, count // 4, width), F32), pltpu.VMEM((1, total + LANES), F32)],
        compiler_params=params(20),
        cost_estimate=cost(count * total * width * 3),
        name="student",
    )(place, meta, rows, line, own, turned, *sums)


def scaled_rows(feats, factor):
    parts = []
    for start in range(0, feats.shape[0], LANES):
        column = jnp.transpose(jnp.broadcast_to(factor[:, start : start + LANES], (LANES, LANES)))
        part = feats[start : start + LANES].astype(F32)
        parts.append(
            jnp.concatenate([part[:, d : d + LANES] * column for d in range(0, part.shape[1], LANES)], axis=1)
        )
    return jnp.concatenate(parts, axis=0)


def feature_kernel(proto_total, first, meta, total_ref, expo_ref, turned_ref, *refs):
    sums_ref = refs[-1]
    scale = col_scale_of(total_ref, expo_ref.shape[1], proto_total)
    scaled = (turned_ref[...].astype(F32) * scale).astype(BF16)
    if first == 0:
        sums_ref[...] = jnp.zeros_like(sums_ref)
        span = (0, jnp.minimum(meta[TILES], SPAN))
    else:
        span = (SPAN, meta[TILES])

    @pl.loop(*span)
    def _(tile):
        start = pl.multiple_of(tile * TILE, TILE)
        turned = jnp.dot(scaled, expo_ref[tile], preferred_element_type=F32)
        sums_ref[pl.ds(start, TILE), :] = jnp.transpose(turned).astype(BF16)


def feature_step(first, meta, total, expo, turned, proto_total, *sums):
    tiles, count, _ = expo.shape
    width = turned.shape[0]
    return pl.pallas_call(
        functools.partial(feature_kernel, proto_total, first),
        out_shape=pltpu.VMEM((tiles * TILE, width), BF16),
        in_specs=[smem()] + [vmem()] * (3 + len(sums)),
        out_specs=vmem(),
        input_output_aliases={4: 0} if sums else {},
        compiler_params=params(14),
        cost_estimate=cost(count * tiles * TILE * width),
        name="feature_step",
    )(meta, total, pinned(expo), turned, *[pinned(value) for value in sums])


def join_kernel(place, meta, total_ref, valid_ref, rank_ref, stud_ref, plan_ref, keep_ref, give_ref, weight_ref, sums_ref):
    weight_ref[...] = weights_of(total_ref, valid_ref)

    @pl.loop(0, meta[TILES])
    def _(tile):
        start = pl.multiple_of(tile * TILE, TILE)
        plan = scaled_rows(plan_ref[pl.ds(start, TILE), :], weight_ref[:, pl.ds(start, TILE)])
        sums_ref[pl.ds(start, TILE), :] = (stud_ref[pl.ds(start, TILE), :].astype(F32) - plan).astype(BF16)

    tail = pl.multiple_of(meta[TILES] * TILE, TILE)
    rows = rank_ref.shape[1]
    sums_ref[pl.ds(tail, rows), :] = jnp.zeros((rows, sums_ref.shape[1]), BF16)
    along = lax.broadcasted_iota(jnp.int32, (LANES, rows), 1).astype(F32)
    first = place[1] == 0
    for block in range(BLOCKS):
        offset = pl.multiple_of(meta[block], ALIGN)
        sums = sums_ref[pl.ds(offset, rows), :]
        pieces = []
        for start in range(0, rows, LANES):
            column = jnp.transpose(jnp.broadcast_to(rank_ref[block : block + 1, start : start + LANES], (LANES, LANES)))
            column = jnp.concatenate([column] * (rows // LANES), axis=1)
            onehot = jnp.where(column == along, 1.0, 0.0).astype(BF16)
            pieces.append(jnp.dot(onehot, sums, preferred_element_type=F32).astype(BF16))
        for half in range(2):
            low, high = pieces[2 * half], pieces[2 * half + 1]
            keep_ref[2 * block + half] = jnp.where(first, low, high)
            give_ref[2 * block + half] = jnp.where(first, high, low)


def join_step(place, meta, total, valid, rank, stud, plan):
    all_rows, width = stud.shape
    out = jax.ShapeDtypeStruct((2 * BLOCKS, LANES, width), BF16)
    return pl.pallas_call(
        join_kernel,
        out_shape=(out, out),
        in_specs=[smem()] * 2 + [vmem()] * 5,
        out_specs=(vmem(),) * 2,
        scratch_shapes=[
            pltpu.VMEM((1, all_rows), F32),
            pltpu.VMEM((all_rows + rank.shape[1], width), BF16),
        ],
        compiler_params=params(14),
        cost_estimate=cost(2**31),
        name="join_step",
    )(place, meta, total, valid, rank, stud, plan)


def grad_kernel(proto_total, place, meta, total_ref, valid_ref, rows_ref, expo_ref, col_ref, *refs):
    studs, grads, (weight_ref, acc_ref) = refs[:4], refs[4:8], refs[8:]
    weight_ref[...] = weights_of(total_ref, valid_ref)
    acc_ref[...] = jnp.zeros_like(acc_ref)
    chunk = 512

    @pl.loop(0, meta[TILES])
    def _(tile):
        start = pl.multiple_of(tile * TILE, TILE)
        scaled = scaled_rows(rows_ref[pl.ds(start, TILE), :], weight_ref[:, pl.ds(start, TILE)]).astype(BF16)
        for k in range(0, acc_ref.shape[0], chunk):
            acc_ref[k : k + chunk] += jnp.dot(
                expo_ref[tile, k : k + chunk], scaled, preferred_element_type=F32
            )

    rows = grads[0].shape[0]
    for piece in range(len(grads)):
        start = pl.multiple_of((place[2] ^ piece) * rows, rows)
        scale = 1.0 / (proto_total * col_ref[:, pl.ds(start, rows)])
        plan = scaled_rows(acc_ref[pl.ds(start, rows), :], scale)
        grads[piece][...] = (studs[piece][...].astype(F32) - plan).astype(BF16)


def grad_step(place, meta, total, valid, rows, expo, col, studs, proto_total):
    tiles, count, _ = expo.shape
    width = rows.shape[1]
    return pl.pallas_call(
        functools.partial(grad_kernel, proto_total),
        out_shape=(jax.ShapeDtypeStruct((count // 4, width), BF16),) * 4,
        in_specs=[smem()] * 2 + [vmem()] * 9,
        out_specs=(vmem(),) * 4,
        scratch_shapes=[pltpu.VMEM((1, tiles * TILE), F32), pltpu.VMEM((count, width), F32)],
        compiler_params=params(18),
        cost_estimate=cost(count * tiles * TILE * width * 2),
        name="grad_step",
    )(place, meta, total, valid, rows, pinned(expo), col, *studs)


def swap(value, axis):
    return lax.ppermute(value, axis, [(0, 1), (1, 0)])


def from_xor(value, axis, mask):
    return lax.ppermute(value, axis, [(i, i ^ mask) for i in range(4)])


def exchange(many, axes):
    return lax.all_to_all(many, axes, 0, 0, tiled=True)


def spread(value, axes, size):
    return exchange(jnp.broadcast_to(value[None], (size,) + value.shape), axes)


def tie(*values):
    return lax.optimization_barrier(values)


def pair_of(half, low):
    return jnp.stack(choose(low, half, swap(half, "xl")))


def double(value, mask):
    return jnp.stack([value, from_xor(value, "y", mask)])


def gather_along(pair):
    return [pair] + [from_xor(pair, "y", mask) for mask in (1, 3, 2)]


def ordered(pieces):
    own, one, three, two = pieces
    return [own, one, two, three]


def scatter_protos(pieces):
    return [pieces[0]] + [from_xor(pieces[mask], "z", mask) for mask in (1, 3, 2)]


def choose(first, one, two):
    return jnp.where(first, one, two), jnp.where(first, two, one)


RINGS = {"x": (("xl", "xh"), (2, 3, 1)), "y": ("y", (1, 3, 2)), "z": ("z", (1, 3, 2))}


def ring(value, name):
    axes, masks = RINGS[name]
    return [lax.ppermute(value, axes, [(i, i ^ mask) for i in range(4)]) for mask in masks]


def total_of(value, got):
    return value + got[0] + got[1] + got[2]


def merged(one, two):
    high = jnp.maximum(one[0], two[0])
    return high, one[1] * jnp.exp((one[0] - high) / student_temp) + two[1] * jnp.exp(
        (two[0] - high) / student_temp
    )


def local(student, teacher, prototypes, masked):
    rows, width = student.shape
    y, xl, z = lax.axis_index("y"), lax.axis_index("xl"), lax.axis_index("z")
    core = lax.axis_index("c")
    block_id = y * 2 + xl
    count = prototypes.shape[0] // BLOCKS
    proto_total = prototypes.shape[0] * 4
    place = jnp.stack([y, core, z, block_id]).astype(jnp.int32)
    low_x, low_c = xl == 0, core == 0
    table = streamed(prototypes)

    teach, stud = compact(masked, streamed(teacher), streamed(student))
    t_half, _ = choose(low_c, teach[:, :LANES], teach[:, LANES:])
    s_half, _ = choose(low_c, stud[:, :LANES], stud[:, LANES:])
    t_half, teach, stud = tie(t_half, teach, stud)
    t_beside = swap(t_half, "xl")
    top = row_max(teach, table, rows, 0, 8)
    t_beside, top, stud, s_half = tie(t_beside, top, stud, s_half)
    t_pair = jnp.stack(choose(low_x, t_half, t_beside))

    t_pair, top, stud = tie(t_pair, top, stud)
    mine = gather_along(t_pair)
    s_beside = swap(s_half, "xl")
    top = jnp.maximum(top, swap(top, "c"))
    far = swap(top, "xh")
    soft = row_soft(stud, table, rows, 0, 2)
    mine, far, soft, top, stud, s_beside = tie(mine, far, soft, top, stud, s_beside)
    s_pair = jnp.stack(choose(low_x, s_half, s_beside))

    top = jnp.maximum(top, far)
    other = [swap(piece, "c") for piece in mine]
    beside = swap(top, "xl")
    mine, other, top, beside, soft, stud, s_pair = tie(mine, other, top, beside, soft, stud, s_pair)

    tops = gather_along(jnp.stack(choose(low_x, top, beside)))
    s_mine = double(s_pair, 1)
    soft_two = row_soft(stud, table, rows, 1, 2)
    mine, other, tops, soft, soft_two, s_mine, place = tie(mine, other, tops, soft, soft_two, s_mine, place)
    soft = jnp.stack(merged(soft, soft_two))
    soft = jnp.stack(merged(soft, swap(soft, "c")))
    soft, tops = tie(soft, tops)

    s_mine = [s_mine[0], s_mine[1], from_xor(s_mine, "y", 3)]
    soft_far = swap(soft, "xh")
    expo, col, valid, meta = expo_step(place, ordered(mine) + ordered(other), ordered(tops), prototypes)
    col, soft, soft_far = tie(col, soft, soft_far)

    got = ring(col, "z")
    soft = merged(soft, soft_far)
    got, s_mine, col, soft = tie(got, s_mine, col, soft)
    s_mine = [s_mine[0], s_mine[1], s_mine[2][0], s_mine[2][1]]
    col = total_of(col, got)
    mask_total = col[0, count]
    col, s_mine = tie(col, s_mine)
    s_other = [swap(piece, "c") for piece in s_mine]
    row = row_step(place, meta, col, expo, proto_total, soft[0] + student_temp * jnp.log(soft[1]))
    row, s_mine, s_other = tie(row, s_mine, s_other)
    row = row + swap(row, "c")
    got = ring(row, "x")
    row, got, s_mine, s_other = tie(row, got, s_mine, s_other)
    row = total_of(row, got)
    got = ring(row, "y")
    loaded = load_step(place, meta, ordered(s_mine) + ordered(s_other), prototypes)
    row, got, loaded = tie(row, got, loaded)
    stud_rows, rank, protos, turned = loaded
    row = total_of(row, got)
    col = col_step(meta, row, valid, expo)

    col, stud_rows, line = tie(col, stud_rows, row)
    got = ring(col, "z")
    one = student_step(0, place, meta, stud_rows, line, protos, turned)
    col, got, one = tie(col, got, one)
    row = row_step(place, meta, total_of(col, got), expo, proto_total)
    row = row + swap(row, "c")
    row, one = tie(row, one)
    got = ring(row, "x")
    two = student_step(1, place, meta, stud_rows, line, protos, turned, one[2])
    row, got, two = tie(row, got, two)
    row = total_of(row, got)
    got = ring(row, "y")
    row, got = tie(row, got)
    col = col_step(meta, total_of(row, got), valid, expo)

    got = ring(col, "z")
    col, got = tie(col, got)
    col = total_of(col, got)
    row = row_step(place, meta, col, expo, proto_total)
    row = row + swap(row, "c")
    row, turned = tie(row, turned)
    got = ring(row, "x")
    plan_sums = feature_step(0, meta, col, expo, turned, proto_total)
    row, got, plan_sums = tie(row, got, plan_sums)
    row = total_of(row, got)
    got = ring(row, "y")
    plan_sums = feature_step(1, meta, col, expo, turned, proto_total, plan_sums)
    row, got, plan_sums = tie(row, got, plan_sums)
    row = total_of(row, got)

    keep, give = join_step(place, meta, row, valid, rank, two[2], pinned(plan_sums))
    keep, give, row = tie(keep, give, row)
    got = swap(give, "c")
    grads = grad_step(
        place, meta, row, valid, stud_rows, expo, col, tuple(one[:2]) + tuple(two[:2]), proto_total
    )
    keep, got, grads = tie(keep, got, grads)
    pieces = scatter_protos(grads)
    keep = (keep.astype(F32) + got.astype(F32)).astype(BF16)
    parts = exchange(keep, ("y", "xl", "xh"))
    proto_grad = (
        sum(piece.astype(F32) for piece in pieces) * (proto_total / jnp.sqrt(mask_total))
    ).astype(BF16)
    parts, proto_grad = tie(parts, proto_grad)
    feature_grad = (
        jnp.sum(parts.astype(F32), axis=0) * (math.sqrt(proto_total) / student_temp)
    ).astype(BF16)
    return feature_grad, proto_grad


def solution(mesh):
    fine = Mesh(mesh.devices.reshape(4, 2, 4, 2, 2), ("y", "xl", "z", "xh", "c"))
    rows, protos = ("y", "xl", "z"), ("xh", "c")
    in_specs = (P(rows, None), P(rows, None), P(protos, None), P(rows))
    out_specs = (P(rows + protos, None), P(protos + rows, None))
    return jax.shard_map(local, mesh=fine, in_specs=in_specs, out_specs=out_specs, check_vma=False)
```

```python
import functools
import math

import jax
import jax.numpy as jnp
from jax import lax
from jax.experimental import pallas as pl
from jax.experimental.pallas import tpu as pltpu
from jax.sharding import Mesh
from jax.sharding import PartitionSpec as P

ITERS = 3
student_temp = 0.1
teacher_temp = 0.05

F32 = jnp.float32
BF16 = jnp.bfloat16
TILE = 512
LANES = 128
ALIGN = 16
FAR = 1e30
INFO = 16
SPAN = 3
BLOCKS = 8
END, TILES = 2 * BLOCKS, 2 * BLOCKS + 1
MIB = 2**20

LOG2E = math.log2(math.e)


def params(mib):
    return pltpu.CompilerParams(vmem_limit_bytes=mib * MIB)


def vmem():
    return pl.BlockSpec(memory_space=pltpu.VMEM)


def smem():
    return pl.BlockSpec(memory_space=pltpu.SMEM)


def hbm():
    return pl.BlockSpec(memory_space=pltpu.HBM)


def pinned(value):
    return pltpu.with_memory_space_constraint(value, pltpu.VMEM)


def streamed(value):
    return pltpu.with_memory_space_constraint(value, pltpu.HBM)


def own_protos(place, proto_ref, own_ref, sem):
    count = own_ref.shape[0]
    start = pl.multiple_of(place[3] * count, count)
    return pltpu.make_async_copy(proto_ref.at[pl.ds(start, count)], own_ref, sem)


def turn(own_ref):
    chunk = 512
    return jnp.concatenate(
        [jnp.transpose(own_ref[k : k + chunk]) for k in range(0, own_ref.shape[0], chunk)], axis=1
    )


def split(value):
    high = value.astype(BF16)
    low = (value - high.astype(F32)).astype(BF16)
    return high, low


def as_row(block):
    pieces = []
    for start in range(0, block.shape[0], LANES):
        part = block[start : start + LANES]
        total = part[:, :LANES]
        for lane in range(LANES, block.shape[1], LANES):
            total = total + part[:, lane : lane + LANES]
        pieces.append(jnp.sum(jnp.transpose(total), axis=0, keepdims=True))
    return jnp.concatenate(pieces, axis=1)


def compact_kernel(mask_ref, teach_ref, stud_ref, teach_out, stud_out):
    rows, width = teach_ref.shape
    mask = mask_ref[...].reshape(1, rows).astype(F32)
    down = lax.broadcasted_iota(jnp.int32, (rows, rows), 0)
    along = lax.broadcasted_iota(jnp.int32, (rows, rows), 1)
    upper = jnp.where(down <= along, 1.0, 0.0).astype(BF16)
    many = jnp.broadcast_to(mask, (16, rows)).astype(BF16)
    rank = jnp.dot(many, upper, preferred_element_type=F32)[:1]
    place = jnp.where(mask > 0, rank - 1.0, -1.0)
    onehot = jnp.where(down.astype(F32) == place, 1.0, 0.0).astype(BF16)
    teach_out[:rows] = jnp.dot(onehot, teach_ref[...], preferred_element_type=F32).astype(BF16)
    stud_out[:rows] = jnp.dot(onehot, stud_ref[...], preferred_element_type=F32).astype(BF16)
    which = lax.broadcasted_iota(jnp.int32, (INFO, width), 0)
    info = jnp.zeros((INFO, width), F32)
    for piece in range(rows // width):
        info = jnp.where(which == piece, mask[:, piece * width : (piece + 1) * width], info)
    teach_out[rows:] = info.astype(BF16)
    stud_out[rows:] = info.astype(BF16)


def compact(masked, teacher, student):
    rows, width = teacher.shape
    return pl.pallas_call(
        compact_kernel,
        out_shape=(jax.ShapeDtypeStruct((rows + INFO, width), BF16),) * 2,
        in_specs=[vmem()] * 3,
        out_specs=(vmem(), vmem()),
        compiler_params=params(12),
        name="compact",
    )(masked, teacher, student)


def max_kernel(teach_ref, proto_ref, out_ref, turned_ref):
    rows = out_ref.shape[1]
    chunk = 512

    @pl.when(pl.program_id(0) == 0)
    def _():
        out_ref[...] = jnp.full_like(out_ref, -FAR)
        turned_ref[...] = jnp.transpose(teach_ref[:rows])

    best = out_ref[...]
    for start in range(0, proto_ref.shape[0], chunk):
        logit = jnp.dot(proto_ref[start : start + chunk], turned_ref[...], preferred_element_type=F32)
        best = jnp.maximum(best, jnp.max(logit, axis=0, keepdims=True))
    out_ref[...] = best


def row_max(feats, protos, rows, first, steps):
    count, width = protos.shape
    block = 2048
    return pl.pallas_call(
        max_kernel,
        grid=(steps,),
        out_shape=jax.ShapeDtypeStruct((1, rows), F32),
        in_specs=[
            pl.BlockSpec(feats.shape, lambda i: (0, 0)),
            pl.BlockSpec((block, width), lambda i: (i + first, 0)),
        ],
        out_specs=pl.BlockSpec((1, rows), lambda i: (0, 0)),
        scratch_shapes=[pltpu.VMEM((width, rows), BF16)],
        compiler_params=params(14),
        cost_estimate=cost(3 * steps * block * width * rows),
        name="row_max",
    )(feats, protos)


def soft_kernel(feat_ref, proto_ref, top_ref, sum_ref, turned_ref):
    chunk = 512

    @pl.when(pl.program_id(0) == 0)
    def _():
        top_ref[...] = jnp.full_like(top_ref, -FAR)
        sum_ref[...] = jnp.zeros_like(sum_ref)
        turned_ref[...] = jnp.transpose(feat_ref[: turned_ref.shape[1]])

    top = top_ref[...]
    total = sum_ref[...]
    for start in range(0, proto_ref.shape[0], chunk):
        logit = jnp.dot(proto_ref[start : start + chunk], turned_ref[...], preferred_element_type=F32)
        higher = jnp.maximum(top, jnp.max(logit, axis=0, keepdims=True))
        total = total * jnp.exp((top - higher) * (1 / student_temp)) + jnp.sum(
            jnp.exp2((logit - higher) * (LOG2E / student_temp)), axis=0, keepdims=True
        )
        top = higher
    top_ref[...] = top
    sum_ref[...] = total


def row_soft(feats, protos, rows, part, parts):
    count, width = protos.shape
    block = 2048
    steps = count // block // parts
    row = pl.BlockSpec((1, rows), lambda i: (0, 0))
    return pl.pallas_call(
        soft_kernel,
        grid=(steps,),
        out_shape=(jax.ShapeDtypeStruct((1, rows), F32),) * 2,
        in_specs=[
            pl.BlockSpec(feats.shape, lambda i: (0, 0)),
            pl.BlockSpec((block, width), lambda i: (i + part * steps, 0)),
        ],
        out_specs=(row, row),
        scratch_shapes=[pltpu.VMEM((width, rows), BF16)],
        compiler_params=params(14),
        cost_estimate=cost(3 * count * width * rows // parts),
        name="row_soft",
    )(feats, protos)


def cost(flops):
    return pl.CostEstimate(flops=flops, bytes_accessed=2**20, transcendentals=0)


def joined(place, refs, block, rows):
    piece, side = block // 2, block % 2
    mine = refs[piece][side, :rows]
    other = refs[4 + piece][side, :rows]
    first = place[1] == 0
    return jnp.where(first, mine, other), jnp.where(first, other, mine)


def true_block(place, block):
    return (place[0] ^ (block // 2)) * 2 + block % 2


def load_rows(place, meta, refs, rows_ref, rows):
    for true in range(BLOCKS):

        def fill(block, true=true):
            @pl.when(place[0] == (true // 2) ^ (block // 2))
            def _():
                offset = pl.multiple_of(meta[true], ALIGN)
                low, high = joined(place, refs, block, rows)
                rows_ref[pl.ds(offset, rows), :LANES] = low
                rows_ref[pl.ds(offset, rows), LANES:] = high

        for piece in range(4):
            fill(piece * 2 + true % 2)
    tail = pl.multiple_of(meta[END], ALIGN)
    rows_ref[pl.ds(tail, TILE), :] = jnp.zeros((TILE, rows_ref.shape[1]), BF16)


def load_line(meta, lines, out_ref, fill):
    rows = lines[0].shape[1]
    out_ref[...] = jnp.full_like(out_ref, fill)
    lane = lax.broadcasted_iota(jnp.int32, (1, rows + LANES), 1)
    for block in range(BLOCKS):
        offset = meta[block]
        shift = lax.rem(offset, LANES)
        base = pl.multiple_of(offset - shift, LANES)
        wide = jnp.concatenate([lines[block], jnp.zeros((1, LANES), F32)], axis=1)
        wide = pltpu.roll(jnp.broadcast_to(wide, (8, rows + LANES)), shift, axis=1)[:1]
        there = (lane >= shift) & (lane < shift + meta[BLOCKS + block])
        out_ref[:, pl.ds(base, rows + LANES)] = jnp.where(
            there, wide, out_ref[:, pl.ds(base, rows + LANES)]
        )


def place_blocks(place, meta, refs, rows):
    for block in range(BLOCKS):
        piece, side = block // 2, block % 2
        info = refs[piece][side, rows:].astype(F32) + refs[4 + piece][side, rows:].astype(F32)
        meta[BLOCKS + true_block(place, block)] = jnp.sum(info).astype(jnp.int32)
    end = jnp.int32(0)
    for block in range(BLOCKS):
        meta[block] = end
        end = end + (meta[BLOCKS + block] + (ALIGN - 1)) // ALIGN * ALIGN
    meta[END] = end
    meta[TILES] = (end + (TILE - 1)) // TILE


def expo_kernel(place, *refs):
    pieces, tops, proto_ref, refs = refs[:8], refs[8:12], refs[12], refs[13:]
    expo_ref, col_ref, valid_ref, meta, rows_ref, line_ref, acc_ref, own_ref, sem = refs
    rows = tops[0].shape[2]
    protos = own_protos(place, proto_ref, own_ref, sem)
    protos.start()
    place_blocks(place, meta, pieces, rows)
    load_rows(place, meta, pieces, rows_ref, rows)
    lines = []
    for block in range(BLOCKS):
        line = tops[0][block % 2]
        for piece in range(1, 4):
            line = jnp.where((place[0] ^ piece) == block // 2, tops[piece][block % 2], line)
        lines.append(line)
    load_line(meta, lines, line_ref, FAR)
    valid_ref[...] = jnp.where(line_ref[:, : valid_ref.shape[1]] < 0.5 * FAR, 1.0, 0.0)
    acc_ref[...] = jnp.zeros_like(acc_ref)
    protos.wait()
    chunk = 512
    count = own_ref.shape[0]

    @pl.loop(0, meta[TILES])
    def _(tile):
        start = pl.multiple_of(tile * TILE, TILE)
        feats = jnp.transpose(rows_ref[pl.ds(start, TILE), :])
        top = line_ref[:, pl.ds(start, TILE)]
        for k in range(0, count, chunk):
            logit = jnp.dot(own_ref[k : k + chunk], feats, preferred_element_type=F32)
            expo = jnp.exp2((logit - top) * (LOG2E / teacher_temp))
            expo_ref[tile, k : k + chunk] = expo.astype(BF16)
            acc_ref[k : k + chunk] += fold(expo)

    col_ref[:, :count] = as_row(acc_ref[...])
    col_ref[:, count:] = jnp.zeros((1, LANES), F32) + jnp.sum(valid_ref[...])


def fold(block):
    total = block[:, :LANES]
    for lane in range(LANES, block.shape[1], LANES):
        total = total + block[:, lane : lane + LANES]
    return total


def expo_step(place, pieces, tops, protos):
    rows = tops[0].shape[2]
    width = protos.shape[1]
    count = protos.shape[0] // BLOCKS
    total = BLOCKS * rows
    return pl.pallas_call(
        expo_kernel,
        out_shape=(
            pltpu.VMEM((total // TILE, count, TILE), BF16),
            jax.ShapeDtypeStruct((1, count + LANES), F32),
            jax.ShapeDtypeStruct((1, total), F32),
            jax.ShapeDtypeStruct((24,), jnp.int32),
        ),
        in_specs=[smem()] + [vmem()] * 12 + [hbm()],
        out_specs=(vmem(), vmem(), vmem(), smem()),
        scratch_shapes=[
            pltpu.VMEM((total + TILE, width), BF16),
            pltpu.VMEM((1, total + LANES), F32),
            pltpu.VMEM((count, LANES), F32),
            pltpu.VMEM((count, width), BF16),
            pltpu.SemaphoreType.DMA,
        ],
        compiler_params=params(26),
        cost_estimate=cost(count * total * width * 2),
        name="expo",
    )(place, *pieces, *tops, streamed(protos))


def col_scale_of(total_ref, count, proto_total):
    return 1.0 / (proto_total * total_ref[:, :count])


def two_rows(value):
    high, low = split(value)
    which = lax.broadcasted_iota(jnp.int32, (16, value.shape[1]), 0)
    return jnp.where(which == 0, high.astype(F32), jnp.where(which == 1, low.astype(F32), 0.0)).astype(BF16)


def row_kernel(proto_total, with_lse, place, meta, total_ref, expo_ref, *refs):
    out_ref = refs[-1]
    lhs = two_rows(col_scale_of(total_ref, expo_ref.shape[1], proto_total))
    out_ref[...] = jnp.zeros_like(out_ref)
    if with_lse:
        lse_ref = refs[0]
        rows = lse_ref.shape[1]
        start = pl.multiple_of(rows * BLOCKS + place[3] * rows, rows)
        out_ref[:, pl.ds(start, rows)] = lse_ref[...] * 0.25

    @pl.loop(0, meta[TILES])
    def _(tile):
        start = pl.multiple_of(tile * TILE, TILE)
        both = jnp.dot(lhs, expo_ref[tile], preferred_element_type=F32)
        out_ref[:, pl.ds(start, TILE)] = both[:1] + both[1:2]


def row_step(place, meta, total, expo, proto_total, lse=None):
    tiles, count, _ = expo.shape
    more = () if lse is None else (lse,)
    return pl.pallas_call(
        functools.partial(row_kernel, proto_total, lse is not None),
        out_shape=jax.ShapeDtypeStruct((1, (1 + len(more)) * tiles * TILE), F32),
        in_specs=[smem()] * 2 + [vmem()] * (2 + len(more)),
        out_specs=vmem(),
        compiler_params=params(10),
        cost_estimate=cost(count * tiles * TILE * 400),
        name="row_step",
    )(place, meta, total, pinned(expo), *more)


def weights_of(total_ref, valid_ref):
    valid = valid_ref[...]
    return valid / jnp.where(valid > 0, total_ref[:, : valid.shape[1]], 1.0)


def col_kernel(meta, total_ref, valid_ref, expo_ref, out_ref, line_ref, acc_ref):
    line_ref[...] = weights_of(total_ref, valid_ref)
    acc_ref[...] = jnp.zeros_like(acc_ref)
    chunk = 64

    @pl.loop(0, meta[TILES])
    def _(tile):
        start = pl.multiple_of(tile * TILE, TILE)
        weight = line_ref[:, pl.ds(start, TILE)]
        for k in range(0, acc_ref.shape[0], chunk):
            acc_ref[k : k + chunk] += fold(expo_ref[tile, k : k + chunk].astype(F32) * weight)

    out_ref[...] = as_row(acc_ref[...])


def col_step(meta, total, valid, expo):
    tiles, count, _ = expo.shape
    return pl.pallas_call(
        col_kernel,
        out_shape=jax.ShapeDtypeStruct((1, count), F32),
        in_specs=[smem()] + [vmem()] * 3,
        out_specs=vmem(),
        scratch_shapes=[pltpu.VMEM((1, tiles * TILE), F32), pltpu.VMEM((count, LANES), F32)],
        compiler_params=params(10),
        cost_estimate=cost(count * tiles * TILE * 400),
        name="col_step",
    )(meta, total, valid, pinned(expo))


def load_kernel(place, meta, *refs):
    pieces, proto_ref, refs = refs[:8], refs[8], refs[9:]
    out_ref, rank_ref, own_out, turned_ref, rows_ref, own_ref, sem = refs
    protos = own_protos(place, proto_ref, own_ref, sem)
    protos.start()
    rows = pieces[0].shape[1] - INFO
    load_rows(place, meta, pieces, rows_ref, rows)
    out_ref[...] = rows_ref[...]
    masks = [jnp.zeros((1, rows), F32)] * BLOCKS
    for block in range(BLOCKS):
        low, high = joined(place, pieces, block, rows + INFO)
        low, high = low[rows:].astype(F32), high[rows:].astype(F32)
        line = []
        for index in range(rows // (2 * LANES)):
            line += [low[index : index + 1], high[index : index + 1]]
        line = jnp.concatenate(line, axis=1)
        for true in range(block % 2, BLOCKS, 2):
            masks[true] = jnp.where(true_block(place, block) == true, line, masks[true])
    masks = jnp.concatenate(masks, axis=0)
    down = lax.broadcasted_iota(jnp.int32, (rows, rows), 0)
    along = lax.broadcasted_iota(jnp.int32, (rows, rows), 1)
    upper = jnp.where(down <= along, 1.0, 0.0).astype(BF16)
    many = jnp.concatenate([masks, masks], axis=0).astype(BF16)
    rank = jnp.dot(many, upper, preferred_element_type=F32)[:BLOCKS]
    rank_ref[...] = jnp.where(masks > 0, rank - 1.0, -1.0)
    protos.wait()
    own_out[...] = own_ref[...]
    turned_ref[...] = turn(own_ref)


def load_step(place, meta, pieces, protos):
    rows = pieces[0].shape[1] - INFO
    width = protos.shape[1]
    count = protos.shape[0] // BLOCKS
    total = BLOCKS * rows
    return pl.pallas_call(
        load_kernel,
        out_shape=(
            jax.ShapeDtypeStruct((total + TILE, width), BF16),
            jax.ShapeDtypeStruct((BLOCKS, rows), F32),
            jax.ShapeDtypeStruct((count, width), BF16),
            jax.ShapeDtypeStruct((width, count), BF16),
        ),
        in_specs=[smem()] * 2 + [vmem()] * 8 + [hbm()],
        out_specs=(vmem(),) * 4,
        scratch_shapes=[
            pltpu.VMEM((total + TILE, width), BF16),
            pltpu.VMEM((count, width), BF16),
            pltpu.SemaphoreType.DMA,
        ],
        compiler_params=params(18),
        cost_estimate=cost(2**31),
        name="load_student",
    )(place, meta, *pieces, streamed(protos))


def student_kernel(part, place, meta, rows_ref, all_ref, own_ref, turned_ref, *refs):
    if part == 1:
        sums_in, refs = refs[0], refs[1:]
    grads, (sums_out, acc_ref, line_ref) = refs[:2], refs[2:]
    total = sums_out.shape[0]
    rows = total // BLOCKS
    load_line(
        meta, [all_ref[:, total + block * rows : total + (block + 1) * rows] for block in range(BLOCKS)], line_ref, FAR
    )
    acc_ref[...] = jnp.zeros_like(acc_ref)
    sums_out[...] = jnp.zeros_like(sums_out)
    chunk = grads[0].shape[0]

    @pl.loop(0, meta[TILES])
    def _(tile):
        start = pl.multiple_of(tile * TILE, TILE)
        feats = rows_ref[pl.ds(start, TILE), :]
        across = jnp.transpose(feats)
        lse = line_ref[:, pl.ds(start, TILE)]
        turned = jnp.zeros((turned_ref.shape[0], TILE), F32)
        for piece in range(2):
            k = pl.multiple_of((place[2] ^ (2 * part + piece)) * chunk, chunk)
            logit = jnp.dot(own_ref[pl.ds(k, chunk), :], across, preferred_element_type=F32)
            probs = jnp.exp2((logit - lse) * (LOG2E / student_temp)).astype(BF16)
            acc_ref[piece] += jnp.dot(probs, feats, preferred_element_type=F32)
            turned += jnp.dot(turned_ref[:, pl.ds(k, chunk)], probs, preferred_element_type=F32)
        sums = jnp.transpose(turned)
        if part == 1:
            sums = sums + sums_in[pl.ds(start, TILE), :].astype(F32)
        sums_out[pl.ds(start, TILE), :] = sums.astype(BF16)

    for piece in range(2):
        grads[piece][...] = acc_ref[piece].astype(BF16)


def student_step(part, place, meta, rows, line, own, turned, *sums):
    width, count = turned.shape
    total = line.shape[1] // 2
    outs = (jax.ShapeDtypeStruct((count // 4, width), BF16),) * 2 + (jax.ShapeDtypeStruct((total, width), BF16),)
    return pl.pallas_call(
        functools.partial(student_kernel, part),
        out_shape=outs,
        in_specs=[smem()] * 2 + [vmem()] * (4 + len(sums)),
        out_specs=(vmem(),) * len(outs),
        scratch_shapes=[pltpu.VMEM((2, count // 4, width), F32), pltpu.VMEM((1, total + LANES), F32)],
        compiler_params=params(20),
        cost_estimate=cost(count * total * width * 3),
        name="student",
    )(place, meta, rows, line, own, turned, *sums)


def scaled_rows(feats, factor):
    parts = []
    for start in range(0, feats.shape[0], LANES):
        column = jnp.transpose(jnp.broadcast_to(factor[:, start : start + LANES], (LANES, LANES)))
        part = feats[start : start + LANES].astype(F32)
        parts.append(
            jnp.concatenate([part[:, d : d + LANES] * column for d in range(0, part.shape[1], LANES)], axis=1)
        )
    return jnp.concatenate(parts, axis=0)


def feature_kernel(proto_total, first, meta, total_ref, expo_ref, turned_ref, *refs):
    sums_ref = refs[-1]
    scale = col_scale_of(total_ref, expo_ref.shape[1], proto_total)
    scaled = (turned_ref[...].astype(F32) * scale).astype(BF16)
    if first == 0:
        sums_ref[...] = jnp.zeros_like(sums_ref)
        span = (0, jnp.minimum(meta[TILES], SPAN))
    else:
        span = (SPAN, meta[TILES])

    @pl.loop(*span)
    def _(tile):
        start = pl.multiple_of(tile * TILE, TILE)
        turned = jnp.dot(scaled, expo_ref[tile], preferred_element_type=F32)
        sums_ref[pl.ds(start, TILE), :] = jnp.transpose(turned).astype(BF16)


def feature_step(first, meta, total, expo, turned, proto_total, *sums):
    tiles, count, _ = expo.shape
    width = turned.shape[0]
    return pl.pallas_call(
        functools.partial(feature_kernel, proto_total, first),
        out_shape=pltpu.VMEM((tiles * TILE, width), BF16),
        in_specs=[smem()] + [vmem()] * (3 + len(sums)),
        out_specs=vmem(),
        input_output_aliases={4: 0} if sums else {},
        compiler_params=params(14),
        cost_estimate=cost(count * tiles * TILE * width),
        name="feature_step",
    )(meta, total, pinned(expo), turned, *[pinned(value) for value in sums])


def join_kernel(place, meta, total_ref, valid_ref, rank_ref, stud_ref, plan_ref, keep_ref, give_ref, weight_ref, sums_ref):
    weight_ref[...] = weights_of(total_ref, valid_ref)

    @pl.loop(0, meta[TILES])
    def _(tile):
        start = pl.multiple_of(tile * TILE, TILE)
        plan = scaled_rows(plan_ref[pl.ds(start, TILE), :], weight_ref[:, pl.ds(start, TILE)])
        sums_ref[pl.ds(start, TILE), :] = (stud_ref[pl.ds(start, TILE), :].astype(F32) - plan).astype(BF16)

    tail = pl.multiple_of(meta[TILES] * TILE, TILE)
    rows = rank_ref.shape[1]
    sums_ref[pl.ds(tail, rows), :] = jnp.zeros((rows, sums_ref.shape[1]), BF16)
    along = lax.broadcasted_iota(jnp.int32, (LANES, rows), 1).astype(F32)
    first = place[1] == 0
    for block in range(BLOCKS):
        offset = pl.multiple_of(meta[block], ALIGN)
        sums = sums_ref[pl.ds(offset, rows), :]
        pieces = []
        for start in range(0, rows, LANES):
            column = jnp.transpose(jnp.broadcast_to(rank_ref[block : block + 1, start : start + LANES], (LANES, LANES)))
            column = jnp.concatenate([column] * (rows // LANES), axis=1)
            onehot = jnp.where(column == along, 1.0, 0.0).astype(BF16)
            pieces.append(jnp.dot(onehot, sums, preferred_element_type=F32).astype(BF16))
        for half in range(2):
            low, high = pieces[2 * half], pieces[2 * half + 1]
            keep_ref[2 * block + half] = jnp.where(first, low, high)
            give_ref[2 * block + half] = jnp.where(first, high, low)


def join_step(place, meta, total, valid, rank, stud, plan):
    all_rows, width = stud.shape
    out = jax.ShapeDtypeStruct((2 * BLOCKS, LANES, width), BF16)
    return pl.pallas_call(
        join_kernel,
        out_shape=(out, out),
        in_specs=[smem()] * 2 + [vmem()] * 5,
        out_specs=(vmem(),) * 2,
        scratch_shapes=[
            pltpu.VMEM((1, all_rows), F32),
            pltpu.VMEM((all_rows + rank.shape[1], width), BF16),
        ],
        compiler_params=params(14),
        cost_estimate=cost(2**31),
        name="join_step",
    )(place, meta, total, valid, rank, stud, plan)


def grad_kernel(proto_total, place, meta, total_ref, valid_ref, rows_ref, expo_ref, col_ref, *refs):
    studs, grads, (weight_ref, acc_ref) = refs[:4], refs[4:8], refs[8:]
    weight_ref[...] = weights_of(total_ref, valid_ref)
    acc_ref[...] = jnp.zeros_like(acc_ref)
    chunk = 512

    @pl.loop(0, meta[TILES])
    def _(tile):
        start = pl.multiple_of(tile * TILE, TILE)
        scaled = scaled_rows(rows_ref[pl.ds(start, TILE), :], weight_ref[:, pl.ds(start, TILE)]).astype(BF16)
        for k in range(0, acc_ref.shape[0], chunk):
            acc_ref[k : k + chunk] += jnp.dot(
                expo_ref[tile, k : k + chunk], scaled, preferred_element_type=F32
            )

    rows = grads[0].shape[0]
    for piece in range(len(grads)):
        start = pl.multiple_of((place[2] ^ piece) * rows, rows)
        scale = 1.0 / (proto_total * col_ref[:, pl.ds(start, rows)])
        plan = scaled_rows(acc_ref[pl.ds(start, rows), :], scale)
        grads[piece][...] = (studs[piece][...].astype(F32) - plan).astype(BF16)


def grad_step(place, meta, total, valid, rows, expo, col, studs, proto_total):
    tiles, count, _ = expo.shape
    width = rows.shape[1]
    return pl.pallas_call(
        functools.partial(grad_kernel, proto_total),
        out_shape=(jax.ShapeDtypeStruct((count // 4, width), BF16),) * 4,
        in_specs=[smem()] * 2 + [vmem()] * 9,
        out_specs=(vmem(),) * 4,
        scratch_shapes=[pltpu.VMEM((1, tiles * TILE), F32), pltpu.VMEM((count, width), F32)],
        compiler_params=params(18),
        cost_estimate=cost(count * tiles * TILE * width * 2),
        name="grad_step",
    )(place, meta, total, valid, rows, pinned(expo), col, *studs)


def swap(value, axis):
    return lax.ppermute(value, axis, [(0, 1), (1, 0)])


def from_xor(value, axis, mask):
    return lax.ppermute(value, axis, [(i, i ^ mask) for i in range(4)])


def exchange(many, axes):
    return lax.all_to_all(many, axes, 0, 0, tiled=True)


def spread(value, axes, size):
    return exchange(jnp.broadcast_to(value[None], (size,) + value.shape), axes)


def tie(*values):
    return lax.optimization_barrier(values)


def pair_of(half, low):
    return jnp.stack(choose(low, half, swap(half, "xl")))


def double(value, mask):
    return jnp.stack([value, from_xor(value, "y", mask)])


def gather_along(pair):
    return [pair] + [from_xor(pair, "y", mask) for mask in (1, 3, 2)]


def ordered(pieces):
    own, one, three, two = pieces
    return [own, one, two, three]


def scatter_protos(pieces):
    return [pieces[0]] + [from_xor(pieces[mask], "z", mask) for mask in (2, 3, 1)]


def choose(first, one, two):
    return jnp.where(first, one, two), jnp.where(first, two, one)


RINGS = {"x": (("xl", "xh"), (2, 3, 1)), "y": ("y", (1, 3, 2)), "z": ("z", (1, 3, 2))}


def ring(value, name):
    axes, masks = RINGS[name]
    return [lax.ppermute(value, axes, [(i, i ^ mask) for i in range(4)]) for mask in masks]


def total_of(value, got):
    return value + got[0] + got[1] + got[2]


def merged(one, two):
    high = jnp.maximum(one[0], two[0])
    return high, one[1] * jnp.exp((one[0] - high) / student_temp) + two[1] * jnp.exp(
        (two[0] - high) / student_temp
    )


def local(student, teacher, prototypes, masked):
    rows, width = student.shape
    y, xl, z = lax.axis_index("y"), lax.axis_index("xl"), lax.axis_index("z")
    core = lax.axis_index("c")
    block_id = y * 2 + xl
    count = prototypes.shape[0] // BLOCKS
    proto_total = prototypes.shape[0] * 4
    place = jnp.stack([y, core, z, block_id]).astype(jnp.int32)
    low_x, low_c = xl == 0, core == 0
    table = streamed(prototypes)

    teach, stud = compact(masked, streamed(teacher), streamed(student))
    t_half, _ = choose(low_c, teach[:, :LANES], teach[:, LANES:])
    s_half, _ = choose(low_c, stud[:, :LANES], stud[:, LANES:])
    t_half, teach, stud = tie(t_half, teach, stud)
    t_beside = swap(t_half, "xl")
    top = row_max(teach, table, rows, 0, 8)
    t_beside, top, stud, s_half = tie(t_beside, top, stud, s_half)
    t_pair = jnp.stack(choose(low_x, t_half, t_beside))

    t_pair, top, stud = tie(t_pair, top, stud)
    mine = gather_along(t_pair)
    s_beside = swap(s_half, "xl")
    top = jnp.maximum(top, swap(top, "c"))
    far = swap(top, "xh")
    soft = row_soft(stud, table, rows, 0, 2)
    mine, far, soft, top, stud, s_beside = tie(mine, far, soft, top, stud, s_beside)
    s_pair = jnp.stack(choose(low_x, s_half, s_beside))

    top = jnp.maximum(top, far)
    other = [swap(piece, "c") for piece in mine]
    beside = swap(top, "xl")
    mine, other, top, beside, soft, stud, s_pair = tie(mine, other, top, beside, soft, stud, s_pair)

    tops = gather_along(jnp.stack(choose(low_x, top, beside)))
    s_mine = double(s_pair, 1)
    soft_two = row_soft(stud, table, rows, 1, 2)
    mine, other, tops, soft, soft_two, s_mine, place = tie(mine, other, tops, soft, soft_two, s_mine, place)
    soft = jnp.stack(merged(soft, soft_two))
    soft = jnp.stack(merged(soft, swap(soft, "c")))
    soft, tops = tie(soft, tops)

    s_mine = [s_mine[0], s_mine[1], from_xor(s_mine, "y", 3)]
    soft_far = swap(soft, "xh")
    expo, col, valid, meta = expo_step(place, ordered(mine) + ordered(other), ordered(tops), prototypes)
    col, soft, soft_far = tie(col, soft, soft_far)

    got = ring(col, "z")
    soft = merged(soft, soft_far)
    got, s_mine, col, soft = tie(got, s_mine, col, soft)
    s_mine = [s_mine[0], s_mine[1], s_mine[2][0], s_mine[2][1]]
    col = total_of(col, got)
    mask_total = col[0, count]
    col, s_mine = tie(col, s_mine)
    s_other = [swap(piece, "c") for piece in s_mine]
    row = row_step(place, meta, col, expo, proto_total, soft[0] + student_temp * jnp.log(soft[1]))
    row, s_mine, s_other = tie(row, s_mine, s_other)
    row = row + swap(row, "c")
    got = ring(row, "x")
    row, got, s_mine, s_other = tie(row, got, s_mine, s_other)
    row = total_of(row, got)
    got = ring(row, "y")
    loaded = load_step(place, meta, ordered(s_mine) + ordered(s_other), prototypes)
    row, got, loaded = tie(row, got, loaded)
    stud_rows, rank, protos, turned = loaded
    row = total_of(row, got)
    col = col_step(meta, row, valid, expo)

    col, stud_rows, line = tie(col, stud_rows, row)
    got = ring(col, "z")
    one = student_step(0, place, meta, stud_rows, line, protos, turned)
    col, got, one = tie(col, got, one)
    row = row_step(place, meta, total_of(col, got), expo, proto_total)
    row = row + swap(row, "c")
    row, one = tie(row, one)
    got = ring(row, "x")
    two = student_step(1, place, meta, stud_rows, line, protos, turned, one[2])
    row, got, two = tie(row, got, two)
    row = total_of(row, got)
    got = ring(row, "y")
    row, got = tie(row, got)
    col = col_step(meta, total_of(row, got), valid, expo)

    got = ring(col, "z")
    col, got = tie(col, got)
    col = total_of(col, got)
    row = row_step(place, meta, col, expo, proto_total)
    row = row + swap(row, "c")
    row, turned = tie(row, turned)
    got = ring(row, "x")
    plan_sums = feature_step(0, meta, col, expo, turned, proto_total)
    row, got, plan_sums = tie(row, got, plan_sums)
    row = total_of(row, got)
    got = ring(row, "y")
    plan_sums = feature_step(1, meta, col, expo, turned, proto_total, plan_sums)
    row, got, plan_sums = tie(row, got, plan_sums)
    row = total_of(row, got)

    keep, give = join_step(place, meta, row, valid, rank, two[2], pinned(plan_sums))
    keep, give, row = tie(keep, give, row)
    got = swap(give, "c")
    grads = grad_step(
        place, meta, row, valid, stud_rows, expo, col, tuple(one[:2]) + tuple(two[:2]), proto_total
    )
    keep, got, grads = tie(keep, got, grads)
    pieces = scatter_protos(grads)
    keep = (keep.astype(F32) + got.astype(F32)).astype(BF16)
    parts = exchange(keep, ("y", "xl", "xh"))
    proto_grad = (
        sum(piece.astype(F32) for piece in pieces) * (proto_total / jnp.sqrt(mask_total))
    ).astype(BF16)
    parts, proto_grad = tie(parts, proto_grad)
    feature_grad = (
        jnp.sum(parts.astype(F32), axis=0) * (math.sqrt(proto_total) / student_temp)
    ).astype(BF16)
    return feature_grad, proto_grad


def solution(mesh):
    fine = Mesh(mesh.devices.reshape(4, 2, 4, 2, 2), ("y", "xl", "z", "xh", "c"))
    rows, protos = ("y", "xl", "z"), ("xh", "c")
    in_specs = (P(rows, None), P(rows, None), P(protos, None), P(rows))
    out_specs = (P(rows + protos, None), P(protos + rows, None))
    return jax.shard_map(local, mesh=fine, in_specs=in_specs, out_specs=out_specs, check_vma=False)
```
